512 devices in a mesh: ctx: 64 (over x, z, core), mp: 8 (over y).
Axes of the slice: x: 4, y: 8, z: 8, core: 2. Of those that a mesh axis runs over, the one named last changes fastest.
Arguments:
- query_proj: bfloat16 [8192, 4096], P(('ctx', 'mp')), may hold values from -91.92388 to 91.92388
- keyval_proj: bfloat16 [8192, 8, 256], P(('ctx', 'mp')), may hold values from -12 to 12
- hidden: bfloat16 [8192, 4096], P('ctx', 'mp'), may hold values from -6 to 6
- weight_x: bfloat16 [4096, 1024], P(None, 'mp'), may hold values from -0.09375 to 0.09375
- conv_x: float32 [4, 1024], P(None, 'mp'), may hold values from -3 to 3
- conv_b: float32 [4, 1024], P(None, 'mp'), may hold values from -3 to 3
- conv_c: float32 [4, 4096], P(None, 'mp'), may hold values from -3 to 3
- step_size: float32 [8192, 32], P('ctx', 'mp'), may hold values from 0 to 1.2, as said below
- decay_log: float32 [32], P('mp'), may hold values from -0.5 to 0.5
- skip_gain: float32 [32], P('mp'), may hold values from 0.5 to 1.5
Outputs:
- student_out: bfloat16 [8192, 4096], P('ctx', 'mp')
- weight_grad: float32 [4096, 1024], P('ctx', 'mp')
The draws below stay inside these ranges and needn't reach their ends.
Inputs may be any that keep to these rules, and one draw needn't show every extreme that they name: `step_size`: positive.
All inputs are finite; a program needn't handle non-finite values.
Results may differ from the reference program's by a relative error of at most 0.001.
The reference program's roundings to bfloat16 on the way (of `x_input` and `input_grad`) count: a program that leaves them out, or rounds other values in their place, can miss the bound.
Values may be sent and summed in bfloat16 or wider, within the bound.
A program may use at most 64 MiB of HBM per device.

```python
import jax
import jax.numpy as jnp
from jax import lax

D = 4096
HEAD_TOTAL = 32
KV = 8
HD = 128
CONV = 4
TOK_DEV = 128
TOKEN_TOTAL = 8192


def draw_query_proj(key, part):
    base_key = jax.random.fold_in(key, 1)
    values = 4.0 * jnp.clip(jax.random.normal(base_key, (TOKEN_TOTAL, HEAD_TOTAL * HD), jnp.float32), -4.0, 4.0)
    return values.astype(jnp.bfloat16)


def draw_keyval_proj(key, part):
    base_key = jax.random.fold_in(key, 2)
    lanes = jnp.arange(2 * HD) < HD
    values = jnp.clip(jax.random.normal(base_key, (TOKEN_TOTAL, KV, 2 * HD), jnp.float32), -4.0, 4.0)
    values = jnp.where(lanes[None, None, :], values, 3.0 * values)
    return values.astype(jnp.bfloat16)


def draw_step_size(key, part):
    kind_key = jax.random.fold_in(key, 21)
    fast_key = jax.random.fold_in(key, 22)
    slow_key = jax.random.fold_in(key, 23)
    rough_key = jax.random.fold_in(key, 24)
    place_key = jax.random.fold_in(key, 25)
    spike_key = jax.random.fold_in(key, 26)
    fast = jax.random.uniform(kind_key, (HEAD_TOTAL,)) < 0.5
    fast_rate = jnp.exp(jax.random.uniform(fast_key, (HEAD_TOTAL,), jnp.float32, jnp.log(1.0 / 50.0), jnp.log(1.0 / 30.0)))
    slow_rate = jnp.exp(jax.random.uniform(slow_key, (HEAD_TOTAL,), jnp.float32, jnp.log(0.3), 0.0)) / TOKEN_TOTAL
    baseline_rate = jnp.where(fast, fast_rate, slow_rate)
    rough_values = jnp.exp(jax.random.uniform(rough_key, (TOKEN_TOTAL, HEAD_TOTAL), jnp.float32, -0.693, 0.693))
    place_indices = jax.random.randint(place_key, (3,), 0, TOKEN_TOTAL)
    amount_values = jax.random.uniform(spike_key, (3, HEAD_TOTAL), jnp.float32, 0.25, 0.35)
    token_positions = jnp.arange(TOKEN_TOTAL)
    spike_values = jnp.zeros((TOKEN_TOTAL, HEAD_TOTAL), jnp.float32)
    for which_index in range(3):
        spike_values = spike_values + jnp.where((token_positions == place_indices[which_index])[:, None], amount_values[which_index][None, :], 0.0)
    return baseline_rate[None, :] * rough_values + spike_values


def level_of(key, dims, split, low, high):
    def one(dim, blocks):
        steps = jax.random.uniform(jax.random.fold_in(jax.random.fold_in(key, 6), dim), (blocks,), jnp.float32, low / len(split), high / len(split))
        return jnp.repeat(jnp.exp(steps), dims[dim] // blocks).reshape((-1,) + (1,) * (len(dims) - dim - 1))

    factor_of = one(*split[0])
    for cut in split[1:]:
        factor_of = factor_of * one(*cut)
    return factor_of


def bell_draw(stream_key, shape, scale, most, shards=(), held_as=jnp.bfloat16):
    loudness = level_of(stream_key, shape, shards, -0.22, 0.18) if shards else 1.0
    values = jax.random.normal(stream_key, shape, jnp.float32) * scale * loudness
    return jnp.minimum(jnp.maximum(values, -most), most).astype(held_as)


def setup_inputs(seed: int = 0) -> dict:
    arg_keys = jax.random.split(jax.random.key(seed), 11)
    return {
        "query_proj": draw_query_proj(jax.random.fold_in(arg_keys[10], 71), 0),
        "keyval_proj": draw_keyval_proj(jax.random.fold_in(arg_keys[10], 71), 0),
        "hidden": bell_draw(arg_keys[2], (TOKEN_TOTAL, D), 1.0, 6.0, ((0, 64), (1, 8))),
        "weight_x": bell_draw(arg_keys[3], (D, KV * HD), D ** -0.5, 0.09375, ((1, 8),)),
        "conv_x": bell_draw(arg_keys[4], (CONV, KV * HD), CONV ** -0.5, 3.0, ((1, 8),), jnp.float32),
        "conv_b": bell_draw(arg_keys[5], (CONV, KV * HD), CONV ** -0.5, 3.0, ((1, 8),), jnp.float32),
        "conv_c": bell_draw(arg_keys[6], (CONV, HEAD_TOTAL * HD), CONV ** -0.5, 3.0, ((1, 8),), jnp.float32),
        "step_size": draw_step_size(jax.random.fold_in(arg_keys[10], 71), 0),
        "decay_log": jnp.clip(jax.random.uniform(arg_keys[8], (HEAD_TOTAL,), jnp.float32, -0.5, 0.5) * level_of(arg_keys[8], (HEAD_TOTAL,), ((0, 8),), -0.4, 0.0), -0.5, 0.5),
        "skip_gain": jnp.clip(0.5 + 1.0 * jax.random.uniform(arg_keys[9], (HEAD_TOTAL,), jnp.float32) ** level_of(arg_keys[9], (HEAD_TOTAL,), ((0, 8),), -0.2, 0.2), 0.5, 1.5),
    }


highest_precision = lax.Precision.HIGHEST

def causal_conv(signal, kernel):
    length = signal.shape[0]
    padded = jnp.pad(signal, ((CONV - 1, 0), (0, 0)))
    result = jnp.zeros_like(signal)
    for offset in range(CONV):
        result = result + kernel[offset][None, :] * padded[offset:offset + length]
    return result

def teacher_attention(query_proj, keyval_proj):
    per_group = HEAD_TOTAL // KV
    key_all = keyval_proj[:, :, :HD].astype(jnp.float32)
    value_all = keyval_proj[:, :, HD:].astype(jnp.float32)
    queries = query_proj.reshape(TOKEN_TOTAL, KV, per_group, HD)
    block_size = TOK_DEV
    block_count = TOKEN_TOTAL // block_size
    token_positions = jnp.arange(TOKEN_TOTAL, dtype=jnp.int32)

    def per_block(block_index):
        first = block_index * block_size
        query_block = lax.dynamic_slice_in_dim(queries, first, block_size, 0)
        row_pos = first + jnp.arange(block_size, dtype=jnp.int32)
        allowed = token_positions[None, :] <= row_pos[:, None]

        def per_head_group(group_index):
            query_group = lax.dynamic_index_in_dim(query_block, group_index, 1, keepdims=False).astype(jnp.float32)
            key_group = lax.dynamic_index_in_dim(key_all, group_index, 1, keepdims=False)
            value_group = lax.dynamic_index_in_dim(value_all, group_index, 1, keepdims=False)
            scores = jnp.einsum('brd,kd->rbk', query_group, key_group) * HD ** (-0.5)
            scores = jnp.where(allowed[None], scores, -1e+30)
            row_max = lax.optimization_barrier(jnp.max(scores, axis=2, keepdims=True))
            weights = jnp.where(allowed[None], jnp.exp(scores - row_max), 0.0)
            totals = lax.optimization_barrier(jnp.sum(weights, axis=2, keepdims=True))
            rounded = lax.optimization_barrier(weights.astype(jnp.bfloat16)).astype(jnp.float32)
            mixed = jnp.einsum('rbk,kd->rbd', rounded, value_group)
            return jnp.transpose(mixed / totals, (1, 0, 2))
        return lax.map(per_head_group, jnp.arange(KV, dtype=jnp.int32))
    blocks = lax.map(per_block, jnp.arange(block_count, dtype=jnp.int32))
    return jnp.transpose(blocks, (0, 2, 1, 3, 4)).reshape(TOKEN_TOTAL, HEAD_TOTAL * HD)

def student_scan(x_conv, b_conv, c_conv, step_size, decay_log, skip_gain):
    per_group = HEAD_TOTAL // KV
    block_size = TOK_DEV
    block_count = TOKEN_TOTAL // block_size
    decay_rate = -jnp.exp(decay_log).reshape(KV, per_group)
    skip_heads = skip_gain.reshape(KV, per_group)
    x_blocks = x_conv.reshape(block_count, block_size, KV, HD)
    b_blocks = b_conv.reshape(block_count, block_size, KV, HD)
    c_blocks = c_conv.reshape(block_count, block_size, KV, per_group, HD)
    step_blocks = step_size.reshape(block_count, block_size, KV, per_group)
    causal = jnp.arange(block_size)[:, None] >= jnp.arange(block_size)[None, :]

    def advance(state_now, inputs):
        x_block, input_proj_block, readout_block, step_block = inputs
        log_decay = jnp.cumsum(step_block * decay_rate[None], axis=0)
        ordered = jnp.transpose(log_decay, (1, 2, 0))
        differ = ordered[:, :, :, None] - ordered[:, :, None, :]
        within = jnp.where(causal, jnp.exp(jnp.where(causal, differ, 0.0)), 0.0)
        pairwise_scores = jnp.einsum('qmzo,imo->mzqi', readout_block, input_proj_block, precision=highest_precision)
        mixing_weights = pairwise_scores * within
        driven_state = step_block[..., None] * x_block[:, :, None, :]
        inner_portion = jnp.einsum('hewl,lhen->when', mixing_weights, driven_state, precision=highest_precision)
        carried = jnp.exp(log_decay)[..., None] * jnp.einsum('tgrn,grnp->tgrp', readout_block, state_now, precision=highest_precision)
        output = inner_portion + carried + skip_heads[None, :, :, None] * x_block[:, :, None, :]
        to_end = jnp.exp(log_decay[-1][None] - log_decay)
        added = jnp.einsum('sgn,sgrp->grnp', input_proj_block, to_end[..., None] * driven_state, precision=highest_precision)
        state_next = jnp.exp(log_decay[-1])[..., None, None] * state_now + added
        return (state_next, output)
    start_state = jnp.zeros((KV, per_group, HD, HD), jnp.float32)
    final_state, outputs = lax.scan(advance, start_state, (x_blocks, b_blocks, c_blocks, step_blocks))
    return outputs.reshape(TOKEN_TOTAL, HEAD_TOTAL * HD)

def reference(query_proj, keyval_proj, hidden, weight_x, conv_x, conv_b, conv_c, step_size, decay_log, skip_gain):
    x_input = jnp.dot(hidden, weight_x, preferred_element_type=jnp.float32).astype(jnp.bfloat16)
    x_pre = causal_conv(x_input.astype(jnp.float32), conv_x)
    x_conv = jax.nn.silu(x_pre)
    key_rows = keyval_proj[:, :, :HD].reshape(TOKEN_TOTAL, KV * HD).astype(jnp.float32)
    b_conv = jax.nn.silu(causal_conv(key_rows, conv_b))
    c_conv = jax.nn.silu(causal_conv(query_proj.astype(jnp.float32), conv_c))

    def forward(value):
        return student_scan(value, b_conv, c_conv, step_size, decay_log, skip_gain)
    student, pullback = jax.vjp(forward, x_conv)
    target = teacher_attention(query_proj, keyval_proj)
    upstream_gradient = 2.0 * (student - target) / (HEAD_TOTAL * HD)
    x_grad = pullback(upstream_gradient)[0]
    sigmoid_x = jax.nn.sigmoid(x_pre)
    pre_grad = x_grad * sigmoid_x * (1.0 + x_pre * (1.0 - sigmoid_x))
    padded = jnp.pad(pre_grad, ((0, CONV - 1), (0, 0)))
    input_grad = jnp.zeros_like(pre_grad)
    for offset in range(CONV):
        input_grad = input_grad + conv_x[offset][None, :] * padded[CONV - 1 - offset:CONV - 1 - offset + TOKEN_TOTAL]
    weight_grad = jnp.dot(hidden.T, input_grad.astype(jnp.bfloat16), preferred_element_type=jnp.float32)
    return (student.astype(jnp.bfloat16), weight_grad)
```

```python
import functools

import jax
import jax.numpy as jnp
from jax import lax
from jax.experimental import pallas as pl
from jax.experimental.pallas import tpu as pltpu
from jax.sharding import Mesh
from jax.sharding import PartitionSpec as P

HEAD_TOTAL = 32
KV = 8
HD = 128
CONV = 4
TOK = 128
PER = HEAD_TOTAL // KV
NX, NZ, NK, NM = 4, 8, 2, 8
CTX = ("ctx_0", "ctx_1", "ctx_2")
CTX_MP = ("ctx_0", "ctx_1", "ctx_2", "mp")
MESH = pl.DeviceIdType.MESH
F32, BF16 = jnp.float32, jnp.bfloat16
NEG = -1e30
SCALE2 = HD**-0.5 * 1.4426950408889634


def place():
    return tuple(lax.axis_index(name) for name in CTX_MP)


def remote(src, dst, send, recv, device):
    return pltpu.make_async_remote_copy(
        src_ref=src, dst_ref=dst, send_sem=send, recv_sem=recv, device_id=device, device_id_type=MESH
    )


def greet(devices):
    barrier = pltpu.get_barrier_semaphore()
    for device in devices:
        pl.semaphore_signal(barrier, inc=1, device_id=device, device_id_type=MESH)
    pl.semaphore_wait(barrier, len(devices))


def exact(a, b, dims=((1,), (0,))):
    return lax.dot_general(
        a, b, (dims, ((), ())), precision=lax.Precision.HIGHEST, preferred_element_type=F32
    )


def front(
    q_in, kv_in, hid_in, wx,
    target, q_loc, k_loc, xin, hidq,
    q2, kvb, hall, qs, m_s, l_s, acc, stat, acc_in, stat_in,
    own_sem, yq, ykv, yh, xkv, ring, cq, co, hq,
):
    x, z, k, m = place()
    zr, zl = lax.rem(z + 1, NZ), lax.rem(z + NZ - 1, NZ)
    sibling = (x, z, 1 - k, m)
    y_peers = [(x, z, k, lax.rem(m + d, NM)) for d in range(1, NM)]
    x_peers = [(lax.rem(x + d, NX), z, k, m) for d in range(1, NX)]
    greet([*y_peers, *x_peers, (x, zr, k, m), (x, zl, k, m), sibling])

    rows = pl.ds(pl.multiple_of(m * 16, 16), 16)
    sent = []
    for d in range(1, NM):
        peer = y_peers[d - 1]
        cols = pl.ds(pl.multiple_of(peer[3] * 256, 256), 256)
        sent.append(remote(kv_in.at[:, cols], kvb.at[z, x, rows], ykv.at[0, d - 1], ykv.at[1, d - 1], peer))
        sent[-1].start()
    for d in range(1, NM):
        peer = y_peers[d - 1]
        cols = pl.ds(pl.multiple_of(peer[3] * 512, 512), 512)
        sent.append(remote(q_in.at[:, cols], q2.at[0, rows], yq.at[0, d - 1], yq.at[1, d - 1], peer))
        sent[-1].start()
    y_moves = list(sent)
    for d in range(1, NM):
        sent.append(remote(hid_in, hall.at[m], yh.at[0, d - 1], yh.at[1, d - 1], y_peers[d - 1]))
        sent[-1].start()
    h_moves = sent[len(y_moves) :]
    mine = [
        pltpu.make_async_copy(
            kv_in.at[:, pl.ds(pl.multiple_of(m * 256, 256), 256)], kvb.at[z, x, rows], own_sem.at[0]
        ),
        pltpu.make_async_copy(
            q_in.at[:, pl.ds(pl.multiple_of(m * 512, 512), 512)], q2.at[0, rows], own_sem.at[1]
        ),
        pltpu.make_async_copy(hid_in, hall.at[m], own_sem.at[2]),
    ]
    for move in mine:
        move.start()

    for xs in range(1, NX):

        @pl.when(xs > x)
        def _(xs=xs):
            kvb[:, xs] = jnp.zeros((NZ, TOK, 2 * HD), BF16)

    m_s[...] = jnp.full(m_s.shape, NEG, F32)
    l_s[...] = jnp.zeros(l_s.shape, F32)
    acc[...] = jnp.zeros(acc.shape, F32)
    for move in mine:
        move.wait()

    def ring_copy(way, step, xs):
        if way == 0:
            column, device = lax.rem(z - (step - 1) + NZ, NZ), (x, zr, k, m)
        else:
            column, device = lax.rem(z + (step - 1), NZ), (x, zl, k, m)
        slot = kvb.at[column, xs]
        at = (way * 4 + step - 1) * NX + xs
        return remote(slot, slot, ring.at[0, at], ring.at[1, at], device)

    def x_copy(d):
        slot = kvb.at[z, x]
        return remote(slot, slot, xkv.at[0, d - 1], xkv.at[1, d - 1], (lax.rem(x + d, NX), z, k, m))

    for move in y_moves[: NM - 1]:
        move.wait_recv()
    for d in range(1, NX):

        @pl.when(x + d < NX)
        def _(d=d):
            x_copy(d).start()

    for xs in range(NX):

        @pl.when(xs == x)
        def _(xs=xs):
            ring_copy(0, 1, xs).start()
            ring_copy(1, 1, xs).start()

    for move in y_moves[NM - 1 :]:
        move.wait_recv()
    q_move = remote(q2.at[0], q2.at[1], cq.at[0], cq.at[1], sibling)
    q_move.start()

    for xs in range(NX):
        for d in range(1, NX):
            if xs + d < NX:

                @pl.when(x == xs + d)
                def _(xs=xs, d=d):
                    slot = kvb.at[z, xs]
                    remote(slot, slot, xkv.at[0, d - 1], xkv.at[1, d - 1], sibling).wait_recv()
                    ring_copy(0, 1, xs).start()
                    ring_copy(1, 1, xs).start()

    for h in range(PER):
        qs[0, h * TOK : (h + 1) * TOK] = q2[0, :, h * HD : (h + 1) * HD]
    q_move.wait_recv()
    for h in range(PER):
        qs[1, h * TOK : (h + 1) * TOK] = q2[1, :, h * HD : (h + 1) * HD]

    def attend(column, masked):
        def tile(i, carry):
            side, first = lax.div(i, 2), pl.multiple_of(lax.rem(i, 2) * 256, 256)
            at = pl.ds(first, 256)
            block = kvb[column].reshape(NX * TOK, 2 * HD)
            s = lax.dot_general(
                qs[side, at], block[:, :HD], (((1,), (1,)), ((), ())), preferred_element_type=F32
            )
            if masked:
                key = lax.broadcasted_iota(jnp.int32, (256, NX * TOK), 1)
                row = lax.broadcasted_iota(jnp.int32, (256, NX * TOK), 0)
                core = jnp.where(side == 0, k, 1 - k)
                ahead = (key - x * TOK) + k * TOK - (lax.rem(row, TOK) + core * TOK)
                allowed = (key < x * TOK) | ((ahead <= 0) & (key < (x + 1) * TOK))
                s = jnp.where(allowed, s * SCALE2, NEG)
            else:
                key = lax.broadcasted_iota(jnp.int32, (1, NX * TOK), 1)
                limit = jnp.where(column < z, (x + 1) * TOK, x * TOK)
                s = s * SCALE2 + jnp.where(key < limit, 0.0, NEG)
            before = m_s[side, at, :1]
            now = jnp.maximum(before, jnp.max(s, axis=1, keepdims=True))
            p = jnp.exp2(s - now)
            alpha = jnp.exp2(before - now)
            m_s[side, at] = jnp.broadcast_to(now, (256, HD))
            l_s[side, at] = l_s[side, at] * alpha + jnp.sum(p, axis=1, keepdims=True)
            acc[side, at] = acc[side, at] * alpha + jnp.dot(
                p.astype(BF16), block[:, HD:], preferred_element_type=F32
            )
            return carry

        lax.fori_loop(0, 4, tile, 0)

    attend(z, True)
    for step in range(1, 5):
        for way in range(2):
            for xs in range(NX):
                if way == 0 or step < 4:

                    @pl.when(xs <= x)
                    def _(way=way, xs=xs, step=step):
                        ring_copy(way, step, xs).wait_recv()
                        if step < (4, 3)[way]:
                            ring_copy(way, step + 1, xs).start()

        attend(lax.rem(z - step + NZ, NZ), False)
        if step < 4:
            attend(lax.rem(z + step, NZ), False)

    lane = lax.broadcasted_iota(jnp.int32, (PER * TOK, HD), 1)
    stat[...] = jnp.where(lane < 64, m_s[1], l_s[1])
    o_moves = [
        remote(acc.at[1], acc_in, co.at[0, 0], co.at[1, 0], sibling),
        remote(stat, stat_in, co.at[0, 1], co.at[1, 1], sibling),
    ]
    for move in o_moves:
        move.start()

    for move in h_moves:
        move.wait_recv()
    hq_moves = []
    for d in range(1, NX):
        there = lax.rem(x + d, NX)
        for e in range(2):
            at = (d - 1) * 2 + e
            into = hidq.at[e, pl.ds(pl.multiple_of(x * TOK, TOK), TOK)]
            hq_moves.append(
                remote(hall.at[2 * there + e], into, hq.at[0, at], hq.at[1, at], x_peers[d - 1])
            )
            hq_moves[-1].start()
    for e in range(2):
        hidq[e, pl.ds(pl.multiple_of(x * TOK, TOK), TOK)] = hall[2 * x + e]
    total = jnp.zeros((TOK, HD), F32)
    for j in range(NM):
        total = total + jnp.dot(hall[j], wx[j * 512 : (j + 1) * 512], preferred_element_type=F32)
    xin[...] = total.astype(BF16)
    q_loc[...] = q2[0]
    k_loc[...] = kvb[z, x, :, :HD]

    for move in o_moves:
        move.wait_recv()
    other = stat_in[:, :1]
    mine_max = m_s[0, :, :1]
    both = jnp.maximum(other, mine_max)
    a0, a1 = jnp.exp2(mine_max - both), jnp.exp2(other - both)
    norm = l_s[0, :, :1] * a0 + stat_in[:, 64:65] * a1
    result = (acc[0] * a0 + acc_in[...] * a1) / norm
    for h in range(PER):
        target[:, h * HD : (h + 1) * HD] = result[h * TOK : (h + 1) * TOK]

    for move in hq_moves:
        move.wait_recv()
    for move in [*sent, q_move, *o_moves, *hq_moves]:
        move.wait_send()
    for d in range(1, NX):

        @pl.when(x + d < NX)
        def _(d=d):
            x_copy(d).wait_send()

    for way in range(2):
        for step in range(1, (4, 3)[way] + 1):
            for xs in range(NX):

                @pl.when(xs <= x)
                def _(way=way, step=step, xs=xs):
                    ring_copy(way, step, xs).wait_send()


def silu(v):
    return v / (1.0 + jnp.exp(-v))


def back(
    xin, k_loc, q_loc, target, step_size, decay_log, skip_gain, conv_x, conv_b, conv_c, hidq,
    out_s, out_w,
    ext, ext2, mix, local_state, sgrad, csib, dec, dsib, zsend, zrecv, xsend, xrecv,
    zbs, zbr, cback, inc, ig, part, wrecv, wsend, wzr, up,
    halo, cs, zs, xs_, bs, ks, igs, wc, wz,
):
    x, z, k, m = place()
    c = (x * NZ + z) * NK + k
    last = NX * NZ * NK - 1
    sibling = (x, z, 1 - k, m)

    def at_ctx(i):
        return (lax.div(i, NZ * NK), lax.rem(lax.div(i, NK), NZ), lax.rem(i, NK), m)

    following, previous = at_ctx(lax.rem(c + 1, last + 1)), at_ctx(lax.rem(c + last, last + 1))
    z_peers = [(x, lax.rem(z + d, NZ), k, m) for d in range(1, NZ)]
    x_peers = [(lax.rem(x + d, NX), z, k, m) for d in range(1, NX)]
    greet([*z_peers, *x_peers, sibling, following, previous])
    sent = []

    def go(*args):
        move = remote(*args)
        move.start()
        sent.append(move)
        return move

    ext[8:, :HD] = xin[...].astype(F32)
    ext[8:, HD : 2 * HD] = k_loc[...].astype(F32)
    ext[8:, 2 * HD :] = q_loc[...].astype(F32)
    tail = remote(ext.at[pl.ds(TOK, 8)], ext.at[pl.ds(0, 8)], halo.at[0], halo.at[1], following)

    @pl.when(c < last)
    def _():
        tail.start()

    @pl.when(c == 0)
    def _():
        ext[:8] = jnp.zeros((8, 6 * HD), F32)

    row = lax.broadcasted_iota(jnp.int32, (TOK, TOK), 0)
    col = lax.broadcasted_iota(jnp.int32, (TOK, TOK), 1)
    causal = row >= col
    lower = jnp.where(causal, 1.0, 0.0)
    rate = -jnp.exp(decay_log[...])
    steps, growth, to_end, within = [], [], [], []
    for h in range(PER):
        step = jnp.broadcast_to(step_size[:, h : h + 1], (TOK, TOK))
        log_decay = exact(lower, step * rate[:, h : h + 1])
        final = log_decay[TOK - 1 :]
        steps.append(step)
        growth.append(jnp.exp(log_decay))
        to_end.append(jnp.exp(final - log_decay))
        within.append(
            jnp.where(causal, jnp.exp(jnp.where(causal, log_decay - log_decay.T, 0.0)), 0.0)
        )
        dec[h : h + 1] = jnp.exp(final)
        dec[PER + h : PER + h + 1] = jnp.exp(final)

    @pl.when(c > 0)
    def _():
        tail.wait_recv()

    def conv(first, taps):
        width = taps.shape[1]
        total = jnp.zeros((TOK, width), F32)
        for j in range(CONV):
            total = total + taps[j : j + 1, :] * ext[5 + j : 5 + j + TOK, first : first + width]
        return total

    x_pre = conv(0, conv_x)
    x_conv = silu(x_pre)
    b_conv = silu(conv(HD, conv_b))
    c_conv = silu(conv(2 * HD, conv_c))
    b_t = b_conv.T
    read = [c_conv[:, h * HD : (h + 1) * HD] for h in range(PER)]
    driven = [steps[h] * x_conv for h in range(PER)]
    for h in range(PER):
        local_state[h] = exact(b_t, to_end[h] * driven[h])

    first_of = pl.ds(2 * k, 2)
    first_other = pl.ds(2 * (1 - k), 2)

    def scan(way, state):
        moves = [go(state.at[first_other], csib.at[way], cs.at[0, way], cs.at[1, way], sibling)]
        if way == 0:
            moves.append(go(dec, dsib, cs.at[0, 2], cs.at[1, 2], sibling))
        yield
        for move in moves:
            move.wait_recv()
        d_mine = [jnp.where(k == 0, dec[h : h + 1], dec[2 + h : 3 + h]) for h in range(2)]
        d_other = [jnp.where(k == 0, dsib[h : h + 1], dsib[2 + h : 3 + h]) for h in range(2)]
        d_chip = [d_mine[h] * d_other[h] for h in range(2)]
        nearer_is_mine = (k == 1) if way == 0 else (k == 0)
        own, theirs = state[first_of], csib[way]
        for h in range(2):
            near = jnp.where(nearer_is_mine, own[h], theirs[h])
            far = jnp.where(nearer_is_mine, theirs[h], own[h])
            d_near = jnp.where(nearer_is_mine, d_mine[h], d_other[h])
            chip = far * d_near + near
            for i in range(4):
                zsend[way, h * 4 + i, :32] = chip[i * 32 : (i + 1) * 32]
                zsend[way, h * 4 + i, 32:] = jnp.broadcast_to(d_chip[h], (8, HD))
        moves = []
        for d in range(1, NZ):
            there = lax.rem(z + d, NZ)
            moves.append(
                go(
                    zsend.at[way, there], zrecv.at[way, z],
                    zs.at[0, way, d - 1], zs.at[1, way, d - 1], z_peers[d - 1],
                )
            )
        zrecv[way, z] = zsend[way, z]
        for move in moves:
            move.wait_recv()
        along = range(NZ) if way == 0 else range(NZ - 1, -1, -1)
        total, decay = jnp.zeros((32, HD), F32), jnp.ones((1, HD), F32)
        for i in along:
            d_i = zrecv[way, i, 32:33]
            total, decay = d_i * total + zrecv[way, i, :32], decay * d_i
        xsend[way, :32] = total
        xsend[way, 32:] = jnp.broadcast_to(decay, (8, HD))
        moves = [
            go(
                xsend.at[way], xrecv.at[way, x],
                xs_.at[0, way, d - 1], xs_.at[1, way, d - 1], x_peers[d - 1],
            )
            for d in range(1, NX)
        ]
        xrecv[way, x] = xsend[way]
        for move in moves:
            move.wait_recv()
        enters = jnp.zeros((32, HD), F32)
        for i in range(NX) if way == 0 else range(NX - 1, -1, -1):
            passed = (i < x) if way == 0 else (i > x)
            enters = jnp.where(passed, xrecv[way, i, 32:33] * enters + xrecv[way, i, :32], enters)
        for i in along:
            zbs[way, i] = enters
            enters = zrecv[way, i, 32:33] * enters + zrecv[way, i, :32]
        moves = []
        for d in range(1, NZ):
            there = lax.rem(z + d, NZ)
            moves.append(
                go(
                    zbs.at[way, there], zbr.at[way, z],
                    bs.at[0, way, d - 1], bs.at[1, way, d - 1], z_peers[d - 1],
                )
            )
        zbr[way, z] = zbs[way, z]
        for move in moves:
            move.wait_recv()
        for h in range(2):
            entering = zbr[way, 4 * h : 4 * h + 4].reshape(HD, HD)
            mine_first = (k == 0) if way == 0 else (k == 1)
            d_first = jnp.where(mine_first, d_mine[h], d_other[h])
            s_first = jnp.where(mine_first, own[h], theirs[h])
            second = d_first * entering + s_first
            inc[way, 2 * k + h] = jnp.where(mine_first, entering, second)
            cback[way, h] = jnp.where(mine_first, second, entering)
        move = go(cback.at[way], inc.at[way, first_of], ks.at[0, way], ks.at[1, way], sibling)
        yield
        move.wait_recv()
        yield

    forward = scan(0, local_state)
    next(forward)
    inner = []
    for h in range(PER):
        mix[h] = exact(read[h], b_t) * within[h]
        inner.append(exact(mix[h], driven[h]) + skip_gain[:, h : h + 1] * x_conv)
    next(forward)
    next(forward)
    for h in range(PER):
        student = inner[h] + growth[h] * exact(read[h], inc[0, h])
        at = slice(h * HD, (h + 1) * HD)
        out_s[:, at] = student.astype(BF16)
        up[h] = 2.0 * (student - target[:, at]) / (HEAD_TOTAL * HD)
        sgrad[h] = exact((growth[h] * read[h]).T, up[h])

    backward = scan(1, sgrad)
    next(backward)
    x_grad = jnp.zeros((TOK, HD), F32)
    for h in range(PER):
        x_grad = x_grad + steps[h] * exact(mix[h].T, up[h]) + skip_gain[:, h : h + 1] * up[h]
    next(backward)
    next(backward)
    for h in range(PER):
        x_grad = x_grad + steps[h] * to_end[h] * exact(b_conv, inc[1, h])
    sigma = 1.0 / (1.0 + jnp.exp(-x_pre))
    ext2[:TOK] = x_grad * sigma * (1.0 + x_pre * (1.0 - sigma))
    head = remote(ext2.at[pl.ds(0, 8)], ext2.at[pl.ds(TOK, 8)], halo.at[2], halo.at[3], previous)

    @pl.when(c > 0)
    def _():
        head.start()

    @pl.when(c == last)
    def _():
        ext2[TOK:] = jnp.zeros((8, HD), F32)

    @pl.when(c < last)
    def _():
        head.wait_recv()

    grad = jnp.zeros((TOK, HD), F32)
    for j in range(CONV):
        grad = grad + conv_x[j : j + 1, :] * ext2[CONV - 1 - j : CONV - 1 - j + TOK]
    here = ig.at[pl.ds(pl.multiple_of(x * TOK, TOK), TOK)]
    here[...] = grad.astype(BF16)
    moves = [
        go(here, here, igs.at[0, d - 1], igs.at[1, d - 1], x_peers[d - 1]) for d in range(1, NX)
    ]
    for move in moves:
        move.wait_recv()
    for e in range(2):
        product = lax.dot_general(
            hidq[e], ig[...], (((0,), (0,)), ((), ())), preferred_element_type=F32
        )
        part[4 * e : 4 * e + 4] = product.reshape(4, NK, 64, HD)
    go(part.at[:, 1 - k], wrecv, wc.at[0], wc.at[1], sibling).wait_recv()
    for i in range(NZ):
        wsend[i] = part[i, k] + wrecv[i]
    moves = []
    for d in range(1, NZ):
        there = lax.rem(z + d, NZ)
        moves.append(go(wsend.at[there], wzr.at[z], wz.at[0, d - 1], wz.at[1, d - 1], z_peers[d - 1]))
    wzr[z] = wsend[z]
    for move in moves:
        move.wait_recv()
    total = wzr[0]
    for i in range(1, NZ):
        total = total + wzr[i]
    out_w[...] = total

    for move in sent:
        move.wait_send()

    @pl.when(c < last)
    def _():
        tail.wait_send()

    @pl.when(c > 0)
    def _():
        head.wait_send()


def shape(dims, dtype=F32):
    return jax.ShapeDtypeStruct(dims, dtype)


def dma(*dims):
    return pltpu.SemaphoreType.DMA(dims)


def call(kernel, collective, outs, scratch, args, limit):
    return pl.pallas_call(
        kernel,
        out_shape=outs,
        in_specs=[pl.BlockSpec(memory_space=pltpu.VMEM)] * len(args),
        out_specs=[pl.BlockSpec(memory_space=pltpu.VMEM)] * len(outs),
        scratch_shapes=scratch,
        compiler_params=pltpu.CompilerParams(
            collective_id=collective, has_side_effects=True, vmem_limit_bytes=limit
        ),
    )(*args)


def local(
    query_proj, keyval_proj, hidden, weight_x, conv_x, conv_b, conv_c, step_size, decay_log, skip_gain
):
    vm = pltpu.VMEM
    target, q_loc, k_loc, xin, hidq = call(
        front,
        0,
        (
            shape((TOK, PER * HD)), shape((TOK, PER * HD), BF16), shape((TOK, HD), BF16),
            shape((TOK, HD), BF16), shape((2, NX * TOK, 512), BF16),
        ),
        [
            vm((2, TOK, PER * HD), BF16), vm((NZ, NX, TOK, 2 * HD), BF16), vm((NM, TOK, 512), BF16),
            vm((2, PER * TOK, HD), BF16), vm((2, PER * TOK, HD), F32), vm((2, PER * TOK, HD), F32),
            vm((2, PER * TOK, HD), F32), vm((PER * TOK, HD), F32), vm((PER * TOK, HD), F32),
            vm((PER * TOK, HD), F32),
            dma(3), dma(2, 7), dma(2, 7), dma(2, 7), dma(2, 3), dma(2, 32), dma(2), dma(2, 2), dma(2, 6),
        ],
        (query_proj, keyval_proj.reshape(16, KV * 2 * HD), hidden, weight_x),
        40 * 2**20,
    )
    student, weight_grad = call(
        back,
        1,
        (shape((TOK, PER * HD), BF16), shape((64, HD))),
        [
            vm((TOK + 8, 6 * HD), F32), vm((TOK + 8, HD), F32), vm((PER, TOK, TOK), F32),
            vm((PER, HD, HD), F32), vm((PER, HD, HD), F32), vm((2, 2, HD, HD), F32),
            vm((8, HD), F32), vm((8, HD), F32),
            vm((2, NZ, 40, HD), F32), vm((2, NZ, 40, HD), F32), vm((2, 40, HD), F32), vm((2, NX, 40, HD), F32),
            vm((2, NZ, 32, HD), F32), vm((2, NZ, 32, HD), F32), vm((2, 2, HD, HD), F32),
            vm((2, PER, HD, HD), F32), vm((NX * TOK, HD), BF16), vm((NZ, NK, 64, HD), F32),
            vm((NZ, 64, HD), F32), vm((NZ, 64, HD), F32), vm((NZ, 64, HD), F32), vm((PER, TOK, HD), F32),
            dma(4), dma(2, 3), dma(2, 2, 7), dma(2, 2, 3), dma(2, 2, 7), dma(2, 2), dma(2, 3), dma(2), dma(2, 7),
        ],
        (
            xin, k_loc, q_loc, target, step_size, decay_log.reshape(1, PER), skip_gain.reshape(1, PER),
            conv_x, conv_b, conv_c, hidq,
        ),
        40 * 2**20,
    )
    return student, weight_grad


def solution(mesh):
    finer = Mesh(mesh.devices.reshape(NX, NZ, NK, mesh.shape["mp"]), CTX_MP)
    placed = (
        P(CTX_MP, None),
        P(CTX_MP, None, None),
        P(CTX, "mp"),
        P(None, "mp"),
        P(None, "mp"),
        P(None, "mp"),
        P(None, "mp"),
        P(CTX, "mp"),
        P("mp"),
        P("mp"),
    )
    return jax.shard_map(
        local, mesh=finer, in_specs=placed, out_specs=(P(CTX, "mp"), P(CTX, "mp")), check_vma=False
    )
```

```python
import types

import jax
import jax.numpy as jnp
from jax import lax
from jax.experimental import pallas as pl
from jax.experimental.pallas import tpu as pltpu
from jax.sharding import Mesh
from jax.sharding import PartitionSpec as P

HEAD_TOTAL = 32
KV = 8
HD = 128
CONV = 4
TOK = 128
PER = HEAD_TOTAL // KV
NX, NZ, NK, NM = 4, 8, 2, 8
CHIPS = NX * NZ
LAST = CHIPS * NK - 1
CTX = ("ctx_0", "ctx_1", "ctx_2")
CTX_MP = ("ctx_0", "ctx_1", "ctx_2", "mp")
MESH = pl.DeviceIdType.MESH
F32, BF16 = jnp.float32, jnp.bfloat16
NEG = -1e30
SCALE2 = HD**-0.5 * 1.4426950408889634
OFFSETS = sorted(
    ((a, b) for a in range(NX) for b in range(NZ) if a or b),
    key=lambda ab: -(min(ab[0], NX - ab[0]) + min(ab[1], NZ - ab[1])),
)


def place():
    return tuple(lax.axis_index(name) for name in CTX_MP)


def remote(src, dst, send, recv, device):
    return pltpu.make_async_remote_copy(
        src_ref=src, dst_ref=dst, send_sem=send, recv_sem=recv, device_id=device, device_id_type=MESH
    )


def greet(devices):
    barrier = pltpu.get_barrier_semaphore()
    for device in devices:
        pl.semaphore_signal(barrier, inc=1, device_id=device, device_id_type=MESH)
    pl.semaphore_wait(barrier, len(devices))


def exact(a, b, dims=((1,), (0,))):
    return lax.dot_general(
        a, b, (dims, ((), ())), precision=lax.Precision.HIGHEST, preferred_element_type=F32
    )


def silu(v):
    return v / (1.0 + jnp.exp(-v))


def dma(*dims):
    return pltpu.SemaphoreType.DMA(dims)


def scratch():
    vm = pltpu.VMEM
    return {
        "q2": vm((2, TOK, PER * HD), BF16),
        "kvb": vm((NZ, NX, TOK, 2 * HD), BF16),
        "hall": vm((NM, TOK, 512), BF16),
        "hidq": vm((2, NX * TOK, 512), BF16),
        "qs": vm((2, PER * TOK, HD), BF16),
        "m_s": vm((2, PER * TOK, HD), F32),
        "l_s": vm((2, PER * TOK, HD), F32),
        "acc": vm((2, PER * TOK, HD), F32),
        "stat": vm((PER * TOK, HD), F32),
        "acc_in": vm((PER * TOK, HD), F32),
        "stat_in": vm((PER * TOK, HD), F32),
        "target": vm((PER, TOK, HD), F32),
        "ext": vm((TOK + 8, 6 * HD), F32),
        "ext2": vm((TOK + 8, HD), F32),
        "growth": vm((PER, TOK, TOK), F32),
        "to_end": vm((PER, TOK, TOK), F32),
        "within": vm((PER, TOK, TOK), F32),
        "mix": vm((PER, TOK, TOK), F32),
        "read": vm((PER, TOK, HD), F32),
        "inner": vm((PER, TOK, HD), F32),
        "up": vm((PER, TOK, HD), F32),
        "bconv": vm((TOK, HD), F32),
        "xconv": vm((TOK, HD), F32),
        "xpre": vm((TOK, HD), F32),
        "state": vm((2, PER, HD, HD), F32),
        "csib": vm((2, 2, HD, HD), F32),
        "cback": vm((2, 2, HD, HD), F32),
        "inc": vm((2, PER, HD, HD), F32),
        "dec": vm((8, HD), F32),
        "dsib": vm((8, HD), F32),
        "dsend": vm((2, 8, HD), F32),
        "drecv": vm((CHIPS, 8, HD), F32),
        "zsend": vm((2, CHIPS, 8, HD), F32),
        "zrecv": vm((2, CHIPS, 8, HD), F32),
        "zbs": vm((2, CHIPS, 8, HD), F32),
        "zbr": vm((2, CHIPS, 8, HD), F32),
        "ig": vm((NX * TOK, HD), BF16),
        "part": vm((NZ, NK, 64, HD), F32),
        "wrecv": vm((NZ, 64, HD), F32),
        "wsend": vm((NZ, 64, HD), F32),
        "wzr": vm((NZ, 64, HD), F32),
        "own_s": dma(3),
        "yq": dma(2, 7),
        "ykv": dma(2, 7),
        "yh": dma(2, 7),
        "xkv": dma(2, NX),
        "xf": dma(2, NX * NZ),
        "ring": dma(2, 32),
        "cq": dma(2),
        "co": dma(2, 2),
        "hq": dma(2, 6),
        "halo": dma(2, 3),
        "cs": dma(2, 3),
        "ds": dma(2, 31),
        "zs": dma(2, 62),
        "bs": dma(2, 62),
        "ks": dma(2, 2),
        "igs": dma(2, 3),
        "wc": dma(2),
        "wz": dma(2, 7),
    }


def layer(
    q_in, kv_in, hid_in, wx, step_size, decay_log, skip_gain, conv_x, conv_b, conv_c, out_s, out_w, *rest
):
    r = types.SimpleNamespace(**dict(zip(scratch(), rest, strict=True)))
    x, z, k, m = place()
    chip = x * NZ + z
    c = chip * NK + k
    sibling = (x, z, 1 - k, m)
    zr, zl = lax.rem(z + 1, NZ), lax.rem(z + NZ - 1, NZ)
    y_peers = [(x, z, k, lax.rem(m + d, NM)) for d in range(1, NM)]
    x_peers = [(lax.rem(x + d, NX), z, k, m) for d in range(1, NX)]
    z_peers = [(x, lax.rem(z + d, NZ), k, m) for d in range(1, NZ)]
    plane = [(lax.rem(x + a, NX), lax.rem(z + b, NZ), k, m) for a, b in OFFSETS]

    def at_ctx(i):
        return (lax.div(i, NZ * NK), lax.rem(lax.div(i, NK), NZ), lax.rem(i, NK), m)

    following, previous = at_ctx(lax.rem(c + 1, LAST + 1)), at_ctx(lax.rem(c + LAST, LAST + 1))
    greet([*y_peers, *plane, sibling, following, previous])
    sent = []

    def go(*args):
        move = remote(*args)
        move.start()
        sent.append(move)
        return move

    def arrived(moves):
        for move in moves:
            move.wait_recv()

    rows = pl.ds(pl.multiple_of(m * 16, 16), 16)

    def columns(i, width):
        return pl.ds(pl.multiple_of(i * width, width), width)

    kv_moves = [
        go(kv_in.at[:, columns(p[3], 256)], r.kvb.at[z, x, rows], r.ykv.at[0, d], r.ykv.at[1, d], p)
        for d, p in enumerate(y_peers)
    ]
    q_moves = [
        go(q_in.at[:, columns(p[3], 512)], r.q2.at[0, rows], r.yq.at[0, d], r.yq.at[1, d], p)
        for d, p in enumerate(y_peers)
    ]
    h_moves = [
        go(hid_in, r.hall.at[m], r.yh.at[0, d], r.yh.at[1, d], p) for d, p in enumerate(y_peers)
    ]
    mine = [
        pltpu.make_async_copy(kv_in.at[:, columns(m, 256)], r.kvb.at[z, x, rows], r.own_s.at[0]),
        pltpu.make_async_copy(q_in.at[:, columns(m, 512)], r.q2.at[0, rows], r.own_s.at[1]),
        pltpu.make_async_copy(hid_in, r.hall.at[m], r.own_s.at[2]),
    ]
    for move in mine:
        move.start()

    row = lax.broadcasted_iota(jnp.int32, (TOK, TOK), 0)
    col = lax.broadcasted_iota(jnp.int32, (TOK, TOK), 1)
    causal = row >= col
    lower = jnp.where(causal, 1.0, 0.0)
    rate = -jnp.exp(decay_log[...])

    def step_of(h):
        return jnp.broadcast_to(step_size[:, h : h + 1], (TOK, HD))

    for h in range(PER):
        log_decay = exact(lower, step_of(h) * rate[:, h : h + 1])
        final = log_decay[TOK - 1 :]
        r.growth[h] = jnp.exp(log_decay)
        r.to_end[h] = jnp.exp(final - log_decay)
        r.within[h] = jnp.where(
            causal, jnp.exp(jnp.where(causal, log_decay - log_decay.T, 0.0)), 0.0
        )
        r.dec[h : h + 1] = jnp.exp(final)
        r.dec[PER + h : PER + h + 1] = jnp.exp(final)
    d_move = go(r.dec, r.dsib, r.cs.at[0, 2], r.cs.at[1, 2], sibling)

    for xs in range(1, NX):

        @pl.when(xs > x)
        def _(xs=xs):
            r.kvb[:, xs] = jnp.zeros((NZ, TOK, 2 * HD), BF16)

    r.m_s[...] = jnp.full(r.m_s.shape, NEG, F32)
    r.l_s[...] = jnp.zeros(r.l_s.shape, F32)
    r.acc[...] = jnp.zeros(r.acc.shape, F32)

    def in_ring(xs):
        return (x == xs) | (x == xs + 2) | ((x == 1) & (xs == 0))

    def by_x(xs):
        return (x == 3 - xs) if xs < 2 else (x == 3) & (xs == 2)

    def ring_copy(way, step, xs):
        if way == 0:
            column, device = lax.rem(z - (step - 1) + NZ, NZ), (x, zr, k, m)
        else:
            column, device = lax.rem(z + (step - 1), NZ), (x, zl, k, m)
        slot = r.kvb.at[column, xs]
        at = (way * 4 + step - 1) * NX + xs
        return remote(slot, slot, r.ring.at[0, at], r.ring.at[1, at], device)

    def first_copy(xs, to):
        slot = r.kvb.at[z, xs]
        return remote(slot, slot, r.xkv.at[0, to], r.xkv.at[1, to], (to, z, k, m))

    FIRST = ((0, 1), (0, 2), (1, 3))

    def across(column, xs):
        to = (3, 2, 3)[xs]
        slot, at = r.kvb.at[column, xs], xs * NZ + column
        return remote(slot, slot, r.xf.at[0, at], r.xf.at[1, at], (to, z, k, m))

    for move in mine:
        move.wait()
    arrived(kv_moves)
    for xs in range(NX):

        @pl.when(x == xs)
        def _(xs=xs):
            for source, to in FIRST:
                if source == xs:
                    first_copy(xs, to).start()
            ring_copy(0, 1, xs).start()
            ring_copy(1, 1, xs).start()
            if xs < 3:
                across(z, xs).start()

    d_move.wait_recv()
    for h in range(2):
        chip_decay = r.dec[...] * r.dsib[...]
        decay_row = jnp.where(k == 0, chip_decay[h : h + 1], chip_decay[2 + h : 3 + h])
        r.dsend[h] = jnp.broadcast_to(decay_row, (8, HD))
    decay_moves = [
        go(r.dsend.at[lax.div(p[0], 2)], r.drecv.at[chip], r.ds.at[0, i], r.ds.at[1, i], p)
        for i, p in enumerate(plane)
    ]
    r.drecv[chip] = r.dsend[lax.div(x, 2)]

    arrived(q_moves)
    cq_move = go(r.q2.at[0], r.q2.at[1], r.cq.at[0], r.cq.at[1], sibling)
    for source, to in FIRST:

        @pl.when(x == to)
        def _(source=source, to=to):
            first_copy(source, to).wait_recv()
            ring_copy(0, 1, source).start()
            ring_copy(1, 1, source).start()

    r.ext[8:, HD : 2 * HD] = r.kvb[z, x, :, :HD].astype(F32)
    r.ext[8:, 2 * HD :] = r.q2[0].astype(F32)

    def tail(i):
        at = pl.ds(HD, 5 * HD) if i == 0 else pl.ds(0, HD)
        return remote(
            r.ext.at[pl.ds(TOK, 8), at], r.ext.at[pl.ds(0, 8), at],
            r.halo.at[0, i], r.halo.at[1, i], following,
        )

    @pl.when(c < LAST)
    def _():
        tail(0).start()

    @pl.when(c == 0)
    def _():
        r.ext[:8] = jnp.zeros((8, 6 * HD), F32)

    for h in range(PER):
        r.qs[0, h * TOK : (h + 1) * TOK] = r.q2[0, :, h * HD : (h + 1) * HD]
    cq_move.wait_recv()
    for h in range(PER):
        r.qs[1, h * TOK : (h + 1) * TOK] = r.q2[1, :, h * HD : (h + 1) * HD]

    def attend(column, masked):
        for xs in range(NX - 1):

            @pl.when(by_x(xs))
            def _(xs=xs):
                across(column, xs).wait_recv()

        def tile(i, carry):
            side, first = lax.div(i, 2), pl.multiple_of(lax.rem(i, 2) * 256, 256)
            at = pl.ds(first, 256)
            block = r.kvb[column].reshape(NX * TOK, 2 * HD)
            s = lax.dot_general(
                r.qs[side, at], block[:, :HD], (((1,), (1,)), ((), ())), preferred_element_type=F32
            )
            if masked:
                key = lax.broadcasted_iota(jnp.int32, (256, NX * TOK), 1)
                query = lax.broadcasted_iota(jnp.int32, (256, NX * TOK), 0)
                core = jnp.where(side == 0, k, 1 - k)
                ahead = (key - x * TOK) + k * TOK - (lax.rem(query, TOK) + core * TOK)
                allowed = (key < x * TOK) | ((ahead <= 0) & (key < (x + 1) * TOK))
                s = jnp.where(allowed, s * SCALE2, NEG)
            else:
                key = lax.broadcasted_iota(jnp.int32, (1, NX * TOK), 1)
                limit = jnp.where(column < z, (x + 1) * TOK, x * TOK)
                s = s * SCALE2 + jnp.where(key < limit, 0.0, NEG)
            before = r.m_s[side, at, :1]
            now = jnp.maximum(before, jnp.max(s, axis=1, keepdims=True))
            p = jnp.exp2(s - now)
            alpha = jnp.exp2(before - now)
            r.m_s[side, at] = jnp.broadcast_to(now, (256, HD))
            r.l_s[side, at] = r.l_s[side, at] * alpha + jnp.sum(p, axis=1, keepdims=True)
            r.acc[side, at] = r.acc[side, at] * alpha + jnp.dot(
                p.astype(BF16), block[:, HD:], preferred_element_type=F32
            )
            return carry

        lax.fori_loop(0, 4, tile, 0)

    def receive(step):
        for way in range(2):
            if way == 1 and step == 4:
                continue
            column = lax.rem(z - step + NZ, NZ) if way == 0 else lax.rem(z + step, NZ)
            for xs in range(NX):

                @pl.when(in_ring(xs))
                def _(way=way, xs=xs):
                    ring_copy(way, step, xs).wait_recv()
                    if step < (4, 3)[way]:
                        ring_copy(way, step + 1, xs).start()
                    if xs < 3:

                        @pl.when(x == xs)
                        def _():
                            across(column, xs).start()

    def right(step):
        return lax.rem(z - step + NZ, NZ)

    def left(step):
        return lax.rem(z + step, NZ)

    def conv(first, taps):
        width = taps.shape[1]
        total = jnp.zeros((TOK, width), F32)
        for j in range(CONV):
            total = total + taps[j : j + 1, :] * r.ext[5 + j : 5 + j + TOK, first : first + width]
        return total

    def readouts():
        @pl.when(c > 0)
        def _():
            tail(0).wait_recv()

        b_conv = silu(conv(HD, conv_b))
        r.bconv[...] = b_conv
        c_conv = silu(conv(2 * HD, conv_c))
        b_t = b_conv.T
        for h in range(PER):
            read = c_conv[:, h * HD : (h + 1) * HD]
            r.read[h] = read
            r.mix[h] = exact(read, b_t) * r.within[h]

    def project():
        arrived(h_moves)
        total = jnp.zeros((TOK, HD), F32)
        for j in range(NM):
            total = total + jnp.dot(
                r.hall[j], wx[j * 512 : (j + 1) * 512], preferred_element_type=F32
            )
        r.ext[8:, :HD] = total.astype(BF16).astype(F32)

        @pl.when(c < LAST)
        def _():
            tail(1).start()

        moves = []
        for d in range(1, NX):
            there = lax.rem(x + d, NX)
            for e in range(2):
                at = (d - 1) * 2 + e
                into = r.hidq.at[e, columns(x, TOK)]
                moves.append(
                    go(r.hall.at[2 * there + e], into, r.hq.at[0, at], r.hq.at[1, at], x_peers[d - 1])
                )
        for e in range(2):
            r.hidq[e, columns(x, TOK)] = r.hall[2 * x + e]
        return moves

    def states():
        @pl.when(c > 0)
        def _():
            tail(1).wait_recv()

        x_pre = conv(0, conv_x)
        x_conv = silu(x_pre)
        r.xpre[...] = x_pre
        r.xconv[...] = x_conv
        b_t = r.bconv[...].T
        for h in range(PER):
            r.state[0, h] = exact(b_t, r.to_end[h] * (step_of(h) * x_conv))

    def inners():
        x_conv = r.xconv[...]
        for h in range(PER):
            r.inner[h] = exact(r.mix[h], step_of(h) * x_conv) + skip_gain[:, h : h + 1] * x_conv

    first_of, first_other = pl.ds(2 * k, 2), pl.ds(2 * (1 - k), 2)

    def scan(way):
        state = r.state.at[way]
        move = go(state.at[first_other], r.csib.at[way], r.cs.at[0, way], r.cs.at[1, way], sibling)
        yield
        move.wait_recv()
        d_mine = [jnp.where(k == 0, r.dec[h : h + 1], r.dec[2 + h : 3 + h]) for h in range(2)]
        d_other = [jnp.where(k == 0, r.dsib[h : h + 1], r.dsib[2 + h : 3 + h]) for h in range(2)]
        mine_first = (k == 0) if way == 0 else (k == 1)
        for h in range(2):
            own, theirs = state[2 * k + h], r.csib[way, h]
            near = jnp.where(mine_first, theirs, own)
            far = jnp.where(mine_first, own, theirs)
            d_near = jnp.where(mine_first, d_other[h], d_mine[h])
            both = far * d_near + near
            r.zsend[way, 16 * h : 16 * h + 16] = both.reshape(16, 8, HD)
        moves = []
        for i, p in enumerate(plane):
            at = way * 31 + i
            there = p[0] * NZ + p[1]
            moves.append(
                go(r.zsend.at[way, there], r.zrecv.at[way, chip], r.zs.at[0, at], r.zs.at[1, at], p)
            )
        r.zrecv[way, chip] = r.zsend[way, chip]
        yield
        arrived(moves)
        enters = jnp.zeros((8, HD), F32)
        for j in range(CHIPS) if way == 0 else range(CHIPS - 1, -1, -1):
            r.zbs[way, j] = enters
            enters = r.drecv[j] * enters + r.zrecv[way, j]
        moves = []
        for i, p in enumerate(plane):
            at = way * 31 + i
            there = p[0] * NZ + p[1]
            moves.append(
                go(r.zbs.at[way, there], r.zbr.at[way, chip], r.bs.at[0, at], r.bs.at[1, at], p)
            )
        r.zbr[way, chip] = r.zbs[way, chip]
        yield
        arrived(moves)
        for h in range(2):
            entering = r.zbr[way, 16 * h : 16 * h + 16].reshape(HD, HD)
            own, theirs = state[2 * k + h], r.csib[way, h]
            d_first = jnp.where(mine_first, d_mine[h], d_other[h])
            second = d_first * entering + jnp.where(mine_first, own, theirs)
            r.inc[way, 2 * k + h] = jnp.where(mine_first, entering, second)
            r.cback[way, h] = jnp.where(mine_first, second, entering)
        move = go(r.cback.at[way], r.inc.at[way, first_of], r.ks.at[0, way], r.ks.at[1, way], sibling)
        yield
        move.wait_recv()
        yield

    receive(1)
    attend(z, True)
    readouts()
    receive(2)
    attend(right(1), False)
    attend(left(1), False)
    receive(3)
    attend(right(2), False)
    attend(left(2), False)
    receive(4)
    hq_moves = project()
    attend(right(3), False)
    states()
    arrived(decay_moves)
    forward = scan(0)
    next(forward)
    inners()
    next(forward)
    attend(left(3), False)
    attend(right(4), False)
    lane = lax.broadcasted_iota(jnp.int32, (PER * TOK, HD), 1)
    r.stat[...] = jnp.where(lane < 64, r.m_s[1], r.l_s[1])
    o_moves = [
        go(r.acc.at[1], r.acc_in, r.co.at[0, 0], r.co.at[1, 0], sibling),
        go(r.stat, r.stat_in, r.co.at[0, 1], r.co.at[1, 1], sibling),
    ]
    next(forward)
    arrived(o_moves)
    other, mine_max = r.stat_in[:, :1], r.m_s[0, :, :1]
    both = jnp.maximum(other, mine_max)
    a0, a1 = jnp.exp2(mine_max - both), jnp.exp2(other - both)
    norm = r.l_s[0, :, :1] * a0 + r.stat_in[:, 64:65] * a1
    r.target[...] = ((r.acc[0] * a0 + r.acc_in[...] * a1) / norm).reshape(PER, TOK, HD)
    next(forward)
    next(forward)
    for h in range(PER):
        student = r.inner[h] + r.growth[h] * exact(r.read[h], r.inc[0, h])
        out_s[:, h * HD : (h + 1) * HD] = student.astype(BF16)
        r.up[h] = 2.0 * (student - r.target[h]) / (HEAD_TOTAL * HD)
        r.state[1, h] = exact((r.growth[h] * r.read[h]).T, r.up[h])

    backward = scan(1)
    next(backward)
    next(backward)
    x_grad = jnp.zeros((TOK, HD), F32)
    for h in range(PER):
        up = r.up[h]
        x_grad = x_grad + step_of(h) * exact(r.mix[h].T, up) + skip_gain[:, h : h + 1] * up
    next(backward)
    next(backward)
    next(backward)
    b_conv = r.bconv[...]
    for h in range(PER):
        x_grad = x_grad + step_of(h) * r.to_end[h] * exact(b_conv, r.inc[1, h])
    x_pre = r.xpre[...]
    sigma = 1.0 / (1.0 + jnp.exp(-x_pre))
    r.ext2[:TOK] = x_grad * sigma * (1.0 + x_pre * (1.0 - sigma))
    head = remote(
        r.ext2.at[pl.ds(0, 8)], r.ext2.at[pl.ds(TOK, 8)], r.halo.at[0, 2], r.halo.at[1, 2], previous
    )

    @pl.when(c > 0)
    def _():
        head.start()

    @pl.when(c == LAST)
    def _():
        r.ext2[TOK:] = jnp.zeros((8, HD), F32)

    @pl.when(c < LAST)
    def _():
        head.wait_recv()

    grad = jnp.zeros((TOK, HD), F32)
    for j in range(CONV):
        grad = grad + conv_x[j : j + 1, :] * r.ext2[CONV - 1 - j : CONV - 1 - j + TOK]
    here = r.ig.at[columns(x, TOK)]
    here[...] = grad.astype(BF16)
    moves = [
        go(here, here, r.igs.at[0, d], r.igs.at[1, d], p) for d, p in enumerate(x_peers)
    ]
    arrived(hq_moves)
    arrived(moves)
    for e in range(2):
        product = lax.dot_general(
            r.hidq[e], r.ig[...], (((0,), (0,)), ((), ())), preferred_element_type=F32
        )
        r.part[4 * e : 4 * e + 4] = product.reshape(4, NK, 64, HD)
    go(r.part.at[:, 1 - k], r.wrecv, r.wc.at[0], r.wc.at[1], sibling).wait_recv()
    for i in range(NZ):
        r.wsend[i] = r.part[i, k] + r.wrecv[i]
    moves = [
        go(r.wsend.at[p[1]], r.wzr.at[z], r.wz.at[0, d], r.wz.at[1, d], p)
        for d, p in enumerate(z_peers)
    ]
    r.wzr[z] = r.wsend[z]
    arrived(moves)
    total = r.wzr[0]
    for i in range(1, NZ):
        total = total + r.wzr[i]
    out_w[...] = total

    for move in sent:
        move.wait_send()

    @pl.when(c < LAST)
    def _():
        tail(0).wait_send()
        tail(1).wait_send()

    @pl.when(c > 0)
    def _():
        head.wait_send()

    for source, to in FIRST:

        @pl.when(x == source)
        def _(source=source, to=to):
            first_copy(source, to).wait_send()

    for xs in range(NX):

        @pl.when(in_ring(xs))
        def _(xs=xs):
            for way in range(2):
                for step in range(1, (4, 3)[way] + 1):
                    ring_copy(way, step, xs).wait_send()

        if xs < 3:

            @pl.when(x == xs)
            def _(xs=xs):
                for column in range(NZ):
                    across(column, xs).wait_send()


def local(
    query_proj, keyval_proj, hidden, weight_x, conv_x, conv_b, conv_c, step_size, decay_log, skip_gain
):
    args = (
        query_proj, keyval_proj.reshape(16, KV * 2 * HD), hidden, weight_x, step_size,
        decay_log.reshape(1, PER), skip_gain.reshape(1, PER), conv_x, conv_b, conv_c,
    )
    return pl.pallas_call(
        layer,
        out_shape=(
            jax.ShapeDtypeStruct((TOK, PER * HD), BF16),
            jax.ShapeDtypeStruct((64, HD), F32),
        ),
        in_specs=[pl.BlockSpec(memory_space=pltpu.VMEM)] * len(args),
        out_specs=[pl.BlockSpec(memory_space=pltpu.VMEM)] * 2,
        scratch_shapes=list(scratch().values()),
        compiler_params=pltpu.CompilerParams(
            collective_id=0, has_side_effects=True, vmem_limit_bytes=48 * 2**20
        ),
    )(*args)


def solution(mesh):
    finer = Mesh(mesh.devices.reshape(NX, NZ, NK, mesh.shape["mp"]), CTX_MP)
    placed = (
        P(CTX_MP, None),
        P(CTX_MP, None, None),
        P(CTX, "mp"),
        P(None, "mp"),
        P(None, "mp"),
        P(None, "mp"),
        P(None, "mp"),
        P(CTX, "mp"),
        P("mp"),
        P("mp"),
    )
    return jax.shard_map(
        local, mesh=finer, in_specs=placed, out_specs=(P(CTX, "mp"), P(CTX, "mp")), check_vma=False
    )
```

```python
import types

import jax
import jax.numpy as jnp
from jax import lax
from jax.experimental import pallas as pl
from jax.experimental.pallas import tpu as pltpu
from jax.sharding import Mesh
from jax.sharding import PartitionSpec as P

HEAD_TOTAL = 32
KV = 8
HD = 128
CONV = 4
TOK = 128
PER = HEAD_TOTAL // KV
NX, NZ, NK, NM = 4, 8, 2, 8
CHIPS = NX * NZ
LAST = CHIPS * NK - 1
CTX = ("ctx_0", "ctx_1", "ctx_2")
CTX_MP = ("ctx_0", "ctx_1", "ctx_2", "mp")
MESH = pl.DeviceIdType.MESH
F32, BF16 = jnp.float32, jnp.bfloat16
NEG = -1e30
SCALE2 = HD**-0.5 * 1.4426950408889634
OFFSETS = sorted(
    ((a, b) for a in range(NX) for b in range(NZ) if a or b),
    key=lambda ab: -(min(ab[0], NX - ab[0]) + min(ab[1], NZ - ab[1])),
)


def place():
    return tuple(lax.axis_index(name) for name in CTX_MP)


def remote(src, dst, send, recv, device):
    return pltpu.make_async_remote_copy(
        src_ref=src, dst_ref=dst, send_sem=send, recv_sem=recv, device_id=device, device_id_type=MESH
    )


def greet(devices):
    barrier = pltpu.get_barrier_semaphore()
    for device in devices:
        pl.semaphore_signal(barrier, inc=1, device_id=device, device_id_type=MESH)
    pl.semaphore_wait(barrier, len(devices))


def exact(a, b, dims=((1,), (0,))):
    return lax.dot_general(
        a, b, (dims, ((), ())), precision=lax.Precision.HIGHEST, preferred_element_type=F32
    )


def silu(v):
    return v / (1.0 + jnp.exp(-v))


def dma(*dims):
    return pltpu.SemaphoreType.DMA(dims)


def scratch():
    vm = pltpu.VMEM
    return {
        "q2": vm((2, TOK, PER * HD), BF16),
        "kvb": vm((NZ, NX, TOK, 2 * HD), BF16),
        "hall": vm((NM, TOK + 16, 512), BF16),
        "wx": vm((4096, HD), BF16),
        "hidq": vm((2, NX * TOK, 512), BF16),
        "qs": vm((2, PER * TOK, HD), BF16),
        "m_s": vm((2, PER * TOK, HD), F32),
        "l_s": vm((2, PER * TOK, HD), F32),
        "acc": vm((2, PER * TOK, HD), F32),
        "stat": vm((PER * TOK, HD), F32),
        "acc_in": vm((PER * TOK, HD), F32),
        "stat_in": vm((PER * TOK, HD), F32),
        "target": vm((PER, TOK, HD), F32),
        "ext": vm((TOK + 8, 6 * HD), F32),
        "ext2": vm((TOK + 8, HD), F32),
        "growth": vm((PER, TOK, TOK), F32),
        "to_end": vm((PER, TOK, TOK), F32),
        "within": vm((PER, TOK, TOK), F32),
        "mix": vm((PER, TOK, TOK), F32),
        "read": vm((PER, TOK, HD), F32),
        "inner": vm((PER, TOK, HD), F32),
        "up": vm((PER, TOK, HD), F32),
        "bconv": vm((TOK, HD), F32),
        "xconv": vm((TOK, HD), F32),
        "xpre": vm((TOK, HD), F32),
        "state": vm((2, PER, HD, HD), F32),
        "csib": vm((2, 2, HD, HD), F32),
        "cback": vm((2, 2, HD, HD), F32),
        "inc": vm((2, PER, HD, HD), F32),
        "dec": vm((8, HD), F32),
        "dsib": vm((8, HD), F32),
        "dsend": vm((2, 8, HD), F32),
        "drecv": vm((CHIPS, 8, HD), F32),
        "zsend": vm((2, CHIPS, 8, HD), F32),
        "zrecv": vm((2, CHIPS, 8, HD), F32),
        "zbs": vm((2, CHIPS, 8, HD), F32),
        "zbr": vm((2, CHIPS, 8, HD), F32),
        "ig": vm((NX * TOK, HD), BF16),
        "part": vm((NZ, NK, 64, HD), F32),
        "wrecv": vm((NZ, 64, HD), F32),
        "wsend": vm((NZ, 64, HD), F32),
        "wzr": vm((NZ, 64, HD), F32),
        "own_s": dma(4),
        "yq": dma(2, 7),
        "ykv": dma(2, 7),
        "yh": dma(2, 24),
        "ht": dma(2),
        "xkv": dma(2, NX),
        "xf": dma(2, NX * NZ),
        "ring": dma(2, 32),
        "cq": dma(2),
        "co": dma(2, 2),
        "hq": dma(2, 6),
        "halo": dma(2, 2),
        "cs": dma(2, 3),
        "ds": dma(2, 31),
        "zs": dma(2, 62),
        "bs": dma(2, 62),
        "ks": dma(2, 2),
        "igs": dma(2, 3),
        "wc": dma(2),
        "wz": dma(2, 7),
    }


def layer(
    q_in, kv_in, hid_in, wx, step_size, decay_log, skip_gain, conv_x, conv_b, conv_c, out_s, out_w, *rest
):
    r = types.SimpleNamespace(**dict(zip(scratch(), rest, strict=True)))
    x, z, k, m = place()
    chip = x * NZ + z
    c = chip * NK + k
    sibling = (x, z, 1 - k, m)
    zr, zl = lax.rem(z + 1, NZ), lax.rem(z + NZ - 1, NZ)
    y_peers = [(x, z, k, lax.rem(m + d, NM)) for d in range(1, NM)]
    x_peers = [(lax.rem(x + d, NX), z, k, m) for d in range(1, NX)]
    z_peers = [(x, lax.rem(z + d, NZ), k, m) for d in range(1, NZ)]
    plane = [(lax.rem(x + a, NX), lax.rem(z + b, NZ), k, m) for a, b in OFFSETS]

    def at_ctx(i):
        return (lax.div(i, NZ * NK), lax.rem(lax.div(i, NK), NZ), lax.rem(i, NK), m)

    following, previous = at_ctx(lax.rem(c + 1, LAST + 1)), at_ctx(lax.rem(c + LAST, LAST + 1))
    greet([*y_peers, *plane, sibling, following, previous])
    sent = []

    def go(*args):
        move = remote(*args)
        move.start()
        sent.append(move)
        return move

    def arrived(moves):
        for move in moves:
            move.wait_recv()

    rows = pl.ds(pl.multiple_of(m * 16, 16), 16)

    def columns(i, width):
        return pl.ds(pl.multiple_of(i * width, width), width)

    kv_moves = [
        go(kv_in.at[:, columns(p[3], 256)], r.kvb.at[z, x, rows], r.ykv.at[0, d], r.ykv.at[1, d], p)
        for d, p in enumerate(y_peers)
    ]
    def hidden_copy(way, step, part):
        block = lax.rem(m - (step - 1) + NM, NM) if way == 0 else lax.rem(m + step - 1, NM)
        peer = y_peers[0] if way == 0 else y_peers[-1]
        at = (way * 4 + step - 1) * 3 + part
        slot = r.hall.at[block, pl.ds((16, 80, 0)[part], (64, 64, 16)[part])]
        source = hid_in.at[pl.ds(64 * part, 64)] if step == 1 and part < 2 else slot
        return remote(source, slot, r.yh.at[0, at], r.yh.at[1, at], peer)

    def hidden_parts(way, step):
        return (0, 1, 2) if step < 4 else ((0, 2), (1,))[way]

    def pass_on(step):
        for part in range(3):
            for way in range(2):
                if part in hidden_parts(way, step):
                    hidden_copy(way, step, part).wait_recv()
                    if step < 4 and part in hidden_parts(way, step + 1):
                        hidden_copy(way, step + 1, part).start()

    end = remote(
        hid_in.at[pl.ds(TOK - 16, 16)], r.hall.at[m, pl.ds(0, 16)], r.ht.at[0], r.ht.at[1], following
    )

    @pl.when(c < LAST)
    def _():
        end.start()

    for part in range(2):
        for way in range(2):
            hidden_copy(way, 1, part).start()
    q_moves = [
        go(q_in.at[:, columns(p[3], 512)], r.q2.at[0, rows], r.yq.at[0, d], r.yq.at[1, d], p)
        for d, p in enumerate(y_peers)
    ]
    mine = [
        pltpu.make_async_copy(kv_in.at[:, columns(m, 256)], r.kvb.at[z, x, rows], r.own_s.at[0]),
        pltpu.make_async_copy(q_in.at[:, columns(m, 512)], r.q2.at[0, rows], r.own_s.at[1]),
        pltpu.make_async_copy(hid_in, r.hall.at[m, pl.ds(16, TOK)], r.own_s.at[2]),
    ]
    wx_move = pltpu.make_async_copy(wx, r.wx, r.own_s.at[3])
    for move in [*mine, wx_move]:
        move.start()

    row = lax.broadcasted_iota(jnp.int32, (TOK, TOK), 0)
    col = lax.broadcasted_iota(jnp.int32, (TOK, TOK), 1)
    causal = row >= col
    lower = jnp.where(causal, 1.0, 0.0)
    rate = -jnp.exp(decay_log[...])

    def step_of(h):
        return jnp.broadcast_to(step_size[:, h : h + 1], (TOK, HD))

    for h in range(PER):
        log_decay = exact(lower, step_of(h) * rate[:, h : h + 1])
        final = log_decay[TOK - 1 :]
        r.growth[h] = jnp.exp(log_decay)
        r.to_end[h] = jnp.exp(final - log_decay)
        r.within[h] = jnp.where(
            causal, jnp.exp(jnp.where(causal, log_decay - log_decay.T, 0.0)), 0.0
        )
        r.dec[h : h + 1] = jnp.exp(final)
        r.dec[PER + h : PER + h + 1] = jnp.exp(final)
    d_move = go(r.dec, r.dsib, r.cs.at[0, 2], r.cs.at[1, 2], sibling)

    for xs in range(1, NX):

        @pl.when(xs > x)
        def _(xs=xs):
            r.kvb[:, xs] = jnp.zeros((NZ, TOK, 2 * HD), BF16)

    r.m_s[...] = jnp.full(r.m_s.shape, NEG, F32)
    r.l_s[...] = jnp.zeros(r.l_s.shape, F32)
    r.acc[...] = jnp.zeros(r.acc.shape, F32)

    def in_ring(xs):
        return (x == xs) | (x == xs + 2) | ((x == 1) & (xs == 0))

    def by_x(xs):
        return (x == 3 - xs) if xs < 2 else (x == 3) & (xs == 2)

    def ring_copy(way, step, xs):
        if way == 0:
            column, device = lax.rem(z - (step - 1) + NZ, NZ), (x, zr, k, m)
        else:
            column, device = lax.rem(z + (step - 1), NZ), (x, zl, k, m)
        slot = r.kvb.at[column, xs]
        at = (way * 4 + step - 1) * NX + xs
        return remote(slot, slot, r.ring.at[0, at], r.ring.at[1, at], device)

    def first_copy(xs, to):
        slot = r.kvb.at[z, xs]
        return remote(slot, slot, r.xkv.at[0, to], r.xkv.at[1, to], (to, z, k, m))

    FIRST = ((0, 1), (0, 2), (1, 3))

    def across(column, xs):
        to = (3, 2, 3)[xs]
        slot, at = r.kvb.at[column, xs], xs * NZ + column
        return remote(slot, slot, r.xf.at[0, at], r.xf.at[1, at], (to, z, k, m))

    for move in mine:
        move.wait()
    arrived(kv_moves)
    for xs in range(NX):

        @pl.when(x == xs)
        def _(xs=xs):
            for source, to in FIRST:
                if source == xs:
                    first_copy(xs, to).start()
            ring_copy(0, 1, xs).start()
            ring_copy(1, 1, xs).start()
            if xs < 3:
                across(z, xs).start()

    @pl.when(c > 0)
    def _():
        end.wait_recv()

    @pl.when(c == 0)
    def _():
        r.hall[m, :16] = jnp.zeros((16, 512), BF16)

    for way in range(2):
        hidden_copy(way, 1, 2).start()
    pass_on(1)

    arrived(q_moves)
    cq_move = go(r.q2.at[0], r.q2.at[1], r.cq.at[0], r.cq.at[1], sibling)
    for source, to in FIRST:

        @pl.when(x == to)
        def _(source=source, to=to):
            first_copy(source, to).wait_recv()
            ring_copy(0, 1, source).start()
            ring_copy(1, 1, source).start()

    r.ext[8:, HD : 2 * HD] = r.kvb[z, x, :, :HD].astype(F32)
    r.ext[8:, 2 * HD :] = r.q2[0].astype(F32)

    at = pl.ds(HD, 5 * HD)
    tail = remote(
        r.ext.at[pl.ds(TOK, 8), at], r.ext.at[pl.ds(0, 8), at], r.halo.at[0, 0], r.halo.at[1, 0], following
    )

    @pl.when(c < LAST)
    def _():
        tail.start()

    @pl.when(c == 0)
    def _():
        r.ext[:8, HD:] = jnp.zeros((8, 5 * HD), F32)

    d_move.wait_recv()
    for h in range(2):
        chip_decay = r.dec[...] * r.dsib[...]
        decay_row = jnp.where(k == 0, chip_decay[h : h + 1], chip_decay[2 + h : 3 + h])
        r.dsend[h] = jnp.broadcast_to(decay_row, (8, HD))
    decay_moves = [
        go(r.dsend.at[lax.div(p[0], 2)], r.drecv.at[chip], r.ds.at[0, i], r.ds.at[1, i], p)
        for i, p in enumerate(plane)
    ]
    r.drecv[chip] = r.dsend[lax.div(x, 2)]

    for h in range(PER):
        r.qs[0, h * TOK : (h + 1) * TOK] = r.q2[0, :, h * HD : (h + 1) * HD]
    pass_on(2)
    cq_move.wait_recv()
    for h in range(PER):
        r.qs[1, h * TOK : (h + 1) * TOK] = r.q2[1, :, h * HD : (h + 1) * HD]

    def attend(column, masked):
        for xs in range(NX - 1):

            @pl.when(by_x(xs))
            def _(xs=xs):
                across(column, xs).wait_recv()

        def tile(i, carry):
            side, first = lax.div(i, 2), pl.multiple_of(lax.rem(i, 2) * 256, 256)
            at = pl.ds(first, 256)
            block = r.kvb[column].reshape(NX * TOK, 2 * HD)
            s = lax.dot_general(
                r.qs[side, at], block[:, :HD], (((1,), (1,)), ((), ())), preferred_element_type=F32
            )
            if masked:
                key = lax.broadcasted_iota(jnp.int32, (256, NX * TOK), 1)
                query = lax.broadcasted_iota(jnp.int32, (256, NX * TOK), 0)
                core = jnp.where(side == 0, k, 1 - k)
                ahead = (key - x * TOK) + k * TOK - (lax.rem(query, TOK) + core * TOK)
                allowed = (key < x * TOK) | ((ahead <= 0) & (key < (x + 1) * TOK))
                s = jnp.where(allowed, s * SCALE2, NEG)
            else:
                key = lax.broadcasted_iota(jnp.int32, (1, NX * TOK), 1)
                limit = jnp.where(column < z, (x + 1) * TOK, x * TOK)
                s = s * SCALE2 + jnp.where(key < limit, 0.0, NEG)
            before = r.m_s[side, at, :1]
            now = jnp.maximum(before, jnp.max(s, axis=1, keepdims=True))
            p = jnp.exp2(s - now)
            alpha = jnp.exp2(before - now)
            r.m_s[side, at] = jnp.broadcast_to(now, (256, HD))
            r.l_s[side, at] = r.l_s[side, at] * alpha + jnp.sum(p, axis=1, keepdims=True)
            r.acc[side, at] = r.acc[side, at] * alpha + jnp.dot(
                p.astype(BF16), block[:, HD:], preferred_element_type=F32
            )
            return carry

        lax.fori_loop(0, 4, tile, 0)

    def receive(step):
        for way in range(2):
            if way == 1 and step == 4:
                continue
            column = lax.rem(z - step + NZ, NZ) if way == 0 else lax.rem(z + step, NZ)
            for xs in range(NX):

                @pl.when(in_ring(xs))
                def _(way=way, xs=xs):
                    ring_copy(way, step, xs).wait_recv()
                    if step < (4, 3)[way]:
                        ring_copy(way, step + 1, xs).start()
                    if xs < 3:

                        @pl.when(x == xs)
                        def _():
                            across(column, xs).start()

    def right(step):
        return lax.rem(z - step + NZ, NZ)

    def left(step):
        return lax.rem(z + step, NZ)

    def conv(first, taps):
        width = taps.shape[1]
        total = jnp.zeros((TOK, width), F32)
        for j in range(CONV):
            total = total + taps[j : j + 1, :] * r.ext[5 + j : 5 + j + TOK, first : first + width]
        return total

    def readouts():
        @pl.when(c > 0)
        def _():
            tail.wait_recv()

        b_conv = silu(conv(HD, conv_b))
        r.bconv[...] = b_conv
        c_conv = silu(conv(2 * HD, conv_c))
        b_t = b_conv.T
        for h in range(PER):
            read = c_conv[:, h * HD : (h + 1) * HD]
            r.read[h] = read
            r.mix[h] = exact(read, b_t) * r.within[h]

    def project():
        total = jnp.zeros((TOK + 16, HD), F32)
        for j in range(NM):
            total = total + jnp.dot(
                r.hall[j], r.wx[j * 512 : (j + 1) * 512], preferred_element_type=F32
            )
        r.ext[:, :HD] = total[8:].astype(BF16).astype(F32)

    def hidden_over_x():
        moves = []
        for d in range(1, NX):
            there = lax.rem(x + d, NX)
            for e in range(2):
                at = (d - 1) * 2 + e
                into = r.hidq.at[e, columns(x, TOK)]
                moves.append(
                    go(
                        r.hall.at[2 * there + e, pl.ds(16, TOK)], into,
                        r.hq.at[0, at], r.hq.at[1, at], x_peers[d - 1],
                    )
                )
        for e in range(2):
            r.hidq[e, columns(x, TOK)] = r.hall[2 * x + e, 16:]
        return moves

    def states():
        x_pre = conv(0, conv_x)
        x_conv = silu(x_pre)
        r.xpre[...] = x_pre
        r.xconv[...] = x_conv
        b_t = r.bconv[...].T
        for h in range(PER):
            r.state[0, h] = exact(b_t, r.to_end[h] * (step_of(h) * x_conv))

    def inners():
        x_conv = r.xconv[...]
        for h in range(PER):
            r.inner[h] = exact(r.mix[h], step_of(h) * x_conv) + skip_gain[:, h : h + 1] * x_conv

    first_of, first_other = pl.ds(2 * k, 2), pl.ds(2 * (1 - k), 2)

    def scan(way):
        state = r.state.at[way]
        move = go(state.at[first_other], r.csib.at[way], r.cs.at[0, way], r.cs.at[1, way], sibling)
        yield
        move.wait_recv()
        d_mine = [jnp.where(k == 0, r.dec[h : h + 1], r.dec[2 + h : 3 + h]) for h in range(2)]
        d_other = [jnp.where(k == 0, r.dsib[h : h + 1], r.dsib[2 + h : 3 + h]) for h in range(2)]
        mine_first = (k == 0) if way == 0 else (k == 1)
        for h in range(2):
            own, theirs = state[2 * k + h], r.csib[way, h]
            near = jnp.where(mine_first, theirs, own)
            far = jnp.where(mine_first, own, theirs)
            d_near = jnp.where(mine_first, d_other[h], d_mine[h])
            both = far * d_near + near
            r.zsend[way, 16 * h : 16 * h + 16] = both.reshape(16, 8, HD)
        moves = []
        for i, p in enumerate(plane):
            at = way * 31 + i
            there = p[0] * NZ + p[1]
            moves.append(
                go(r.zsend.at[way, there], r.zrecv.at[way, chip], r.zs.at[0, at], r.zs.at[1, at], p)
            )
        r.zrecv[way, chip] = r.zsend[way, chip]
        yield
        arrived(moves)
        enters = jnp.zeros((8, HD), F32)
        for j in range(CHIPS) if way == 0 else range(CHIPS - 1, -1, -1):
            r.zbs[way, j] = enters
            enters = r.drecv[j] * enters + r.zrecv[way, j]
        moves = []
        for i, p in enumerate(plane):
            at = way * 31 + i
            there = p[0] * NZ + p[1]
            moves.append(
                go(r.zbs.at[way, there], r.zbr.at[way, chip], r.bs.at[0, at], r.bs.at[1, at], p)
            )
        r.zbr[way, chip] = r.zbs[way, chip]
        yield
        arrived(moves)
        for h in range(2):
            entering = r.zbr[way, 16 * h : 16 * h + 16].reshape(HD, HD)
            own, theirs = state[2 * k + h], r.csib[way, h]
            d_first = jnp.where(mine_first, d_mine[h], d_other[h])
            second = d_first * entering + jnp.where(mine_first, own, theirs)
            r.inc[way, 2 * k + h] = jnp.where(mine_first, entering, second)
            r.cback[way, h] = jnp.where(mine_first, second, entering)
        move = go(r.cback.at[way], r.inc.at[way, first_of], r.ks.at[0, way], r.ks.at[1, way], sibling)
        yield
        move.wait_recv()
        yield

    receive(1)
    attend(z, True)
    pass_on(3)
    readouts()
    receive(2)
    attend(right(1), False)
    pass_on(4)
    wx_move.wait()
    project()
    states()
    forward = scan(0)
    next(forward)
    hq_moves = hidden_over_x()
    inners()
    arrived(decay_moves)
    next(forward)
    attend(left(1), False)
    receive(3)
    attend(right(2), False)
    next(forward)
    attend(left(2), False)
    receive(4)
    attend(right(3), False)
    next(forward)
    attend(left(3), False)
    attend(right(4), False)
    lane = lax.broadcasted_iota(jnp.int32, (PER * TOK, HD), 1)
    r.stat[...] = jnp.where(lane < 64, r.m_s[1], r.l_s[1])
    o_moves = [
        go(r.acc.at[1], r.acc_in, r.co.at[0, 0], r.co.at[1, 0], sibling),
        go(r.stat, r.stat_in, r.co.at[0, 1], r.co.at[1, 1], sibling),
    ]
    arrived(o_moves)
    other, mine_max = r.stat_in[:, :1], r.m_s[0, :, :1]
    both = jnp.maximum(other, mine_max)
    a0, a1 = jnp.exp2(mine_max - both), jnp.exp2(other - both)
    norm = r.l_s[0, :, :1] * a0 + r.stat_in[:, 64:65] * a1
    r.target[...] = ((r.acc[0] * a0 + r.acc_in[...] * a1) / norm).reshape(PER, TOK, HD)
    next(forward)
    for h in range(PER):
        student = r.inner[h] + r.growth[h] * exact(r.read[h], r.inc[0, h])
        out_s[:, h * HD : (h + 1) * HD] = student.astype(BF16)
        r.up[h] = 2.0 * (student - r.target[h]) / (HEAD_TOTAL * HD)
        r.state[1, h] = exact((r.growth[h] * r.read[h]).T, r.up[h])

    backward = scan(1)
    next(backward)
    next(backward)
    x_grad = jnp.zeros((TOK, HD), F32)
    for h in range(PER):
        up = r.up[h]
        x_grad = x_grad + step_of(h) * exact(r.mix[h].T, up) + skip_gain[:, h : h + 1] * up
    next(backward)
    next(backward)
    next(backward)
    b_conv = r.bconv[...]
    for h in range(PER):
        x_grad = x_grad + step_of(h) * r.to_end[h] * exact(b_conv, r.inc[1, h])
    x_pre = r.xpre[...]
    sigma = 1.0 / (1.0 + jnp.exp(-x_pre))
    r.ext2[:TOK] = x_grad * sigma * (1.0 + x_pre * (1.0 - sigma))
    head = remote(
        r.ext2.at[pl.ds(0, 8)], r.ext2.at[pl.ds(TOK, 8)], r.halo.at[0, 1], r.halo.at[1, 1], previous
    )

    @pl.when(c > 0)
    def _():
        head.start()

    @pl.when(c == LAST)
    def _():
        r.ext2[TOK:] = jnp.zeros((8, HD), F32)

    @pl.when(c < LAST)
    def _():
        head.wait_recv()

    grad = jnp.zeros((TOK, HD), F32)
    for j in range(CONV):
        grad = grad + conv_x[j : j + 1, :] * r.ext2[CONV - 1 - j : CONV - 1 - j + TOK]
    here = r.ig.at[columns(x, TOK)]
    here[...] = grad.astype(BF16)
    moves = [
        go(here, here, r.igs.at[0, d], r.igs.at[1, d], p) for d, p in enumerate(x_peers)
    ]
    arrived(hq_moves)
    arrived(moves)
    for e in range(2):
        product = lax.dot_general(
            r.hidq[e], r.ig[...], (((0,), (0,)), ((), ())), preferred_element_type=F32
        )
        r.part[4 * e : 4 * e + 4] = product.reshape(4, NK, 64, HD)
    go(r.part.at[:, 1 - k], r.wrecv, r.wc.at[0], r.wc.at[1], sibling).wait_recv()
    for i in range(NZ):
        r.wsend[i] = r.part[i, k] + r.wrecv[i]
    moves = [
        go(r.wsend.at[p[1]], r.wzr.at[z], r.wz.at[0, d], r.wz.at[1, d], p)
        for d, p in enumerate(z_peers)
    ]
    r.wzr[z] = r.wsend[z]
    arrived(moves)
    total = r.wzr[0]
    for i in range(1, NZ):
        total = total + r.wzr[i]
    out_w[...] = total

    for move in sent:
        move.wait_send()

    @pl.when(c < LAST)
    def _():
        tail.wait_send()
        end.wait_send()

    @pl.when(c > 0)
    def _():
        head.wait_send()

    for way in range(2):
        for step in range(1, 5):
            for part in hidden_parts(way, step):
                hidden_copy(way, step, part).wait_send()

    for source, to in FIRST:

        @pl.when(x == source)
        def _(source=source, to=to):
            first_copy(source, to).wait_send()

    for xs in range(NX):

        @pl.when(in_ring(xs))
        def _(xs=xs):
            for way in range(2):
                for step in range(1, (4, 3)[way] + 1):
                    ring_copy(way, step, xs).wait_send()

        if xs < 3:

            @pl.when(x == xs)
            def _(xs=xs):
                for column in range(NZ):
                    across(column, xs).wait_send()


def local(
    query_proj, keyval_proj, hidden, weight_x, conv_x, conv_b, conv_c, step_size, decay_log, skip_gain
):
    args = (
        query_proj, keyval_proj.reshape(16, KV * 2 * HD), hidden, weight_x, step_size,
        decay_log.reshape(1, PER), skip_gain.reshape(1, PER), conv_x, conv_b, conv_c,
    )
    return pl.pallas_call(
        layer,
        out_shape=(
            jax.ShapeDtypeStruct((TOK, PER * HD), BF16),
            jax.ShapeDtypeStruct((64, HD), F32),
        ),
        in_specs=[pl.BlockSpec(memory_space=pl.ANY if i in (0, 2, 3) else pltpu.VMEM) for i in range(len(args))],
        out_specs=[pl.BlockSpec(memory_space=pltpu.VMEM)] * 2,
        scratch_shapes=list(scratch().values()),
        compiler_params=pltpu.CompilerParams(
            collective_id=0, has_side_effects=True, vmem_limit_bytes=48 * 2**20
        ),
    )(*args)


def solution(mesh):
    finer = Mesh(mesh.devices.reshape(NX, NZ, NK, mesh.shape["mp"]), CTX_MP)
    placed = (
        P(CTX_MP, None),
        P(CTX_MP, None, None),
        P(CTX, "mp"),
        P(None, "mp"),
        P(None, "mp"),
        P(None, "mp"),
        P(None, "mp"),
        P(CTX, "mp"),
        P("mp"),
        P("mp"),
    )
    return jax.shard_map(
        local, mesh=finer, in_specs=placed, out_specs=(P(CTX, "mp"), P(CTX, "mp")), check_vma=False
    )
```

```python
import types

import jax
import jax.numpy as jnp
from jax import lax
from jax.experimental import pallas as pl
from jax.experimental.pallas import tpu as pltpu
from jax.sharding import Mesh
from jax.sharding import PartitionSpec as P

HEAD_TOTAL = 32
KV = 8
HD = 128
CONV = 4
TOK = 128
PER = HEAD_TOTAL // KV
NX, NZ, NK, NM = 4, 8, 2, 8
CHIPS = NX * NZ
LAST = CHIPS * NK - 1
CTX = ("ctx_0", "ctx_1", "ctx_2")
CTX_MP = ("ctx_0", "ctx_1", "ctx_2", "mp")
MESH = pl.DeviceIdType.MESH
F32, BF16 = jnp.float32, jnp.bfloat16
NEG = -1e30
SCALE2 = HD**-0.5 * 1.4426950408889634
OFFSETS = sorted(
    ((a, b) for a in range(NX) for b in range(NZ) if a or b),
    key=lambda ab: -(min(ab[0], NX - ab[0]) + min(ab[1], NZ - ab[1])),
)


def place():
    return tuple(lax.axis_index(name) for name in CTX_MP)


def remote(src, dst, send, recv, device):
    return pltpu.make_async_remote_copy(
        src_ref=src, dst_ref=dst, send_sem=send, recv_sem=recv, device_id=device, device_id_type=MESH
    )


def greet(devices):
    barrier = pltpu.get_barrier_semaphore()
    for device in devices:
        pl.semaphore_signal(barrier, inc=1, device_id=device, device_id_type=MESH)
    pl.semaphore_wait(barrier, len(devices))


def exact(a, b, dims=((1,), (0,))):
    return lax.dot_general(
        a, b, (dims, ((), ())), precision=lax.Precision.HIGHEST, preferred_element_type=F32
    )


def silu(v):
    return v / (1.0 + jnp.exp(-v))


def dma(*dims):
    return pltpu.SemaphoreType.DMA(dims)


def scratch():
    vm = pltpu.VMEM
    return {
        "q2": vm((2, TOK, PER * HD), BF16),
        "kvb": vm((NZ, NX, TOK, 2 * HD), BF16),
        "hall": vm((NM, TOK + 16, 512), BF16),
        "wx": vm((4096, HD), BF16),
        "hidq": vm((2, NX * TOK, 512), BF16),
        "qs": vm((2 * PER * TOK, HD), BF16),
        "m_s": vm((8, 2 * PER * TOK), F32),
        "l_s": vm((8, 2 * PER * TOK), F32),
        "acc": vm((HD, 2 * PER * TOK), F32),
        "stat": vm((8, PER * TOK), F32),
        "acc_in": vm((HD, PER * TOK), F32),
        "stat_in": vm((8, PER * TOK), F32),
        "hid_t": vm((2, 512, NX * TOK), BF16),
        "target": vm((PER, TOK, HD), F32),
        "ext": vm((TOK + 8, 6 * HD), F32),
        "ext2": vm((TOK + 8, HD), F32),
        "growth": vm((PER, TOK, TOK), F32),
        "to_end": vm((PER, TOK, TOK), F32),
        "within": vm((PER, TOK, TOK), F32),
        "mix": vm((PER, TOK, TOK), F32),
        "read": vm((PER, TOK, HD), F32),
        "inner": vm((PER, TOK, HD), F32),
        "up": vm((PER, TOK, HD), F32),
        "bconv": vm((TOK, HD), F32),
        "xconv": vm((TOK, HD), F32),
        "xpre": vm((TOK, HD), F32),
        "state": vm((2, PER, HD, HD), F32),
        "csib": vm((2, 2, HD, HD), F32),
        "cback": vm((2, 2, HD, HD), F32),
        "inc": vm((2, PER, HD, HD), F32),
        "dec": vm((8, HD), F32),
        "dsib": vm((8, HD), F32),
        "dsend": vm((2, 8, HD), F32),
        "drecv": vm((CHIPS, 8, HD), F32),
        "zsend": vm((2, CHIPS, 8, HD), F32),
        "zrecv": vm((2, CHIPS, 8, HD), F32),
        "zbs": vm((2, CHIPS, 8, HD), F32),
        "zbr": vm((2, CHIPS, 8, HD), F32),
        "ig": vm((NX * TOK, HD), BF16),
        "part": vm((NZ, NK, 64, HD), F32),
        "wrecv": vm((NZ, 64, HD), F32),
        "wsend": vm((NZ, 64, HD), F32),
        "wzr": vm((NZ, 64, HD), F32),
        "own_s": dma(4),
        "yq": dma(2, 7),
        "ykv": dma(2, 7),
        "yh": dma(2, 24),
        "ht": dma(2),
        "xkv": dma(2, NX),
        "xf": dma(2, NX * NZ),
        "ring": dma(2, 32),
        "cq": dma(2),
        "co": dma(2, 2),
        "hq": dma(2, 6),
        "halo": dma(2, 2),
        "cs": dma(2, 3),
        "ds": dma(2, 31),
        "zs": dma(2, 62),
        "bs": dma(2, 62),
        "ks": dma(2, 2),
        "igs": dma(2, 3),
        "wc": dma(2),
        "wz": dma(2, 7),
    }


def layer(
    q_in, kv_in, hid_in, wx, step_size, decay_log, skip_gain, conv_x, conv_b, conv_c, out_s, out_w, *rest
):
    r = types.SimpleNamespace(**dict(zip(scratch(), rest, strict=True)))
    x, z, k, m = place()
    chip = x * NZ + z
    c = chip * NK + k
    sibling = (x, z, 1 - k, m)
    zr, zl = lax.rem(z + 1, NZ), lax.rem(z + NZ - 1, NZ)
    y_peers = [(x, z, k, lax.rem(m + d, NM)) for d in range(1, NM)]
    x_peers = [(lax.rem(x + d, NX), z, k, m) for d in range(1, NX)]
    z_peers = [(x, lax.rem(z + d, NZ), k, m) for d in range(1, NZ)]
    plane = [(lax.rem(x + a, NX), lax.rem(z + b, NZ), k, m) for a, b in OFFSETS]

    def at_ctx(i):
        return (lax.div(i, NZ * NK), lax.rem(lax.div(i, NK), NZ), lax.rem(i, NK), m)

    following, previous = at_ctx(lax.rem(c + 1, LAST + 1)), at_ctx(lax.rem(c + LAST, LAST + 1))
    greet([*y_peers, *plane, sibling, following, previous])
    sent = []

    def go(*args):
        move = remote(*args)
        move.start()
        sent.append(move)
        return move

    def arrived(moves):
        for move in moves:
            move.wait_recv()

    rows = pl.ds(pl.multiple_of(m * 16, 16), 16)

    def columns(i, width):
        return pl.ds(pl.multiple_of(i * width, width), width)

    def hidden_copy(way, step, part):
        block = lax.rem(m - (step - 1) + NM, NM) if way == 0 else lax.rem(m + step - 1, NM)
        peer = y_peers[0] if way == 0 else y_peers[-1]
        at = (way * 4 + step - 1) * 3 + part
        slot = r.hall.at[block, pl.ds((16, 80, 0)[part], (64, 64, 16)[part])]
        source = hid_in.at[pl.ds(64 * part, 64)] if step == 1 and part < 2 else slot
        return remote(source, slot, r.yh.at[0, at], r.yh.at[1, at], peer)

    def hidden_parts(way, step):
        return (0, 1, 2) if step < 4 else ((0, 2), (1,))[way]

    def pass_on(step):
        for part in range(3):
            for way in range(2):
                if part in hidden_parts(way, step):
                    hidden_copy(way, step, part).wait_recv()
                    if step < 4 and part in hidden_parts(way, step + 1):
                        hidden_copy(way, step + 1, part).start()

    end = remote(
        hid_in.at[pl.ds(TOK - 16, 16)], r.hall.at[m, pl.ds(0, 16)], r.ht.at[0], r.ht.at[1], following
    )

    @pl.when(c < LAST)
    def _():
        end.start()

    for part in range(2):
        for way in range(2):
            hidden_copy(way, 1, part).start()
    kv_moves = [
        go(kv_in.at[:, columns(p[3], 256)], r.kvb.at[z, x, rows], r.ykv.at[0, d], r.ykv.at[1, d], p)
        for d, p in enumerate(y_peers)
    ]
    q_moves = [
        go(q_in.at[:, columns(p[3], 512)], r.q2.at[0, rows], r.yq.at[0, d], r.yq.at[1, d], p)
        for d, p in enumerate(y_peers)
    ]
    mine = [
        pltpu.make_async_copy(kv_in.at[:, columns(m, 256)], r.kvb.at[z, x, rows], r.own_s.at[0]),
        pltpu.make_async_copy(q_in.at[:, columns(m, 512)], r.q2.at[0, rows], r.own_s.at[1]),
        pltpu.make_async_copy(hid_in, r.hall.at[m, pl.ds(16, TOK)], r.own_s.at[2]),
    ]
    wx_move = pltpu.make_async_copy(wx, r.wx, r.own_s.at[3])
    for move in [*mine, wx_move]:
        move.start()

    row = lax.broadcasted_iota(jnp.int32, (TOK, TOK), 0)
    col = lax.broadcasted_iota(jnp.int32, (TOK, TOK), 1)
    causal = row >= col
    lower = jnp.where(causal, 1.0, 0.0)
    rate = -jnp.exp(decay_log[...])

    def step_of(h):
        return jnp.broadcast_to(step_size[:, h : h + 1], (TOK, HD))

    for h in range(PER):
        log_decay = exact(lower, step_of(h) * rate[:, h : h + 1])
        final = log_decay[TOK - 1 :]
        r.growth[h] = jnp.exp(log_decay)
        r.to_end[h] = jnp.exp(final - log_decay)
        r.within[h] = jnp.where(
            causal, jnp.exp(jnp.where(causal, log_decay - log_decay.T, 0.0)), 0.0
        )
        r.dec[h : h + 1] = jnp.exp(final)
        r.dec[PER + h : PER + h + 1] = jnp.exp(final)
    d_move = go(r.dec, r.dsib, r.cs.at[0, 2], r.cs.at[1, 2], sibling)

    for xs in range(1, NX):

        @pl.when(xs > x)
        def _(xs=xs):
            r.kvb[:, xs] = jnp.zeros((NZ, TOK, 2 * HD), BF16)

    r.m_s[...] = jnp.full(r.m_s.shape, NEG, F32)
    r.l_s[...] = jnp.zeros(r.l_s.shape, F32)
    r.acc[...] = jnp.zeros(r.acc.shape, F32)

    def in_ring(xs):
        return (x == xs) | (x == xs + 2) | ((x == 1) & (xs == 0))

    def by_x(xs):
        return (x == 3 - xs) if xs < 2 else (x == 3) & (xs == 2)

    def ring_copy(way, step, xs):
        if way == 0:
            column, device = lax.rem(z - (step - 1) + NZ, NZ), (x, zr, k, m)
        else:
            column, device = lax.rem(z + (step - 1), NZ), (x, zl, k, m)
        slot = r.kvb.at[column, xs]
        at = (way * 4 + step - 1) * NX + xs
        return remote(slot, slot, r.ring.at[0, at], r.ring.at[1, at], device)

    def first_copy(xs, to):
        slot = r.kvb.at[z, xs]
        return remote(slot, slot, r.xkv.at[0, to], r.xkv.at[1, to], (to, z, k, m))

    FIRST = ((0, 1), (0, 2), (1, 3))

    def across(column, xs):
        to = (3, 2, 3)[xs]
        slot, at = r.kvb.at[column, xs], xs * NZ + column
        return remote(slot, slot, r.xf.at[0, at], r.xf.at[1, at], (to, z, k, m))

    for move in mine:
        move.wait()
    arrived(kv_moves)
    for xs in range(NX):

        @pl.when(x == xs)
        def _(xs=xs):
            for source, to in FIRST:
                if source == xs:
                    first_copy(xs, to).start()
            ring_copy(0, 1, xs).start()
            ring_copy(1, 1, xs).start()
            if xs < 3:
                across(z, xs).start()

    @pl.when(c > 0)
    def _():
        end.wait_recv()

    @pl.when(c == 0)
    def _():
        r.hall[m, :16] = jnp.zeros((16, 512), BF16)

    for way in range(2):
        hidden_copy(way, 1, 2).start()
    pass_on(1)

    arrived(q_moves)
    cq_move = go(r.q2.at[0], r.q2.at[1], r.cq.at[0], r.cq.at[1], sibling)
    for source, to in FIRST:

        @pl.when(x == to)
        def _(source=source, to=to):
            first_copy(source, to).wait_recv()
            ring_copy(0, 1, source).start()
            ring_copy(1, 1, source).start()

    r.ext[8:, HD : 2 * HD] = r.kvb[z, x, :, :HD].astype(F32)
    r.ext[8:, 2 * HD :] = r.q2[0].astype(F32)

    at = pl.ds(HD, 5 * HD)
    tail = remote(
        r.ext.at[pl.ds(TOK, 8), at], r.ext.at[pl.ds(0, 8), at], r.halo.at[0, 0], r.halo.at[1, 0], following
    )

    @pl.when(c < LAST)
    def _():
        tail.start()

    @pl.when(c == 0)
    def _():
        r.ext[:8, HD:] = jnp.zeros((8, 5 * HD), F32)

    d_move.wait_recv()
    for h in range(2):
        chip_decay = r.dec[...] * r.dsib[...]
        decay_row = jnp.where(k == 0, chip_decay[h : h + 1], chip_decay[2 + h : 3 + h])
        r.dsend[h] = jnp.broadcast_to(decay_row, (8, HD))
    decay_moves = [
        go(r.dsend.at[lax.div(p[0], 2)], r.drecv.at[chip], r.ds.at[0, i], r.ds.at[1, i], p)
        for i, p in enumerate(plane)
    ]
    r.drecv[chip] = r.dsend[lax.div(x, 2)]

    for h in range(PER):
        r.qs[h * TOK : (h + 1) * TOK] = r.q2[0, :, h * HD : (h + 1) * HD]
    pass_on(2)
    cq_move.wait_recv()
    for h in range(PER):
        r.qs[(PER + h) * TOK : (PER + h + 1) * TOK] = r.q2[1, :, h * HD : (h + 1) * HD]

    def attend(column, masked):
        for xs in range(NX - 1):

            @pl.when(by_x(xs))
            def _(xs=xs):
                across(column, xs).wait_recv()

        block = r.kvb[column].reshape(NX * TOK, 2 * HD)
        scores = lax.dot_general(
            block[:, :HD], r.qs[...], (((1,), (1,)), ((), ())), preferred_element_type=F32
        )
        parts = [scores[b * TOK : (b + 1) * TOK] for b in range(NX)]
        if masked:
            key = lax.broadcasted_iota(jnp.int32, (TOK, 2 * PER * TOK), 0)
            query = lax.broadcasted_iota(jnp.int32, (TOK, 2 * PER * TOK), 1)
            core = jnp.where(query < PER * TOK, k, 1 - k)
            own = key + k * TOK <= lax.rem(query, TOK) + core * TOK
            parts = [jnp.where((b != x) | own, part, NEG) for b, part in enumerate(parts)]
            shut = [jnp.where(b <= x, 0.0, NEG) for b in range(NX)]
        else:
            shut = [jnp.where((b < x) | ((b == x) & (column < z)), 0.0, NEG) for b in range(NX)]
        before = now = r.m_s[:1]
        for part, off in zip(parts, shut, strict=True):
            now = jnp.maximum(now, jnp.max(part, axis=0, keepdims=True) * SCALE2 + off)
        alpha = jnp.exp2(before - now)
        parts = [
            jnp.exp2(part * SCALE2 - (now - off)) for part, off in zip(parts, shut, strict=True)
        ]
        total = r.l_s[:1] * alpha
        for part in parts:
            total = total + jnp.sum(part, axis=0, keepdims=True)
        r.l_s[:1] = total
        r.m_s[:1] = now
        weights = jnp.concatenate([part.astype(BF16) for part in parts], axis=0)
        r.acc[...] = r.acc[...] * alpha + lax.dot_general(
            block[:, HD:], weights, (((0,), (0,)), ((), ())), preferred_element_type=F32
        )

    def receive(step):
        for way in range(2):
            if way == 1 and step == 4:
                continue
            column = lax.rem(z - step + NZ, NZ) if way == 0 else lax.rem(z + step, NZ)
            for xs in range(NX):

                @pl.when(in_ring(xs))
                def _(way=way, xs=xs):
                    ring_copy(way, step, xs).wait_recv()
                    if step < (4, 3)[way]:
                        ring_copy(way, step + 1, xs).start()
                    if xs < 3:

                        @pl.when(x == xs)
                        def _():
                            across(column, xs).start()

    def right(step):
        return lax.rem(z - step + NZ, NZ)

    def left(step):
        return lax.rem(z + step, NZ)

    def conv(first, taps):
        width = taps.shape[1]
        total = jnp.zeros((TOK, width), F32)
        for j in range(CONV):
            total = total + taps[j : j + 1, :] * r.ext[5 + j : 5 + j + TOK, first : first + width]
        return total

    def readouts():
        @pl.when(c > 0)
        def _():
            tail.wait_recv()

        b_conv = silu(conv(HD, conv_b))
        r.bconv[...] = b_conv
        c_conv = silu(conv(2 * HD, conv_c))
        b_t = b_conv.T
        for h in range(PER):
            read = c_conv[:, h * HD : (h + 1) * HD]
            r.read[h] = read
            r.mix[h] = exact(read, b_t) * r.within[h]

    def project():
        total = jnp.zeros((TOK + 16, HD), F32)
        for j in range(NM):
            total = total + jnp.dot(
                r.hall[j], r.wx[j * 512 : (j + 1) * 512], preferred_element_type=F32
            )
        r.ext[:, :HD] = total[8:].astype(BF16).astype(F32)

    def hidden_over_x():
        moves = []
        for d in range(1, NX):
            there = lax.rem(x + d, NX)
            for e in range(2):
                at = (d - 1) * 2 + e
                into = r.hidq.at[e, columns(x, TOK)]
                moves.append(
                    go(
                        r.hall.at[2 * there + e, pl.ds(16, TOK)], into,
                        r.hq.at[0, at], r.hq.at[1, at], x_peers[d - 1],
                    )
                )
        for e in range(2):
            r.hidq[e, columns(x, TOK)] = r.hall[2 * x + e, 16:]
        return moves

    def states():
        x_pre = conv(0, conv_x)
        x_conv = silu(x_pre)
        r.xpre[...] = x_pre
        r.xconv[...] = x_conv
        b_t = r.bconv[...].T
        for h in range(PER):
            r.state[0, h] = exact(b_t, r.to_end[h] * (step_of(h) * x_conv))

    def inners():
        x_conv = r.xconv[...]
        for h in range(PER):
            r.inner[h] = exact(r.mix[h], step_of(h) * x_conv) + skip_gain[:, h : h + 1] * x_conv

    first_of, first_other = pl.ds(2 * k, 2), pl.ds(2 * (1 - k), 2)

    def scan(way):
        state = r.state.at[way]
        move = go(state.at[first_other], r.csib.at[way], r.cs.at[0, way], r.cs.at[1, way], sibling)
        yield
        move.wait_recv()
        d_mine = [jnp.where(k == 0, r.dec[h : h + 1], r.dec[2 + h : 3 + h]) for h in range(2)]
        d_other = [jnp.where(k == 0, r.dsib[h : h + 1], r.dsib[2 + h : 3 + h]) for h in range(2)]
        mine_first = (k == 0) if way == 0 else (k == 1)
        for h in range(2):
            own, theirs = state[2 * k + h], r.csib[way, h]
            near = jnp.where(mine_first, theirs, own)
            far = jnp.where(mine_first, own, theirs)
            d_near = jnp.where(mine_first, d_other[h], d_mine[h])
            both = far * d_near + near
            r.zsend[way, 16 * h : 16 * h + 16] = both.reshape(16, 8, HD)
        moves = []
        for i, p in enumerate(plane):
            at = way * 31 + i
            there = p[0] * NZ + p[1]
            moves.append(
                go(r.zsend.at[way, there], r.zrecv.at[way, chip], r.zs.at[0, at], r.zs.at[1, at], p)
            )
        r.zrecv[way, chip] = r.zsend[way, chip]
        yield
        arrived(moves)
        enters = jnp.zeros((8, HD), F32)
        for j in range(CHIPS) if way == 0 else range(CHIPS - 1, -1, -1):
            r.zbs[way, j] = enters
            enters = r.drecv[j] * enters + r.zrecv[way, j]
        moves = []
        for i, p in enumerate(plane):
            at = way * 31 + i
            there = p[0] * NZ + p[1]
            moves.append(
                go(r.zbs.at[way, there], r.zbr.at[way, chip], r.bs.at[0, at], r.bs.at[1, at], p)
            )
        r.zbr[way, chip] = r.zbs[way, chip]
        yield
        arrived(moves)
        for h in range(2):
            entering = r.zbr[way, 16 * h : 16 * h + 16].reshape(HD, HD)
            own, theirs = state[2 * k + h], r.csib[way, h]
            d_first = jnp.where(mine_first, d_mine[h], d_other[h])
            second = d_first * entering + jnp.where(mine_first, own, theirs)
            r.inc[way, 2 * k + h] = jnp.where(mine_first, entering, second)
            r.cback[way, h] = jnp.where(mine_first, second, entering)
        move = go(r.cback.at[way], r.inc.at[way, first_of], r.ks.at[0, way], r.ks.at[1, way], sibling)
        yield
        move.wait_recv()
        yield

    receive(1)
    attend(z, True)
    readouts()
    pass_on(3)
    receive(2)
    attend(right(1), False)
    attend(left(1), False)
    pass_on(4)
    wx_move.wait()
    project()
    states()
    forward = scan(0)
    next(forward)
    receive(3)
    inners()
    arrived(decay_moves)
    next(forward)
    attend(right(2), False)
    attend(left(2), False)
    receive(4)
    hq_moves = hidden_over_x()
    attend(right(3), False)
    attend(left(3), False)
    next(forward)
    attend(right(4), False)
    half = PER * TOK
    r.stat[:1] = r.m_s[:1, half:]
    r.stat[1:2] = r.l_s[:1, half:]
    r.stat[2:] = jnp.zeros((6, half), F32)
    o_moves = [
        go(r.acc.at[:, pl.ds(half, half)], r.acc_in, r.co.at[0, 0], r.co.at[1, 0], sibling),
        go(r.stat, r.stat_in, r.co.at[0, 1], r.co.at[1, 1], sibling),
    ]
    next(forward)
    arrived(o_moves)
    other, mine_max = r.stat_in[:1], r.m_s[:1, :half]
    both = jnp.maximum(other, mine_max)
    a0, a1 = jnp.exp2(mine_max - both), jnp.exp2(other - both)
    norm = r.l_s[:1, :half] * a0 + r.stat_in[1:2] * a1
    result = (r.acc[:, :half] * a0 + r.acc_in[...] * a1) / norm
    for h in range(PER):
        r.target[h] = result[:, h * TOK : (h + 1) * TOK].T
    next(forward)
    for h in range(PER):
        student = r.inner[h] + r.growth[h] * exact(r.read[h], r.inc[0, h])
        out_s[:, h * HD : (h + 1) * HD] = student.astype(BF16)
        r.up[h] = 2.0 * (student - r.target[h]) / (HEAD_TOTAL * HD)
        r.state[1, h] = exact((r.growth[h] * r.read[h]).T, r.up[h])

    backward = scan(1)
    next(backward)
    next(backward)
    x_grad = jnp.zeros((TOK, HD), F32)
    for h in range(PER):
        up = r.up[h]
        x_grad = x_grad + step_of(h) * exact(r.mix[h].T, up) + skip_gain[:, h : h + 1] * up
    next(backward)
    arrived(hq_moves)
    for e in range(2):
        r.hid_t[e] = r.hidq[e].T
    next(backward)
    next(backward)
    b_conv = r.bconv[...]
    for h in range(PER):
        x_grad = x_grad + step_of(h) * r.to_end[h] * exact(b_conv, r.inc[1, h])
    x_pre = r.xpre[...]
    sigma = 1.0 / (1.0 + jnp.exp(-x_pre))
    r.ext2[:TOK] = x_grad * sigma * (1.0 + x_pre * (1.0 - sigma))
    head = remote(
        r.ext2.at[pl.ds(0, 8)], r.ext2.at[pl.ds(TOK, 8)], r.halo.at[0, 1], r.halo.at[1, 1], previous
    )

    @pl.when(c > 0)
    def _():
        head.start()

    @pl.when(c == LAST)
    def _():
        r.ext2[TOK:] = jnp.zeros((8, HD), F32)

    @pl.when(c < LAST)
    def _():
        head.wait_recv()

    grad = jnp.zeros((TOK, HD), F32)
    for j in range(CONV):
        grad = grad + conv_x[j : j + 1, :] * r.ext2[CONV - 1 - j : CONV - 1 - j + TOK]
    here = r.ig.at[columns(x, TOK)]
    here[...] = grad.astype(BF16)
    moves = [
        go(here, here, r.igs.at[0, d], r.igs.at[1, d], p) for d, p in enumerate(x_peers)
    ]
    arrived(moves)
    for e in range(2):
        product = jnp.dot(r.hid_t[e], r.ig[...], preferred_element_type=F32)
        r.part[4 * e : 4 * e + 4] = product.reshape(4, NK, 64, HD)
    go(r.part.at[:, 1 - k], r.wrecv, r.wc.at[0], r.wc.at[1], sibling).wait_recv()
    for i in range(NZ):
        r.wsend[i] = r.part[i, k] + r.wrecv[i]
    moves = [
        go(r.wsend.at[p[1]], r.wzr.at[z], r.wz.at[0, d], r.wz.at[1, d], p)
        for d, p in enumerate(z_peers)
    ]
    r.wzr[z] = r.wsend[z]
    arrived(moves)
    total = r.wzr[0]
    for i in range(1, NZ):
        total = total + r.wzr[i]
    out_w[...] = total

    for move in sent:
        move.wait_send()

    @pl.when(c < LAST)
    def _():
        tail.wait_send()
        end.wait_send()

    @pl.when(c > 0)
    def _():
        head.wait_send()

    for way in range(2):
        for step in range(1, 5):
            for part in hidden_parts(way, step):
                hidden_copy(way, step, part).wait_send()

    for source, to in FIRST:

        @pl.when(x == source)
        def _(source=source, to=to):
            first_copy(source, to).wait_send()

    for xs in range(NX):

        @pl.when(in_ring(xs))
        def _(xs=xs):
            for way in range(2):
                for step in range(1, (4, 3)[way] + 1):
                    ring_copy(way, step, xs).wait_send()

        if xs < 3:

            @pl.when(x == xs)
            def _(xs=xs):
                for column in range(NZ):
                    across(column, xs).wait_send()


def local(
    query_proj, keyval_proj, hidden, weight_x, conv_x, conv_b, conv_c, step_size, decay_log, skip_gain
):
    args = (
        query_proj, keyval_proj.reshape(16, KV * 2 * HD), hidden, weight_x, step_size,
        decay_log.reshape(1, PER), skip_gain.reshape(1, PER), conv_x, conv_b, conv_c,
    )
    return pl.pallas_call(
        layer,
        out_shape=(
            jax.ShapeDtypeStruct((TOK, PER * HD), BF16),
            jax.ShapeDtypeStruct((64, HD), F32),
        ),
        in_specs=[pl.BlockSpec(memory_space=pl.ANY if i in (0, 2, 3) else pltpu.VMEM) for i in range(len(args))],
        out_specs=[pl.BlockSpec(memory_space=pltpu.VMEM)] * 2,
        scratch_shapes=list(scratch().values()),
        compiler_params=pltpu.CompilerParams(
            collective_id=0, has_side_effects=True, vmem_limit_bytes=48 * 2**20
        ),
    )(*args)


def solution(mesh):
    finer = Mesh(mesh.devices.reshape(NX, NZ, NK, mesh.shape["mp"]), CTX_MP)
    placed = (
        P(CTX_MP, None),
        P(CTX_MP, None, None),
        P(CTX, "mp"),
        P(None, "mp"),
        P(None, "mp"),
        P(None, "mp"),
        P(None, "mp"),
        P(CTX, "mp"),
        P("mp"),
        P("mp"),
    )
    return jax.shard_map(
        local, mesh=finer, in_specs=placed, out_specs=(P(CTX, "mp"), P(CTX, "mp")), check_vma=False
    )
```

```python
import types

import jax
import jax.numpy as jnp
from jax import lax
from jax.experimental import pallas as pl
from jax.experimental.pallas import tpu as pltpu
from jax.sharding import Mesh
from jax.sharding import PartitionSpec as P

HEAD_TOTAL = 32
KV = 8
HD = 128
CONV = 4
TOK = 128
PER = HEAD_TOTAL // KV
NX, NZ, NK, NM = 4, 8, 2, 8
CHIPS = NX * NZ
LAST = CHIPS * NK - 1
CTX = ("ctx_0", "ctx_1", "ctx_2")
CTX_MP = ("ctx_0", "ctx_1", "ctx_2", "mp")
MESH = pl.DeviceIdType.MESH
F32, BF16 = jnp.float32, jnp.bfloat16
NEG = -1e30
SCALE2 = HD**-0.5 * 1.4426950408889634
OFFSETS = sorted(
    ((a, b) for a in range(NX) for b in range(NZ) if a or b),
    key=lambda ab: -(min(ab[0], NX - ab[0]) + min(ab[1], NZ - ab[1])),
)


def place():
    return tuple(lax.axis_index(name) for name in CTX_MP)


def remote(src, dst, send, recv, device):
    return pltpu.make_async_remote_copy(
        src_ref=src, dst_ref=dst, send_sem=send, recv_sem=recv, device_id=device, device_id_type=MESH
    )


def greet(devices):
    barrier = pltpu.get_barrier_semaphore()
    for device in devices:
        pl.semaphore_signal(barrier, inc=1, device_id=device, device_id_type=MESH)
    pl.semaphore_wait(barrier, len(devices))


def exact(a, b, dims=((1,), (0,))):
    return lax.dot_general(
        a, b, (dims, ((), ())), precision=lax.Precision.HIGHEST, preferred_element_type=F32
    )


def silu(v):
    return v / (1.0 + jnp.exp(-v))


def dma(*dims):
    return pltpu.SemaphoreType.DMA(dims)


def scratch():
    vm = pltpu.VMEM
    return {
        "q2": vm((2, TOK, PER * HD), BF16),
        "kvb": vm((NZ, NX, TOK, 2 * HD), BF16),
        "hall": vm((NM, TOK + 16, 512), BF16),
        "wx": vm((4096, HD), BF16),
        "hidq": vm((2, NX * TOK, 512), BF16),
        "qs": vm((2 * PER * TOK, HD), BF16),
        "m_s": vm((8, 2 * PER * TOK), F32),
        "l_s": vm((8, 2 * PER * TOK), F32),
        "acc": vm((HD, 2 * PER * TOK), F32),
        "stat": vm((8, PER * TOK), F32),
        "acc_in": vm((HD, PER * TOK), F32),
        "stat_in": vm((8, PER * TOK), F32),
        "hid_t": vm((2, 512, NX * TOK), BF16),
        "target": vm((PER, TOK, HD), F32),
        "ext": vm((TOK + 8, 6 * HD), F32),
        "ext2": vm((TOK + 8, HD), F32),
        "growth": vm((PER, TOK, TOK), F32),
        "to_end": vm((PER, TOK, TOK), F32),
        "within": vm((PER, TOK, TOK), F32),
        "mix": vm((PER, TOK, TOK), F32),
        "read": vm((PER, TOK, HD), F32),
        "inner": vm((PER, TOK, HD), F32),
        "up": vm((PER, TOK, HD), F32),
        "bconv": vm((TOK, HD), F32),
        "xconv": vm((TOK, HD), F32),
        "xpre": vm((TOK, HD), F32),
        "state": vm((2, PER, HD, HD), F32),
        "csib": vm((2, 2, HD, HD), F32),
        "cback": vm((2, 2, HD, HD), F32),
        "inc": vm((2, PER, HD, HD), F32),
        "dec": vm((8, HD), F32),
        "dsib": vm((8, HD), F32),
        "dsend": vm((2, 8, HD), F32),
        "drecv": vm((CHIPS, 8, HD), F32),
        "zsend": vm((2, CHIPS, 8, HD), F32),
        "zrecv": vm((2, CHIPS, 8, HD), F32),
        "zbs": vm((2, CHIPS, 8, HD), F32),
        "zbr": vm((2, CHIPS, 8, HD), F32),
        "ig": vm((NX * TOK, HD), BF16),
        "part": vm((NZ, NK, 64, HD), F32),
        "wrecv": vm((NZ, 64, HD), F32),
        "wsend": vm((NZ, 64, HD), F32),
        "wzr": vm((NZ, 64, HD), F32),
        "own_s": dma(4),
        "yq": dma(2, 7),
        "ykv": dma(2, 7),
        "yh": dma(2, 24),
        "ht": dma(2),
        "xkv": dma(2, NX),
        "xf": dma(2, NX * NZ),
        "ring": dma(2, 32),
        "cq": dma(2),
        "co": dma(2, 2),
        "hq": dma(2, 6),
        "halo": dma(2, 2),
        "cs": dma(2, 3),
        "ds": dma(2, 31),
        "zs": dma(2, 62),
        "bs": dma(2, 62),
        "ks": dma(2, 2),
        "igs": dma(2, 3),
        "wc": dma(2),
        "wz": dma(2, 7),
    }


def layer(
    q_in, kv_in, hid_in, wx, step_size, decay_log, skip_gain, conv_x, conv_b, conv_c, out_s, out_w, *rest
):
    r = types.SimpleNamespace(**dict(zip(scratch(), rest, strict=True)))
    x, z, k, m = place()
    chip = x * NZ + z
    c = chip * NK + k
    sibling = (x, z, 1 - k, m)
    zr, zl = lax.rem(z + 1, NZ), lax.rem(z + NZ - 1, NZ)
    y_peers = [(x, z, k, lax.rem(m + d, NM)) for d in range(1, NM)]
    x_peers = [(lax.rem(x + d, NX), z, k, m) for d in range(1, NX)]
    z_peers = [(x, lax.rem(z + d, NZ), k, m) for d in range(1, NZ)]
    plane = [(lax.rem(x + a, NX), lax.rem(z + b, NZ), k, m) for a, b in OFFSETS]

    def at_ctx(i):
        return (lax.div(i, NZ * NK), lax.rem(lax.div(i, NK), NZ), lax.rem(i, NK), m)

    following, previous = at_ctx(lax.rem(c + 1, LAST + 1)), at_ctx(lax.rem(c + LAST, LAST + 1))
    greet([*y_peers, *plane, sibling, following, previous])
    sent = []

    def go(*args):
        move = remote(*args)
        move.start()
        sent.append(move)
        return move

    def arrived(moves):
        for move in moves:
            move.wait_recv()

    rows = pl.ds(pl.multiple_of(m * 16, 16), 16)

    def columns(i, width):
        return pl.ds(pl.multiple_of(i * width, width), width)

    def hidden_copy(way, step, part):
        block = lax.rem(m - (step - 1) + NM, NM) if way == 0 else lax.rem(m + step - 1, NM)
        peer = y_peers[0] if way == 0 else y_peers[-1]
        at = (way * 4 + step - 1) * 3 + part
        slot = r.hall.at[block, pl.ds((16, 80, 0)[part], (64, 64, 16)[part])]
        source = hid_in.at[pl.ds(64 * part, 64)] if step == 1 and part < 2 else slot
        return remote(source, slot, r.yh.at[0, at], r.yh.at[1, at], peer)

    def hidden_parts(way, step):
        return (0, 1, 2) if step < 4 else ((0, 2), (1,))[way]

    def pass_on(step):
        for part in range(3):
            for way in range(2):
                if part in hidden_parts(way, step):
                    hidden_copy(way, step, part).wait_recv()
                    if step < 4 and part in hidden_parts(way, step + 1):
                        hidden_copy(way, step + 1, part).start()

    end = remote(
        hid_in.at[pl.ds(TOK - 16, 16)], r.hall.at[m, pl.ds(0, 16)], r.ht.at[0], r.ht.at[1], following
    )

    @pl.when(c < LAST)
    def _():
        end.start()

    for part in range(2):
        for way in range(2):
            hidden_copy(way, 1, part).start()
    kv_moves = [
        go(kv_in.at[:, columns(p[3], 256)], r.kvb.at[z, x, rows], r.ykv.at[0, d], r.ykv.at[1, d], p)
        for d, p in enumerate(y_peers)
    ]
    q_moves = [
        go(q_in.at[:, columns(p[3], 512)], r.q2.at[0, rows], r.yq.at[0, d], r.yq.at[1, d], p)
        for d, p in enumerate(y_peers)
    ]
    mine = [
        pltpu.make_async_copy(kv_in.at[:, columns(m, 256)], r.kvb.at[z, x, rows], r.own_s.at[0]),
        pltpu.make_async_copy(q_in.at[:, columns(m, 512)], r.q2.at[0, rows], r.own_s.at[1]),
        pltpu.make_async_copy(hid_in, r.hall.at[m, pl.ds(16, TOK)], r.own_s.at[2]),
    ]
    wx_move = pltpu.make_async_copy(wx, r.wx, r.own_s.at[3])
    for move in [*mine, wx_move]:
        move.start()

    row = lax.broadcasted_iota(jnp.int32, (TOK, TOK), 0)
    col = lax.broadcasted_iota(jnp.int32, (TOK, TOK), 1)
    causal = row >= col
    lower = jnp.where(causal, 1.0, 0.0)
    rate = -jnp.exp(decay_log[...])

    def step_of(h):
        return jnp.broadcast_to(step_size[:, h : h + 1], (TOK, HD))

    for h in range(PER):
        log_decay = exact(lower, step_of(h) * rate[:, h : h + 1])
        final = log_decay[TOK - 1 :]
        r.growth[h] = jnp.exp(log_decay)
        r.to_end[h] = jnp.exp(final - log_decay)
        r.within[h] = jnp.where(
            causal, jnp.exp(jnp.where(causal, log_decay - log_decay.T, 0.0)), 0.0
        )
        r.dec[h : h + 1] = jnp.exp(final)
        r.dec[PER + h : PER + h + 1] = jnp.exp(final)
    d_move = go(r.dec, r.dsib, r.cs.at[0, 2], r.cs.at[1, 2], sibling)

    for xs in range(1, NX):

        @pl.when(xs > x)
        def _(xs=xs):
            r.kvb[:, xs] = jnp.zeros((NZ, TOK, 2 * HD), BF16)

    r.m_s[...] = jnp.full(r.m_s.shape, NEG, F32)
    r.l_s[...] = jnp.zeros(r.l_s.shape, F32)
    r.acc[...] = jnp.zeros(r.acc.shape, F32)

    def in_ring(xs):
        return (x == xs) | (x == xs + 2) | ((x == 1) & (xs == 0))

    def by_x(xs):
        return (x == 3 - xs) if xs < 2 else (x == 3) & (xs == 2)

    def ring_copy(way, step, xs):
        if way == 0:
            column, device = lax.rem(z - (step - 1) + NZ, NZ), (x, zr, k, m)
        else:
            column, device = lax.rem(z + (step - 1), NZ), (x, zl, k, m)
        slot = r.kvb.at[column, xs]
        at = (way * 4 + step - 1) * NX + xs
        return remote(slot, slot, r.ring.at[0, at], r.ring.at[1, at], device)

    def first_copy(xs, to):
        slot = r.kvb.at[z, xs]
        return remote(slot, slot, r.xkv.at[0, to], r.xkv.at[1, to], (to, z, k, m))

    FIRST = ((0, 1), (0, 2), (1, 3))

    def across(column, xs):
        to = (3, 2, 3)[xs]
        slot, at = r.kvb.at[column, xs], xs * NZ + column
        return remote(slot, slot, r.xf.at[0, at], r.xf.at[1, at], (to, z, k, m))

    for move in mine:
        move.wait()
    arrived(kv_moves)
    for xs in range(NX):

        @pl.when(x == xs)
        def _(xs=xs):
            for source, to in FIRST:
                if source == xs:
                    first_copy(xs, to).start()
            ring_copy(0, 1, xs).start()
            ring_copy(1, 1, xs).start()
            if xs < 3:
                across(z, xs).start()

    @pl.when(c > 0)
    def _():
        end.wait_recv()

    @pl.when(c == 0)
    def _():
        r.hall[m, :16] = jnp.zeros((16, 512), BF16)

    for way in range(2):
        hidden_copy(way, 1, 2).start()
    pass_on(1)

    arrived(q_moves)
    cq_move = go(r.q2.at[0], r.q2.at[1], r.cq.at[0], r.cq.at[1], sibling)
    for source, to in FIRST:

        @pl.when(x == to)
        def _(source=source, to=to):
            first_copy(source, to).wait_recv()
            ring_copy(0, 1, source).start()
            ring_copy(1, 1, source).start()

    r.ext[8:, HD : 2 * HD] = r.kvb[z, x, :, :HD].astype(F32)
    r.ext[8:, 2 * HD :] = r.q2[0].astype(F32)

    at = pl.ds(HD, 5 * HD)
    tail = remote(
        r.ext.at[pl.ds(TOK, 8), at], r.ext.at[pl.ds(0, 8), at], r.halo.at[0, 0], r.halo.at[1, 0], following
    )

    @pl.when(c < LAST)
    def _():
        tail.start()

    @pl.when(c == 0)
    def _():
        r.ext[:8, HD:] = jnp.zeros((8, 5 * HD), F32)

    d_move.wait_recv()
    for h in range(2):
        chip_decay = r.dec[...] * r.dsib[...]
        decay_row = jnp.where(k == 0, chip_decay[h : h + 1], chip_decay[2 + h : 3 + h])
        r.dsend[h] = jnp.broadcast_to(decay_row, (8, HD))
    decay_moves = [
        go(r.dsend.at[lax.div(p[0], 2)], r.drecv.at[chip], r.ds.at[0, i], r.ds.at[1, i], p)
        for i, p in enumerate(plane)
    ]
    r.drecv[chip] = r.dsend[lax.div(x, 2)]

    for h in range(PER):
        r.qs[h * TOK : (h + 1) * TOK] = r.q2[0, :, h * HD : (h + 1) * HD]
    pass_on(2)
    cq_move.wait_recv()
    for h in range(PER):
        r.qs[(PER + h) * TOK : (PER + h + 1) * TOK] = r.q2[1, :, h * HD : (h + 1) * HD]

    def attend(column, masked):
        for xs in range(NX - 1):

            @pl.when(by_x(xs))
            def _(xs=xs):
                across(column, xs).wait_recv()

        block = r.kvb[column].reshape(NX * TOK, 2 * HD)
        scores = lax.dot_general(
            block[:, :HD], r.qs[...], (((1,), (1,)), ((), ())), preferred_element_type=F32
        )
        parts = [scores[b * TOK : (b + 1) * TOK] for b in range(NX)]
        if masked:
            key = lax.broadcasted_iota(jnp.int32, (TOK, 2 * PER * TOK), 0)
            query = lax.broadcasted_iota(jnp.int32, (TOK, 2 * PER * TOK), 1)
            core = jnp.where(query < PER * TOK, k, 1 - k)
            own = key + k * TOK <= lax.rem(query, TOK) + core * TOK
            parts = [jnp.where((b != x) | own, part, NEG) for b, part in enumerate(parts)]
            shut = [jnp.where(b <= x, 0.0, NEG) for b in range(NX)]
        else:
            shut = [jnp.where((b < x) | ((b == x) & (column < z)), 0.0, NEG) for b in range(NX)]
        before = now = r.m_s[:1]
        for part, off in zip(parts, shut, strict=True):
            now = jnp.maximum(now, jnp.max(part, axis=0, keepdims=True) * SCALE2 + off)
        alpha = jnp.exp2(before - now)
        parts = [
            jnp.exp2(part * SCALE2 - (now - off)) for part, off in zip(parts, shut, strict=True)
        ]
        total = r.l_s[:1] * alpha
        for part in parts:
            total = total + jnp.sum(part, axis=0, keepdims=True)
        r.l_s[:1] = total
        r.m_s[:1] = now
        weights = jnp.concatenate([part.astype(BF16) for part in parts], axis=0)
        r.acc[...] = r.acc[...] * alpha + lax.dot_general(
            block[:, HD:], weights, (((0,), (0,)), ((), ())), preferred_element_type=F32
        )

    def receive(step):
        for own in (True, False):
            for xs in range(NX) if own else range(NX - 2):

                @pl.when((x == xs) if own else in_ring(xs) & (x != xs))
                def _(own=own, xs=xs):
                    for way in range(2):
                        if way == 1 and step == 4:
                            continue
                        column = right(step) if way == 0 else left(step)
                        ring_copy(way, step, xs).wait_recv()
                        if step < (4, 3)[way]:
                            ring_copy(way, step + 1, xs).start()
                        if own and xs < 3:
                            across(column, xs).start()

    def right(step):
        return lax.rem(z - step + NZ, NZ)

    def left(step):
        return lax.rem(z + step, NZ)

    def conv(first, taps):
        width = taps.shape[1]
        total = jnp.zeros((TOK, width), F32)
        for j in range(CONV):
            total = total + taps[j : j + 1, :] * r.ext[5 + j : 5 + j + TOK, first : first + width]
        return total

    def inputs():
        @pl.when(c > 0)
        def _():
            tail.wait_recv()

        r.bconv[...] = silu(conv(HD, conv_b))

    def readouts():
        c_conv = silu(conv(2 * HD, conv_c))
        b_t = r.bconv[...].T
        for h in range(PER):
            read = c_conv[:, h * HD : (h + 1) * HD]
            r.read[h] = read
            r.mix[h] = exact(read, b_t) * r.within[h]

    def project():
        total = jnp.zeros((TOK + 16, HD), F32)
        for j in range(NM):
            total = total + jnp.dot(
                r.hall[j], r.wx[j * 512 : (j + 1) * 512], preferred_element_type=F32
            )
        r.ext[:, :HD] = total[8:].astype(BF16).astype(F32)

    def hidden_over_x():
        moves = []
        for d in range(1, NX):
            there = lax.rem(x + d, NX)
            for e in range(2):
                at = (d - 1) * 2 + e
                into = r.hidq.at[e, columns(x, TOK)]
                moves.append(
                    go(
                        r.hall.at[2 * there + e, pl.ds(16, TOK)], into,
                        r.hq.at[0, at], r.hq.at[1, at], x_peers[d - 1],
                    )
                )
        for e in range(2):
            r.hidq[e, columns(x, TOK)] = r.hall[2 * x + e, 16:]
        return moves

    def states():
        x_pre = conv(0, conv_x)
        x_conv = silu(x_pre)
        r.xpre[...] = x_pre
        r.xconv[...] = x_conv
        b_t = r.bconv[...].T
        for h in range(PER):
            r.state[0, h] = exact(b_t, r.to_end[h] * (step_of(h) * x_conv))

    def inners():
        x_conv = r.xconv[...]
        for h in range(PER):
            r.inner[h] = exact(r.mix[h], step_of(h) * x_conv) + skip_gain[:, h : h + 1] * x_conv

    first_of, first_other = pl.ds(2 * k, 2), pl.ds(2 * (1 - k), 2)

    def scan(way):
        state = r.state.at[way]
        move = go(state.at[first_other], r.csib.at[way], r.cs.at[0, way], r.cs.at[1, way], sibling)
        yield
        move.wait_recv()
        d_mine = [jnp.where(k == 0, r.dec[h : h + 1], r.dec[2 + h : 3 + h]) for h in range(2)]
        d_other = [jnp.where(k == 0, r.dsib[h : h + 1], r.dsib[2 + h : 3 + h]) for h in range(2)]
        mine_first = (k == 0) if way == 0 else (k == 1)
        for h in range(2):
            own, theirs = state[2 * k + h], r.csib[way, h]
            near = jnp.where(mine_first, theirs, own)
            far = jnp.where(mine_first, own, theirs)
            d_near = jnp.where(mine_first, d_other[h], d_mine[h])
            both = far * d_near + near
            r.zsend[way, 16 * h : 16 * h + 16] = both.reshape(16, 8, HD)
        moves = []
        for i, p in enumerate(plane):
            at = way * 31 + i
            there = p[0] * NZ + p[1]
            moves.append(
                go(r.zsend.at[way, there], r.zrecv.at[way, chip], r.zs.at[0, at], r.zs.at[1, at], p)
            )
        r.zrecv[way, chip] = r.zsend[way, chip]
        yield
        arrived(moves)
        enters = jnp.zeros((8, HD), F32)
        for j in range(CHIPS) if way == 0 else range(CHIPS - 1, -1, -1):
            r.zbs[way, j] = enters
            enters = r.drecv[j] * enters + r.zrecv[way, j]
        moves = []
        for i, p in enumerate(plane):
            at = way * 31 + i
            there = p[0] * NZ + p[1]
            moves.append(
                go(r.zbs.at[way, there], r.zbr.at[way, chip], r.bs.at[0, at], r.bs.at[1, at], p)
            )
        r.zbr[way, chip] = r.zbs[way, chip]
        yield
        arrived(moves)
        for h in range(2):
            entering = r.zbr[way, 16 * h : 16 * h + 16].reshape(HD, HD)
            own, theirs = state[2 * k + h], r.csib[way, h]
            d_first = jnp.where(mine_first, d_mine[h], d_other[h])
            second = d_first * entering + jnp.where(mine_first, own, theirs)
            r.inc[way, 2 * k + h] = jnp.where(mine_first, entering, second)
            r.cback[way, h] = jnp.where(mine_first, second, entering)
        move = go(r.cback.at[way], r.inc.at[way, first_of], r.ks.at[0, way], r.ks.at[1, way], sibling)
        yield
        move.wait_recv()
        yield

    receive(1)
    pass_on(3)
    receive(2)
    inputs()
    wx_move.wait()
    pass_on(4)
    project()
    states()
    forward = scan(0)
    next(forward)
    arrived(decay_moves)
    receive(3)
    next(forward)
    hq_moves = hidden_over_x()
    attend(z, True)
    attend(right(1), False)
    attend(left(1), False)
    receive(4)
    readouts()
    inners()
    attend(right(2), False)
    next(forward)
    attend(left(2), False)
    attend(right(3), False)
    attend(left(3), False)
    attend(right(4), False)
    half = PER * TOK
    r.stat[:1] = r.m_s[:1, half:]
    r.stat[1:2] = r.l_s[:1, half:]
    r.stat[2:] = jnp.zeros((6, half), F32)
    o_moves = [
        go(r.acc.at[:, pl.ds(half, half)], r.acc_in, r.co.at[0, 0], r.co.at[1, 0], sibling),
        go(r.stat, r.stat_in, r.co.at[0, 1], r.co.at[1, 1], sibling),
    ]
    next(forward)
    arrived(o_moves)
    other, mine_max = r.stat_in[:1], r.m_s[:1, :half]
    both = jnp.maximum(other, mine_max)
    a0, a1 = jnp.exp2(mine_max - both), jnp.exp2(other - both)
    norm = r.l_s[:1, :half] * a0 + r.stat_in[1:2] * a1
    result = (r.acc[:, :half] * a0 + r.acc_in[...] * a1) / norm
    for h in range(PER):
        r.target[h] = result[:, h * TOK : (h + 1) * TOK].T
    next(forward)
    for h in range(PER):
        student = r.inner[h] + r.growth[h] * exact(r.read[h], r.inc[0, h])
        out_s[:, h * HD : (h + 1) * HD] = student.astype(BF16)
        r.up[h] = 2.0 * (student - r.target[h]) / (HEAD_TOTAL * HD)
        r.state[1, h] = exact((r.growth[h] * r.read[h]).T, r.up[h])

    backward = scan(1)
    next(backward)
    next(backward)
    x_grad = jnp.zeros((TOK, HD), F32)
    for h in range(PER):
        up = r.up[h]
        x_grad = x_grad + step_of(h) * exact(r.mix[h].T, up) + skip_gain[:, h : h + 1] * up
    arrived(hq_moves)
    for e in range(2):
        r.hid_t[e] = r.hidq[e].T
    next(backward)

    for move in sent:
        move.wait_send()
    sent.clear()

    @pl.when(c < LAST)
    def _():
        tail.wait_send()
        end.wait_send()

    for way in range(2):
        for step in range(1, 5):
            for part in hidden_parts(way, step):
                hidden_copy(way, step, part).wait_send()

    for source, to in FIRST:

        @pl.when(x == source)
        def _(source=source, to=to):
            first_copy(source, to).wait_send()

    for xs in range(NX):

        @pl.when(in_ring(xs))
        def _(xs=xs):
            for way in range(2):
                for step in range(1, (4, 3)[way] + 1):
                    ring_copy(way, step, xs).wait_send()

        if xs < 3:

            @pl.when(x == xs)
            def _(xs=xs):
                for column in range(NZ):
                    across(column, xs).wait_send()

    next(backward)
    next(backward)
    b_conv = r.bconv[...]
    for h in range(PER):
        x_grad = x_grad + step_of(h) * r.to_end[h] * exact(b_conv, r.inc[1, h])
    x_pre = r.xpre[...]
    sigma = 1.0 / (1.0 + jnp.exp(-x_pre))
    r.ext2[:TOK] = x_grad * sigma * (1.0 + x_pre * (1.0 - sigma))
    head = remote(
        r.ext2.at[pl.ds(0, 8)], r.ext2.at[pl.ds(TOK, 8)], r.halo.at[0, 1], r.halo.at[1, 1], previous
    )

    @pl.when(c > 0)
    def _():
        head.start()

    @pl.when(c == LAST)
    def _():
        r.ext2[TOK:] = jnp.zeros((8, HD), F32)

    @pl.when(c < LAST)
    def _():
        head.wait_recv()

    grad = jnp.zeros((TOK, HD), F32)
    for j in range(CONV):
        grad = grad + conv_x[j : j + 1, :] * r.ext2[CONV - 1 - j : CONV - 1 - j + TOK]
    here = r.ig.at[columns(x, TOK)]
    here[...] = grad.astype(BF16)
    moves = [
        go(here, here, r.igs.at[0, d], r.igs.at[1, d], p) for d, p in enumerate(x_peers)
    ]
    arrived(moves)
    for e in range(2):
        product = jnp.dot(r.hid_t[e], r.ig[...], preferred_element_type=F32)
        r.part[4 * e : 4 * e + 4] = product.reshape(4, NK, 64, HD)
    go(r.part.at[:, 1 - k], r.wrecv, r.wc.at[0], r.wc.at[1], sibling).wait_recv()
    for i in range(NZ):
        r.wsend[i] = r.part[i, k] + r.wrecv[i]
    moves = [
        go(r.wsend.at[p[1]], r.wzr.at[z], r.wz.at[0, d], r.wz.at[1, d], p)
        for d, p in enumerate(z_peers)
    ]
    r.wzr[z] = r.wsend[z]
    arrived(moves)
    total = r.wzr[0]
    for i in range(1, NZ):
        total = total + r.wzr[i]
    out_w[...] = total

    for move in sent:
        move.wait_send()

    @pl.when(c > 0)
    def _():
        head.wait_send()


def local(
    query_proj, keyval_proj, hidden, weight_x, conv_x, conv_b, conv_c, step_size, decay_log, skip_gain
):
    args = (
        query_proj, keyval_proj.reshape(16, KV * 2 * HD), hidden, weight_x, step_size,
        decay_log.reshape(1, PER), skip_gain.reshape(1, PER), conv_x, conv_b, conv_c,
    )
    return pl.pallas_call(
        layer,
        out_shape=(
            jax.ShapeDtypeStruct((TOK, PER * HD), BF16),
            jax.ShapeDtypeStruct((64, HD), F32),
        ),
        in_specs=[pl.BlockSpec(memory_space=pl.ANY if i in (0, 2, 3) else pltpu.VMEM) for i in range(len(args))],
        out_specs=[pl.BlockSpec(memory_space=pltpu.VMEM)] * 2,
        scratch_shapes=list(scratch().values()),
        compiler_params=pltpu.CompilerParams(
            collective_id=0, has_side_effects=True, vmem_limit_bytes=48 * 2**20
        ),
    )(*args)


def solution(mesh):
    finer = Mesh(mesh.devices.reshape(NX, NZ, NK, mesh.shape["mp"]), CTX_MP)
    placed = (
        P(CTX_MP, None),
        P(CTX_MP, None, None),
        P(CTX, "mp"),
        P(None, "mp"),
        P(None, "mp"),
        P(None, "mp"),
        P(None, "mp"),
        P(CTX, "mp"),
        P("mp"),
        P("mp"),
    )
    return jax.shard_map(
        local, mesh=finer, in_specs=placed, out_specs=(P(CTX, "mp"), P(CTX, "mp")), check_vma=False
    )
```

```python
import types

import jax
import jax.numpy as jnp
from jax import lax
from jax.experimental import pallas as pl
from jax.experimental.pallas import tpu as pltpu
from jax.sharding import Mesh
from jax.sharding import PartitionSpec as P

HEAD_TOTAL = 32
KV = 8
HD = 128
CONV = 4
TOK = 128
PER = HEAD_TOTAL // KV
NX, NZ, NK, NM = 4, 8, 2, 8
CHIPS = NX * NZ
LAST = CHIPS * NK - 1
CTX = ("ctx_0", "ctx_1", "ctx_2")
CTX_MP = ("ctx_0", "ctx_1", "ctx_2", "mp")
MESH = pl.DeviceIdType.MESH
F32, BF16 = jnp.float32, jnp.bfloat16
NEG = -1e30
SCALE2 = HD**-0.5 * 1.4426950408889634
OFFSETS = sorted(
    ((a, b) for a in range(NX) for b in range(NZ) if a or b),
    key=lambda ab: -(min(ab[0], NX - ab[0]) + min(ab[1], NZ - ab[1])),
)


def place():
    return tuple(lax.axis_index(name) for name in CTX_MP)


def remote(src, dst, send, recv, device):
    return pltpu.make_async_remote_copy(
        src_ref=src, dst_ref=dst, send_sem=send, recv_sem=recv, device_id=device, device_id_type=MESH
    )


def greet(devices):
    barrier = pltpu.get_barrier_semaphore()
    for device in devices:
        pl.semaphore_signal(barrier, inc=1, device_id=device, device_id_type=MESH)
    pl.semaphore_wait(barrier, len(devices))


def exact(a, b, dims=((1,), (0,))):
    return lax.dot_general(
        a, b, (dims, ((), ())), precision=lax.Precision.HIGHEST, preferred_element_type=F32
    )


def silu(v):
    return v / (1.0 + jnp.exp(-v))


def dma(*dims):
    return pltpu.SemaphoreType.DMA(dims)


def scratch():
    vm = pltpu.VMEM
    return {
        "q2": vm((2, TOK, PER * HD), BF16),
        "kvb": vm((NZ, NX, TOK, 2 * HD), BF16),
        "hall": vm((NM, TOK + 16, 512), BF16),
        "wx": vm((4096, HD), BF16),
        "hidq": vm((2, NX * TOK, 512), BF16),
        "qs": vm((2 * PER * TOK, HD), BF16),
        "m_s": vm((8, 2 * PER * TOK), F32),
        "l_s": vm((8, 2 * PER * TOK), F32),
        "acc": vm((HD, 2 * PER * TOK), F32),
        "stat": vm((8, PER * TOK), F32),
        "acc_in": vm((HD, PER * TOK), F32),
        "stat_in": vm((8, PER * TOK), F32),
        "hid_t": vm((2, 512, NX * TOK), BF16),
        "target": vm((PER, TOK, HD), F32),
        "ext": vm((TOK + 8, 6 * HD), F32),
        "ext2": vm((TOK + 8, HD), F32),
        "ext3": vm((24, HD), F32),
        "last": vm((NX, 16, HD), F32),
        "share": vm((16, HD), F32),
        "shares": vm((NX, 16, HD), F32),
        "growth": vm((PER, TOK, TOK), F32),
        "to_end": vm((PER, TOK, TOK), F32),
        "within": vm((PER, TOK, TOK), F32),
        "mix": vm((PER, TOK, TOK), F32),
        "read": vm((PER, TOK, HD), F32),
        "inner": vm((PER, TOK, HD), F32),
        "up": vm((PER, TOK, HD), F32),
        "bconv": vm((TOK, HD), F32),
        "xconv": vm((TOK, HD), F32),
        "xpre": vm((TOK, HD), F32),
        "state": vm((2, PER, HD, HD), F32),
        "csib": vm((2, 2, HD, HD), F32),
        "cback": vm((2, 2, HD, HD), F32),
        "inc": vm((2, PER, HD, HD), F32),
        "dec": vm((8, HD), F32),
        "dsib": vm((8, HD), F32),
        "dsend": vm((2, 8, HD), F32),
        "drecv": vm((CHIPS, 8, HD), F32),
        "zsend": vm((2, CHIPS, 8, HD), F32),
        "zrecv": vm((2, CHIPS, 8, HD), F32),
        "zbs": vm((2, CHIPS, 8, HD), F32),
        "zbr": vm((2, CHIPS, 8, HD), F32),
        "ig": vm((NX * TOK, HD), BF16),
        "part": vm((NZ, NK, 64, HD), F32),
        "wrecv": vm((NZ, 64, HD), F32),
        "wsend": vm((NZ, 64, HD), F32),
        "wzr": vm((NZ, 64, HD), F32),
        "own_s": dma(4),
        "yq": dma(2, 7),
        "ykv": dma(2, 7),
        "yh": dma(2, 24),
        "ht": dma(2),
        "xkv": dma(2, NX),
        "xf": dma(2, NX * NZ),
        "ring": dma(2, 32),
        "cq": dma(2),
        "co": dma(2, 2),
        "hq": dma(2, 6),
        "halo": dma(2, 2),
        "cs": dma(2, 3),
        "ds": dma(2, 31),
        "zs": dma(2, 62),
        "bs": dma(2, 62),
        "ks": dma(2, 2),
        "igs": dma(2, 6),
        "hs": dma(2, NX),
        "wc": dma(2),
        "wz": dma(2, 7),
    }


def layer(
    q_in, kv_in, hid_in, wx, step_size, decay_log, skip_gain, conv_x, conv_b, conv_c, out_s, out_w, *rest
):
    r = types.SimpleNamespace(**dict(zip(scratch(), rest, strict=True)))
    x, z, k, m = place()
    chip = x * NZ + z
    c = chip * NK + k
    sibling = (x, z, 1 - k, m)
    zr, zl = lax.rem(z + 1, NZ), lax.rem(z + NZ - 1, NZ)
    y_peers = [(x, z, k, lax.rem(m + d, NM)) for d in range(1, NM)]
    x_peers = [(lax.rem(x + d, NX), z, k, m) for d in range(1, NX)]
    z_peers = [(x, lax.rem(z + d, NZ), k, m) for d in range(1, NZ)]
    plane = [(lax.rem(x + a, NX), lax.rem(z + b, NZ), k, m) for a, b in OFFSETS]

    def at_ctx(i):
        return (lax.div(i, NZ * NK), lax.rem(lax.div(i, NK), NZ), lax.rem(i, NK), m)

    following, previous = at_ctx(lax.rem(c + 1, LAST + 1)), at_ctx(lax.rem(c + LAST, LAST + 1))
    before = [(lax.rem(previous[0] + i, NX), *previous[1:]) for i in range(NX)]
    after = [(lax.rem(following[0] + i, NX), *following[1:]) for i in range(NX)]
    greet([*y_peers, *plane, sibling, *before, *after])
    sent = []

    def go(*args):
        move = remote(*args)
        move.start()
        sent.append(move)
        return move

    def arrived(moves):
        for move in moves:
            move.wait_recv()

    rows = pl.ds(pl.multiple_of(m * 16, 16), 16)

    def columns(i, width):
        return pl.ds(pl.multiple_of(i * width, width), width)

    def hidden_copy(way, step, part):
        block = lax.rem(m - (step - 1) + NM, NM) if way == 0 else lax.rem(m + step - 1, NM)
        peer = y_peers[0] if way == 0 else y_peers[-1]
        at = (way * 4 + step - 1) * 3 + part
        slot = r.hall.at[block, pl.ds((16, 80, 0)[part], (64, 64, 16)[part])]
        source = hid_in.at[pl.ds(64 * part, 64)] if step == 1 and part < 2 else slot
        return remote(source, slot, r.yh.at[0, at], r.yh.at[1, at], peer)

    def hidden_parts(way, step):
        return (0, 1, 2) if step < 4 else ((0, 2), (1,))[way]

    def pass_on(step):
        for part in range(3):
            for way in range(2):
                if part in hidden_parts(way, step):
                    hidden_copy(way, step, part).wait_recv()
                    if step < 4 and part in hidden_parts(way, step + 1):
                        hidden_copy(way, step + 1, part).start()

    end = remote(
        hid_in.at[pl.ds(TOK - 16, 16)], r.hall.at[m, pl.ds(0, 16)], r.ht.at[0], r.ht.at[1], following
    )

    @pl.when(c < LAST)
    def _():
        end.start()

    for part in range(2):
        for way in range(2):
            hidden_copy(way, 1, part).start()
    kv_moves = [
        go(kv_in.at[:, columns(p[3], 256)], r.kvb.at[z, x, rows], r.ykv.at[0, d], r.ykv.at[1, d], p)
        for d, p in enumerate(y_peers)
    ]
    mine = [
        pltpu.make_async_copy(kv_in.at[:, columns(m, 256)], r.kvb.at[z, x, rows], r.own_s.at[0]),
        pltpu.make_async_copy(q_in.at[:, columns(m, 512)], r.q2.at[0, rows], r.own_s.at[1]),
        pltpu.make_async_copy(hid_in, r.hall.at[m, pl.ds(16, TOK)], r.own_s.at[2]),
    ]
    wx_move = pltpu.make_async_copy(wx, r.wx, r.own_s.at[3])
    for move in [*mine, wx_move]:
        move.start()

    row = lax.broadcasted_iota(jnp.int32, (TOK, TOK), 0)
    col = lax.broadcasted_iota(jnp.int32, (TOK, TOK), 1)
    causal = row >= col
    lower = jnp.where(causal, 1.0, 0.0)
    rate = -jnp.exp(decay_log[...])

    def step_of(h):
        return jnp.broadcast_to(step_size[:, h : h + 1], (TOK, HD))

    for h in range(PER):
        log_decay = exact(lower, step_of(h) * rate[:, h : h + 1])
        final = log_decay[TOK - 1 :]
        r.growth[h] = jnp.exp(log_decay)
        r.to_end[h] = jnp.exp(final - log_decay)
        r.within[h] = jnp.where(
            causal, jnp.exp(jnp.where(causal, log_decay - log_decay.T, 0.0)), 0.0
        )
        r.dec[h : h + 1] = jnp.exp(final)
        r.dec[PER + h : PER + h + 1] = jnp.exp(final)
    d_move = go(r.dec, r.dsib, r.cs.at[0, 2], r.cs.at[1, 2], sibling)

    for xs in range(1, NX):

        @pl.when(xs > x)
        def _(xs=xs):
            r.kvb[:, xs] = jnp.zeros((NZ, TOK, 2 * HD), BF16)

    r.m_s[...] = jnp.full(r.m_s.shape, NEG, F32)
    r.l_s[...] = jnp.zeros(r.l_s.shape, F32)
    r.acc[...] = jnp.zeros(r.acc.shape, F32)

    def in_ring(xs):
        return (x == xs) | (x == xs + 2) | ((x == 1) & (xs == 0))

    def by_x(xs):
        return (x == 3 - xs) if xs < 2 else (x == 3) & (xs == 2)

    def ring_copy(way, step, xs):
        if way == 0:
            column, device = lax.rem(z - (step - 1) + NZ, NZ), (x, zr, k, m)
        else:
            column, device = lax.rem(z + (step - 1), NZ), (x, zl, k, m)
        slot = r.kvb.at[column, xs]
        at = (way * 4 + step - 1) * NX + xs
        return remote(slot, slot, r.ring.at[0, at], r.ring.at[1, at], device)

    def first_copy(xs, to):
        slot = r.kvb.at[z, xs]
        return remote(slot, slot, r.xkv.at[0, to], r.xkv.at[1, to], (to, z, k, m))

    FIRST = ((0, 1), (0, 2), (1, 3))

    def across(column, xs):
        to = (3, 2, 3)[xs]
        slot, at = r.kvb.at[column, xs], xs * NZ + column
        return remote(slot, slot, r.xf.at[0, at], r.xf.at[1, at], (to, z, k, m))

    for move in mine:
        move.wait()
    arrived(kv_moves)
    for xs in range(NX):

        @pl.when(x == xs)
        def _(xs=xs):
            for source, to in FIRST:
                if source == xs:
                    first_copy(xs, to).start()
            ring_copy(0, 1, xs).start()
            ring_copy(1, 1, xs).start()
            if xs < 3:
                across(z, xs).start()

    @pl.when(c > 0)
    def _():
        end.wait_recv()

    @pl.when(c == 0)
    def _():
        r.hall[m, :16] = jnp.zeros((16, 512), BF16)

    for way in range(2):
        hidden_copy(way, 1, 2).start()
    pass_on(1)

    q_moves = [
        go(q_in.at[:, columns(p[3], 512)], r.q2.at[0, rows], r.yq.at[0, d], r.yq.at[1, d], p)
        for d, p in enumerate(y_peers)
    ]
    def tail(i):
        at = (pl.ds(HD, HD), pl.ds(2 * HD, 4 * HD))[i]
        return remote(
            r.ext.at[pl.ds(TOK, 8), at], r.ext.at[pl.ds(0, 8), at],
            r.halo.at[0, i], r.halo.at[1, i], following,
        )

    def pass_tail(i):
        @pl.when(c < LAST)
        def _():
            tail(i).start()

    def tail_here(i):
        @pl.when(c > 0)
        def _():
            tail(i).wait_recv()

    r.ext[8:, HD : 2 * HD] = r.kvb[z, x, :, :HD].astype(F32)
    pass_tail(0)

    @pl.when(c == 0)
    def _():
        r.ext[:8, HD:] = jnp.zeros((8, 5 * HD), F32)

    for source, to in FIRST:

        @pl.when(x == to)
        def _(source=source, to=to):
            first_copy(source, to).wait_recv()
            ring_copy(0, 1, source).start()
            ring_copy(1, 1, source).start()

    pass_on(2)

    def queries():
        arrived(q_moves)
        move = go(r.q2.at[0], r.q2.at[1], r.cq.at[0], r.cq.at[1], sibling)
        r.ext[8:, 2 * HD :] = r.q2[0].astype(F32)
        pass_tail(1)
        for h in range(PER):
            r.qs[h * TOK : (h + 1) * TOK] = r.q2[0, :, h * HD : (h + 1) * HD]
        return move

    def sibling_queries(move):
        move.wait_recv()
        for h in range(PER):
            r.qs[(PER + h) * TOK : (PER + h + 1) * TOK] = r.q2[1, :, h * HD : (h + 1) * HD]

    def attend(column, masked):
        for xs in range(NX - 1):

            @pl.when(by_x(xs))
            def _(xs=xs):
                across(column, xs).wait_recv()

        block = r.kvb[column].reshape(NX * TOK, 2 * HD)
        scores = lax.dot_general(
            block[:, :HD], r.qs[...], (((1,), (1,)), ((), ())), preferred_element_type=F32
        )
        parts = [scores[b * TOK : (b + 1) * TOK] for b in range(NX)]
        if masked:
            key = lax.broadcasted_iota(jnp.int32, (TOK, 2 * PER * TOK), 0)
            query = lax.broadcasted_iota(jnp.int32, (TOK, 2 * PER * TOK), 1)
            core = jnp.where(query < PER * TOK, k, 1 - k)
            own = key + k * TOK <= lax.rem(query, TOK) + core * TOK
            parts = [jnp.where((b != x) | own, part, NEG) for b, part in enumerate(parts)]
            shut = [jnp.where(b <= x, 0.0, NEG) for b in range(NX)]
        else:
            shut = [jnp.where((b < x) | ((b == x) & (column < z)), 0.0, NEG) for b in range(NX)]
        before = now = r.m_s[:1]
        for part, off in zip(parts, shut, strict=True):
            now = jnp.maximum(now, jnp.max(part, axis=0, keepdims=True) * SCALE2 + off)
        alpha = jnp.exp2(before - now)
        parts = [
            jnp.exp2(part * SCALE2 - (now - off)) for part, off in zip(parts, shut, strict=True)
        ]
        total = r.l_s[:1] * alpha
        for part in parts:
            total = total + jnp.sum(part, axis=0, keepdims=True)
        r.l_s[:1] = total
        r.m_s[:1] = now
        weights = jnp.concatenate([part.astype(BF16) for part in parts], axis=0)
        r.acc[...] = r.acc[...] * alpha + lax.dot_general(
            block[:, HD:], weights, (((0,), (0,)), ((), ())), preferred_element_type=F32
        )

    def receive(step):
        for own in (True, False):
            for xs in range(NX) if own else range(NX - 2):

                @pl.when((x == xs) if own else in_ring(xs) & (x != xs))
                def _(own=own, xs=xs):
                    for way in range(2):
                        if way == 1 and step == 4:
                            continue
                        column = right(step) if way == 0 else left(step)
                        ring_copy(way, step, xs).wait_recv()
                        if step < (4, 3)[way]:
                            ring_copy(way, step + 1, xs).start()
                        if own and xs < 3:
                            across(column, xs).start()

    def right(step):
        return lax.rem(z - step + NZ, NZ)

    def left(step):
        return lax.rem(z + step, NZ)

    def conv(first, taps):
        width = taps.shape[1]
        total = jnp.zeros((TOK, width), F32)
        for j in range(CONV):
            total = total + taps[j : j + 1, :] * r.ext[5 + j : 5 + j + TOK, first : first + width]
        return total

    def inputs():
        tail_here(0)
        r.bconv[...] = silu(conv(HD, conv_b))

    def readouts():
        tail_here(1)
        c_conv = silu(conv(2 * HD, conv_c))
        b_t = r.bconv[...].T
        for h in range(PER):
            read = c_conv[:, h * HD : (h + 1) * HD]
            r.read[h] = read
            r.mix[h] = exact(read, b_t) * r.within[h]

    def project():
        total = jnp.zeros((TOK + 16, HD), F32)
        for j in range(NM):
            total = total + jnp.dot(
                r.hall[j], r.wx[j * 512 : (j + 1) * 512], preferred_element_type=F32
            )
        r.ext[:, :HD] = total[8:].astype(BF16).astype(F32)

    def hidden_over_x():
        moves = []
        for d in range(1, NX):
            there = lax.rem(x + d, NX)
            for e in range(2):
                at = (d - 1) * 2 + e
                into = r.hidq.at[e, columns(x, TOK)]
                moves.append(
                    go(
                        r.hall.at[2 * there + e, pl.ds(16, TOK)], into,
                        r.hq.at[0, at], r.hq.at[1, at], x_peers[d - 1],
                    )
                )
        for e in range(2):
            r.hidq[e, columns(x, TOK)] = r.hall[2 * x + e, 16:]
        return moves

    def states():
        x_pre = conv(0, conv_x)
        x_conv = silu(x_pre)
        r.xpre[...] = x_pre
        r.xconv[...] = x_conv
        b_t = r.bconv[...].T
        for h in range(PER):
            r.state[0, h] = exact(b_t, r.to_end[h] * (step_of(h) * x_conv))

    def inners():
        x_conv = r.xconv[...]
        for h in range(PER):
            r.inner[h] = exact(r.mix[h], step_of(h) * x_conv) + skip_gain[:, h : h + 1] * x_conv

    first_of, first_other = pl.ds(2 * k, 2), pl.ds(2 * (1 - k), 2)

    def scan(way):
        state = r.state.at[way]
        move = go(state.at[first_other], r.csib.at[way], r.cs.at[0, way], r.cs.at[1, way], sibling)
        yield
        move.wait_recv()
        d_mine = [jnp.where(k == 0, r.dec[h : h + 1], r.dec[2 + h : 3 + h]) for h in range(2)]
        d_other = [jnp.where(k == 0, r.dsib[h : h + 1], r.dsib[2 + h : 3 + h]) for h in range(2)]
        mine_first = (k == 0) if way == 0 else (k == 1)
        for h in range(2):
            own, theirs = state[2 * k + h], r.csib[way, h]
            near = jnp.where(mine_first, theirs, own)
            far = jnp.where(mine_first, own, theirs)
            d_near = jnp.where(mine_first, d_other[h], d_mine[h])
            both = far * d_near + near
            r.zsend[way, 16 * h : 16 * h + 16] = both.reshape(16, 8, HD)
        moves = []
        for i, p in enumerate(plane):
            at = way * 31 + i
            there = p[0] * NZ + p[1]
            moves.append(
                go(r.zsend.at[way, there], r.zrecv.at[way, chip], r.zs.at[0, at], r.zs.at[1, at], p)
            )
        r.zrecv[way, chip] = r.zsend[way, chip]
        yield
        arrived(moves)
        enters = jnp.zeros((8, HD), F32)
        for j in range(CHIPS) if way == 0 else range(CHIPS - 1, -1, -1):
            r.zbs[way, j] = enters
            enters = r.drecv[j] * enters + r.zrecv[way, j]
        moves = []
        for i, p in enumerate(plane):
            at = way * 31 + i
            there = p[0] * NZ + p[1]
            moves.append(
                go(r.zbs.at[way, there], r.zbr.at[way, chip], r.bs.at[0, at], r.bs.at[1, at], p)
            )
        r.zbr[way, chip] = r.zbs[way, chip]
        yield
        arrived(moves)
        for h in range(2):
            entering = r.zbr[way, 16 * h : 16 * h + 16].reshape(HD, HD)
            own, theirs = state[2 * k + h], r.csib[way, h]
            d_first = jnp.where(mine_first, d_mine[h], d_other[h])
            second = d_first * entering + jnp.where(mine_first, own, theirs)
            r.inc[way, 2 * k + h] = jnp.where(mine_first, entering, second)
            r.cback[way, h] = jnp.where(mine_first, second, entering)
        move = go(r.cback.at[way], r.inc.at[way, first_of], r.ks.at[0, way], r.ks.at[1, way], sibling)
        yield
        move.wait_recv()
        yield

    receive(1)
    pass_on(3)
    d_move.wait_recv()
    for h in range(2):
        chip_decay = r.dec[...] * r.dsib[...]
        decay_row = jnp.where(k == 0, chip_decay[h : h + 1], chip_decay[2 + h : 3 + h])
        r.dsend[h] = jnp.broadcast_to(decay_row, (8, HD))
    decay_moves = [
        go(r.dsend.at[lax.div(p[0], 2)], r.drecv.at[chip], r.ds.at[0, i], r.ds.at[1, i], p)
        for i, p in enumerate(plane)
    ]
    r.drecv[chip] = r.dsend[lax.div(x, 2)]

    receive(2)
    inputs()
    wx_move.wait()
    pass_on(4)
    project()
    states()
    forward = scan(0)
    next(forward)
    cq_move = queries()
    receive(3)
    next(forward)
    arrived(decay_moves)
    hq_moves = hidden_over_x()
    sibling_queries(cq_move)
    attend(z, True)
    attend(right(1), False)
    attend(left(1), False)
    receive(4)
    readouts()
    inners()
    attend(right(2), False)
    next(forward)
    attend(left(2), False)
    attend(right(3), False)
    attend(left(3), False)
    attend(right(4), False)
    half = PER * TOK
    r.stat[:1] = r.m_s[:1, half:]
    r.stat[1:2] = r.l_s[:1, half:]
    r.stat[2:] = jnp.zeros((6, half), F32)
    o_moves = [
        go(r.acc.at[:, pl.ds(half, half)], r.acc_in, r.co.at[0, 0], r.co.at[1, 0], sibling),
        go(r.stat, r.stat_in, r.co.at[0, 1], r.co.at[1, 1], sibling),
    ]
    next(forward)
    arrived(o_moves)
    other, mine_max = r.stat_in[:1], r.m_s[:1, :half]
    both = jnp.maximum(other, mine_max)
    a0, a1 = jnp.exp2(mine_max - both), jnp.exp2(other - both)
    norm = r.l_s[:1, :half] * a0 + r.stat_in[1:2] * a1
    result = (r.acc[:, :half] * a0 + r.acc_in[...] * a1) / norm
    for h in range(PER):
        r.target[h] = result[:, h * TOK : (h + 1) * TOK].T
    next(forward)
    for h in range(PER):
        student = r.inner[h] + r.growth[h] * exact(r.read[h], r.inc[0, h])
        out_s[:, h * HD : (h + 1) * HD] = student.astype(BF16)
        r.up[h] = 2.0 * (student - r.target[h]) / (HEAD_TOTAL * HD)
        r.state[1, h] = exact((r.growth[h] * r.read[h]).T, r.up[h])

    backward = scan(1)
    next(backward)
    next(backward)
    x_grad = jnp.zeros((TOK, HD), F32)
    for h in range(PER):
        up = r.up[h]
        x_grad = x_grad + step_of(h) * exact(r.mix[h].T, up) + skip_gain[:, h : h + 1] * up
    arrived(hq_moves)
    for e in range(2):
        r.hid_t[e] = r.hidq[e].T
    next(backward)

    for move in sent:
        move.wait_send()
    sent.clear()

    @pl.when(c < LAST)
    def _():
        tail(0).wait_send()
        tail(1).wait_send()
        end.wait_send()

    for way in range(2):
        for step in range(1, 5):
            for part in hidden_parts(way, step):
                hidden_copy(way, step, part).wait_send()

    for source, to in FIRST:

        @pl.when(x == source)
        def _(source=source, to=to):
            first_copy(source, to).wait_send()

    for xs in range(NX):

        @pl.when(in_ring(xs))
        def _(xs=xs):
            for way in range(2):
                for step in range(1, (4, 3)[way] + 1):
                    ring_copy(way, step, xs).wait_send()

        if xs < 3:

            @pl.when(x == xs)
            def _(xs=xs):
                for column in range(NZ):
                    across(column, xs).wait_send()

    next(backward)
    next(backward)
    b_conv = r.bconv[...]
    for h in range(PER):
        x_grad = x_grad + step_of(h) * r.to_end[h] * exact(b_conv, r.inc[1, h])
    x_pre = r.xpre[...]
    sigma = 1.0 / (1.0 + jnp.exp(-x_pre))
    r.ext2[:TOK] = x_grad * sigma * (1.0 + x_pre * (1.0 - sigma))
    r.ext2[TOK:] = jnp.zeros((8, HD), F32)
    r.ext3[:16] = jnp.zeros((16, HD), F32)
    r.ext3[16:] = r.ext2[:8]
    grad, share = jnp.zeros((TOK, HD), F32), jnp.zeros((16, HD), F32)
    for j in range(CONV):
        first = CONV - 1 - j
        grad = grad + conv_x[j : j + 1, :] * r.ext2[first : first + TOK]
        share = share + conv_x[j : j + 1, :] * r.ext3[first : first + 16]
    r.share[...] = share
    r.last[x] = grad[TOK - 16 :]

    def share_copy(i):
        return remote(
            r.share, r.shares.at[previous[0]], r.hs.at[0, i], r.hs.at[1, previous[0]], before[i]
        )

    @pl.when(c > 0)
    def _():
        for i in range(NX):
            share_copy(i).start()

    here = r.ig.at[pl.ds(pl.multiple_of(x * TOK, TOK), TOK - 16)]
    here[...] = grad[: TOK - 16].astype(BF16)
    moves = []
    for d, p in enumerate(x_peers):
        moves.append(go(r.last.at[x], r.last.at[x], r.igs.at[0, d], r.igs.at[1, d], p))
        moves.append(go(here, here, r.igs.at[0, 3 + d], r.igs.at[1, 3 + d], p))
    at_end = (z == NZ - 1) & (k == NK - 1)
    for i in range(NX):
        arrival = remote(r.share, r.shares.at[i], r.hs.at[0, i], r.hs.at[1, i], sibling)
        if i < NX - 1:
            arrival.wait_recv()
        else:
            pl.when(jnp.logical_not(at_end))(arrival.wait_recv)

            @pl.when(at_end)
            def _(i=i):
                r.shares[i] = jnp.zeros((16, HD), F32)

    arrived(moves)
    for i in range(NX):
        r.ig[(i + 1) * TOK - 16 : (i + 1) * TOK] = (r.last[i] + r.shares[i]).astype(BF16)
    for e in range(2):
        product = jnp.dot(r.hid_t[e], r.ig[...], preferred_element_type=F32)
        r.part[4 * e : 4 * e + 4] = product.reshape(4, NK, 64, HD)
    go(r.part.at[:, 1 - k], r.wrecv, r.wc.at[0], r.wc.at[1], sibling).wait_recv()
    for i in range(NZ):
        r.wsend[i] = r.part[i, k] + r.wrecv[i]
    moves = [
        go(r.wsend.at[p[1]], r.wzr.at[z], r.wz.at[0, d], r.wz.at[1, d], p)
        for d, p in enumerate(z_peers)
    ]
    r.wzr[z] = r.wsend[z]
    arrived(moves)
    total = r.wzr[0]
    for i in range(1, NZ):
        total = total + r.wzr[i]
    out_w[...] = total

    for move in sent:
        move.wait_send()

    @pl.when(c > 0)
    def _():
        for i in range(NX):
            share_copy(i).wait_send()


def local(
    query_proj, keyval_proj, hidden, weight_x, conv_x, conv_b, conv_c, step_size, decay_log, skip_gain
):
    args = (
        query_proj, keyval_proj.reshape(16, KV * 2 * HD), hidden, weight_x, step_size,
        decay_log.reshape(1, PER), skip_gain.reshape(1, PER), conv_x, conv_b, conv_c,
    )
    return pl.pallas_call(
        layer,
        out_shape=(
            jax.ShapeDtypeStruct((TOK, PER * HD), BF16),
            jax.ShapeDtypeStruct((64, HD), F32),
        ),
        in_specs=[pl.BlockSpec(memory_space=pl.ANY if i in (0, 2, 3) else pltpu.VMEM) for i in range(len(args))],
        out_specs=[pl.BlockSpec(memory_space=pltpu.VMEM)] * 2,
        scratch_shapes=list(scratch().values()),
        compiler_params=pltpu.CompilerParams(
            collective_id=0, has_side_effects=True, vmem_limit_bytes=48 * 2**20
        ),
    )(*args)


def solution(mesh):
    finer = Mesh(mesh.devices.reshape(NX, NZ, NK, mesh.shape["mp"]), CTX_MP)
    placed = (
        P(CTX_MP, None),
        P(CTX_MP, None, None),
        P(CTX, "mp"),
        P(None, "mp"),
        P(None, "mp"),
        P(None, "mp"),
        P(None, "mp"),
        P(CTX, "mp"),
        P("mp"),
        P("mp"),
    )
    return jax.shard_map(
        local, mesh=finer, in_specs=placed, out_specs=(P(CTX, "mp"), P(CTX, "mp")), check_vma=False
    )
```

```python
import types

import jax
import jax.numpy as jnp
from jax import lax
from jax.experimental import pallas as pl
from jax.experimental.pallas import tpu as pltpu
from jax.sharding import Mesh
from jax.sharding import PartitionSpec as P

HEAD_TOTAL = 32
KV = 8
HD = 128
CONV = 4
TOK = 128
PER = HEAD_TOTAL // KV
NX, NZ, NK, NM = 4, 8, 2, 8
CHIPS = NX * NZ
LAST = CHIPS * NK - 1
CTX = ("ctx_0", "ctx_1", "ctx_2")
CTX_MP = ("ctx_0", "ctx_1", "ctx_2", "mp")
MESH = pl.DeviceIdType.MESH
F32, BF16 = jnp.float32, jnp.bfloat16
NEG = -1e30
SCALE2 = HD**-0.5 * 1.4426950408889634
OFFSETS = sorted(
    ((a, b) for a in range(NX) for b in range(NZ) if a or b),
    key=lambda ab: -(min(ab[0], NX - ab[0]) + min(ab[1], NZ - ab[1])),
)


def place():
    return tuple(lax.axis_index(name) for name in CTX_MP)


def remote(src, dst, send, recv, device):
    return pltpu.make_async_remote_copy(
        src_ref=src, dst_ref=dst, send_sem=send, recv_sem=recv, device_id=device, device_id_type=MESH
    )


def greet(devices):
    barrier = pltpu.get_barrier_semaphore()
    for device in devices:
        pl.semaphore_signal(barrier, inc=1, device_id=device, device_id_type=MESH)
    pl.semaphore_wait(barrier, len(devices))


def exact(a, b, dims=((1,), (0,))):
    return lax.dot_general(
        a, b, (dims, ((), ())), precision=lax.Precision.HIGHEST, preferred_element_type=F32
    )


def silu(v):
    return v / (1.0 + jnp.exp(-v))


def dma(*dims):
    return pltpu.SemaphoreType.DMA(dims)


def scratch():
    vm = pltpu.VMEM
    return {
        "q2": vm((2, TOK, PER * HD), BF16),
        "kvb": vm((NZ, NX, TOK, 2 * HD), BF16),
        "hall": vm((NM, TOK + 16, 512), BF16),
        "wx": vm((4096, HD), BF16),
        "hidq": vm((2, NX * TOK, 512), BF16),
        "qs": vm((2 * PER * TOK, HD), BF16),
        "m_s": vm((8, 2 * PER * TOK), F32),
        "l_s": vm((8, 2 * PER * TOK), F32),
        "acc": vm((HD, 2 * PER * TOK), F32),
        "stat": vm((8, PER * TOK), F32),
        "acc_in": vm((HD, PER * TOK), F32),
        "stat_in": vm((8, PER * TOK), F32),
        "hid_t": vm((2, 512, NX * TOK), BF16),
        "target": vm((PER, TOK, HD), F32),
        "ext": vm((TOK + 8, 6 * HD), F32),
        "ext2": vm((TOK + 8, HD), F32),
        "ext3": vm((24, HD), F32),
        "last": vm((NX, 16, HD), F32),
        "share": vm((16, HD), F32),
        "shares": vm((NX, 16, HD), F32),
        "growth": vm((PER, TOK, TOK), F32),
        "to_end": vm((PER, TOK, TOK), F32),
        "within": vm((PER, TOK, TOK), F32),
        "mix": vm((PER, TOK, TOK), F32),
        "read": vm((PER, TOK, HD), F32),
        "inner": vm((PER, TOK, HD), F32),
        "up": vm((PER, TOK, HD), F32),
        "bconv": vm((TOK, HD), F32),
        "xconv": vm((TOK, HD), F32),
        "xpre": vm((TOK, HD), F32),
        "state": vm((2, PER, HD, HD), F32),
        "csib": vm((2, 2, HD, HD), F32),
        "cback": vm((2, 2, HD, HD), F32),
        "inc": vm((2, PER, HD, HD), F32),
        "dec": vm((8, HD), F32),
        "dsib": vm((8, HD), F32),
        "dsend": vm((2, 8, HD), F32),
        "drecv": vm((CHIPS, 8, HD), F32),
        "zsend": vm((2, CHIPS, 8, HD), F32),
        "zrecv": vm((2, CHIPS, 8, HD), F32),
        "zbs": vm((2, CHIPS, 8, HD), F32),
        "zbr": vm((2, CHIPS, 8, HD), F32),
        "ig": vm((NX * TOK, HD), BF16),
        "part": vm((NZ, NK, 64, HD), F32),
        "wrecv": vm((NZ, 64, HD), F32),
        "wsend": vm((NZ, 64, HD), F32),
        "wzr": vm((NZ, 64, HD), F32),
        "own_s": dma(4),
        "yq": dma(2, 7),
        "ykv": dma(2, 7),
        "yh": dma(2, 24),
        "ht": dma(2),
        "xkv": dma(2, NX),
        "xf": dma(2, NX * NZ),
        "ring": dma(2, 32),
        "cq": dma(2),
        "co": dma(2, 2),
        "hq": dma(2, 6),
        "halo": dma(2, 2),
        "cs": dma(2, 3),
        "ds": dma(2, 31),
        "zs": dma(2, 62),
        "bs": dma(2, 62),
        "ks": dma(2, 2),
        "igs": dma(2, 6),
        "hs": dma(2, NX),
        "wc": dma(2),
        "wz": dma(2, 7),
    }


def layer(
    q_in, kv_in, hid_in, wx, step_size, decay_log, skip_gain, conv_x, conv_b, conv_c, out_s, out_w, *rest
):
    r = types.SimpleNamespace(**dict(zip(scratch(), rest, strict=True)))
    x, z, k, m = place()
    chip = x * NZ + z
    c = chip * NK + k
    sibling = (x, z, 1 - k, m)
    zr, zl = lax.rem(z + 1, NZ), lax.rem(z + NZ - 1, NZ)
    y_peers = [(x, z, k, lax.rem(m + d, NM)) for d in range(1, NM)]
    x_peers = [(lax.rem(x + d, NX), z, k, m) for d in range(1, NX)]
    z_peers = [(x, lax.rem(z + d, NZ), k, m) for d in range(1, NZ)]
    plane = [(lax.rem(x + a, NX), lax.rem(z + b, NZ), k, m) for a, b in OFFSETS]

    def at_ctx(i):
        return (lax.div(i, NZ * NK), lax.rem(lax.div(i, NK), NZ), lax.rem(i, NK), m)

    following, previous = at_ctx(lax.rem(c + 1, LAST + 1)), at_ctx(lax.rem(c + LAST, LAST + 1))
    before = [(lax.rem(previous[0] + i, NX), *previous[1:]) for i in range(NX)]
    after = [(lax.rem(following[0] + i, NX), *following[1:]) for i in range(NX)]
    greet([*y_peers, *plane, sibling, *before, *after])
    sent = []

    def go(*args):
        move = remote(*args)
        move.start()
        sent.append(move)
        return move

    def arrived(moves):
        for move in moves:
            move.wait_recv()

    rows = pl.ds(pl.multiple_of(m * 16, 16), 16)

    def columns(i, width):
        return pl.ds(pl.multiple_of(i * width, width), width)

    def hidden_copy(way, step, part):
        block = lax.rem(m - (step - 1) + NM, NM) if way == 0 else lax.rem(m + step - 1, NM)
        peer = y_peers[0] if way == 0 else y_peers[-1]
        at = (way * 4 + step - 1) * 3 + part
        slot = r.hall.at[block, pl.ds((16, 80, 0)[part], (64, 64, 16)[part])]
        source = hid_in.at[pl.ds(64 * part, 64)] if step == 1 and part < 2 else slot
        return remote(source, slot, r.yh.at[0, at], r.yh.at[1, at], peer)

    def hidden_parts(way, step):
        return (0, 1, 2) if step < 4 else ((0, 2), (1,))[way]

    def pass_on(step):
        for part in range(3):
            for way in range(2):
                if part in hidden_parts(way, step):
                    hidden_copy(way, step, part).wait_recv()
                    if step < 4 and part in hidden_parts(way, step + 1):
                        hidden_copy(way, step + 1, part).start()

    end = remote(
        hid_in.at[pl.ds(TOK - 16, 16)], r.hall.at[m, pl.ds(0, 16)], r.ht.at[0], r.ht.at[1], following
    )

    @pl.when(c < LAST)
    def _():
        end.start()

    for part in range(2):
        for way in range(2):
            hidden_copy(way, 1, part).start()
    kv_moves = [
        go(kv_in.at[:, columns(p[3], 256)], r.kvb.at[z, x, rows], r.ykv.at[0, d], r.ykv.at[1, d], p)
        for d, p in enumerate(y_peers)
    ]
    mine = [
        pltpu.make_async_copy(kv_in.at[:, columns(m, 256)], r.kvb.at[z, x, rows], r.own_s.at[0]),
        pltpu.make_async_copy(q_in.at[:, columns(m, 512)], r.q2.at[0, rows], r.own_s.at[1]),
        pltpu.make_async_copy(hid_in, r.hall.at[m, pl.ds(16, TOK)], r.own_s.at[2]),
    ]
    wx_move = pltpu.make_async_copy(wx, r.wx, r.own_s.at[3])
    for move in [*mine, wx_move]:
        move.start()

    row = lax.broadcasted_iota(jnp.int32, (TOK, TOK), 0)
    col = lax.broadcasted_iota(jnp.int32, (TOK, TOK), 1)
    causal = row >= col
    lower = jnp.where(causal, 1.0, 0.0)
    rate = -jnp.exp(decay_log[...])

    def step_of(h):
        return jnp.broadcast_to(step_size[:, h : h + 1], (TOK, HD))

    for h in range(PER):
        log_decay = exact(lower, step_of(h) * rate[:, h : h + 1])
        final = log_decay[TOK - 1 :]
        r.growth[h] = jnp.exp(log_decay)
        r.to_end[h] = jnp.exp(final - log_decay)
        r.within[h] = jnp.where(
            causal, jnp.exp(jnp.where(causal, log_decay - log_decay.T, 0.0)), 0.0
        )
        r.dec[h : h + 1] = jnp.exp(final)
        r.dec[PER + h : PER + h + 1] = jnp.exp(final)
    d_move = go(r.dec, r.dsib, r.cs.at[0, 2], r.cs.at[1, 2], sibling)

    for xs in range(1, NX):

        @pl.when(xs > x)
        def _(xs=xs):
            r.kvb[:, xs] = jnp.zeros((NZ, TOK, 2 * HD), BF16)

    r.m_s[...] = jnp.full(r.m_s.shape, NEG, F32)
    r.l_s[...] = jnp.zeros(r.l_s.shape, F32)
    r.acc[...] = jnp.zeros(r.acc.shape, F32)

    def in_ring(xs):
        return (x == xs) | (x == xs + 2) | ((x == 1) & (xs == 0))

    def by_x(xs):
        return (x == 3 - xs) if xs < 2 else (x == 3) & (xs == 2)

    def ring_copy(way, step, xs):
        if way == 0:
            column, device = lax.rem(z - (step - 1) + NZ, NZ), (x, zr, k, m)
        else:
            column, device = lax.rem(z + (step - 1), NZ), (x, zl, k, m)
        slot = r.kvb.at[column, xs]
        at = (way * 4 + step - 1) * NX + xs
        return remote(slot, slot, r.ring.at[0, at], r.ring.at[1, at], device)

    def first_copy(xs, to):
        slot = r.kvb.at[z, xs]
        return remote(slot, slot, r.xkv.at[0, to], r.xkv.at[1, to], (to, z, k, m))

    FIRST = ((0, 1), (0, 2), (1, 3))

    def across(column, xs):
        to = (3, 2, 3)[xs]
        slot, at = r.kvb.at[column, xs], xs * NZ + column
        return remote(slot, slot, r.xf.at[0, at], r.xf.at[1, at], (to, z, k, m))

    for move in mine:
        move.wait()
    arrived(kv_moves)
    for xs in range(NX):

        @pl.when(x == xs)
        def _(xs=xs):
            for source, to in FIRST:
                if source == xs:
                    first_copy(xs, to).start()
            ring_copy(0, 1, xs).start()
            ring_copy(1, 1, xs).start()
            if xs < 3:
                across(z, xs).start()

    @pl.when(c > 0)
    def _():
        end.wait_recv()

    @pl.when(c == 0)
    def _():
        r.hall[m, :16] = jnp.zeros((16, 512), BF16)

    for way in range(2):
        hidden_copy(way, 1, 2).start()
    pass_on(1)

    q_moves = [
        go(q_in.at[:, columns(p[3], 512)], r.q2.at[0, rows], r.yq.at[0, d], r.yq.at[1, d], p)
        for d, p in enumerate(y_peers)
    ]
    def tail(i):
        at = (pl.ds(HD, HD), pl.ds(2 * HD, 4 * HD))[i]
        return remote(
            r.ext.at[pl.ds(TOK, 8), at], r.ext.at[pl.ds(0, 8), at],
            r.halo.at[0, i], r.halo.at[1, i], following,
        )

    def pass_tail(i):
        @pl.when(c < LAST)
        def _():
            tail(i).start()

    def tail_here(i):
        @pl.when(c > 0)
        def _():
            tail(i).wait_recv()

    r.ext[8:, HD : 2 * HD] = r.kvb[z, x, :, :HD].astype(F32)
    pass_tail(0)

    @pl.when(c == 0)
    def _():
        r.ext[:8, HD:] = jnp.zeros((8, 5 * HD), F32)

    for source, to in FIRST:

        @pl.when(x == to)
        def _(source=source, to=to):
            first_copy(source, to).wait_recv()
            ring_copy(0, 1, source).start()
            ring_copy(1, 1, source).start()

    pass_on(2)

    def queries():
        arrived(q_moves)
        move = go(r.q2.at[0], r.q2.at[1], r.cq.at[0], r.cq.at[1], sibling)
        r.ext[8:, 2 * HD :] = r.q2[0].astype(F32)
        pass_tail(1)
        for h in range(PER):
            r.qs[h * TOK : (h + 1) * TOK] = r.q2[0, :, h * HD : (h + 1) * HD]
        return move

    def sibling_queries(move):
        move.wait_recv()
        for h in range(PER):
            r.qs[(PER + h) * TOK : (PER + h + 1) * TOK] = r.q2[1, :, h * HD : (h + 1) * HD]

    def attend(column, masked):
        for xs in range(NX - 1):

            @pl.when(by_x(xs))
            def _(xs=xs):
                across(column, xs).wait_recv()

        block = r.kvb[column].reshape(NX * TOK, 2 * HD)
        scores = lax.dot_general(
            block[:, :HD], r.qs[...], (((1,), (1,)), ((), ())), preferred_element_type=F32
        )
        parts = [scores[b * TOK : (b + 1) * TOK] for b in range(NX)]
        if masked:
            key = lax.broadcasted_iota(jnp.int32, (TOK, 2 * PER * TOK), 0)
            query = lax.broadcasted_iota(jnp.int32, (TOK, 2 * PER * TOK), 1)
            core = jnp.where(query < PER * TOK, k, 1 - k)
            own = key + k * TOK <= lax.rem(query, TOK) + core * TOK
            parts = [jnp.where((b != x) | own, part, NEG) for b, part in enumerate(parts)]
            shut = [jnp.where(b <= x, 0.0, NEG) for b in range(NX)]
        else:
            shut = [jnp.where((b < x) | ((b == x) & (column < z)), 0.0, NEG) for b in range(NX)]
        before = now = r.m_s[:1]
        for part, off in zip(parts, shut, strict=True):
            now = jnp.maximum(now, jnp.max(part, axis=0, keepdims=True) * SCALE2 + off)
        alpha = jnp.exp2(before - now)
        parts = [
            jnp.exp2(part * SCALE2 - (now - off)) for part, off in zip(parts, shut, strict=True)
        ]
        total = r.l_s[:1] * alpha
        for part in parts:
            total = total + jnp.sum(part, axis=0, keepdims=True)
        r.l_s[:1] = total
        r.m_s[:1] = now
        weights = jnp.concatenate([part.astype(BF16) for part in parts], axis=0)
        r.acc[...] = r.acc[...] * alpha + lax.dot_general(
            block[:, HD:], weights, (((0,), (0,)), ((), ())), preferred_element_type=F32
        )

    def receive(step):
        for own in (True, False):
            for xs in range(NX) if own else range(NX - 2):

                @pl.when((x == xs) if own else in_ring(xs) & (x != xs))
                def _(own=own, xs=xs):
                    for way in range(2):
                        if way == 1 and step == 4:
                            continue
                        column = right(step) if way == 0 else left(step)
                        ring_copy(way, step, xs).wait_recv()
                        if step < (4, 3)[way]:
                            ring_copy(way, step + 1, xs).start()
                        if own and xs < 3:
                            across(column, xs).start()

    def right(step):
        return lax.rem(z - step + NZ, NZ)

    def left(step):
        return lax.rem(z + step, NZ)

    def conv(first, taps):
        width = taps.shape[1]
        total = jnp.zeros((TOK, width), F32)
        for j in range(CONV):
            total = total + taps[j : j + 1, :] * r.ext[5 + j : 5 + j + TOK, first : first + width]
        return total

    def inputs():
        tail_here(0)
        r.bconv[...] = silu(conv(HD, conv_b))

    def readouts():
        tail_here(1)
        c_conv = silu(conv(2 * HD, conv_c))
        b_t = r.bconv[...].T
        for h in range(PER):
            read = c_conv[:, h * HD : (h + 1) * HD]
            r.read[h] = read
            r.mix[h] = exact(read, b_t) * r.within[h]

    def project(distances):
        total = jnp.zeros((TOK + 16, HD), F32)
        for d in distances:
            j = lax.rem(m + d + NM, NM)
            weights = r.wx[pl.ds(pl.multiple_of(j * 512, 512), 512)]
            total = total + jnp.dot(r.hall[j], weights, preferred_element_type=F32)
        return total

    def hidden_over_x():
        moves = []
        for d in range(1, NX):
            there = lax.rem(x + d, NX)
            for e in range(2):
                at = (d - 1) * 2 + e
                into = r.hidq.at[e, columns(x, TOK)]
                moves.append(
                    go(
                        r.hall.at[2 * there + e, pl.ds(16, TOK)], into,
                        r.hq.at[0, at], r.hq.at[1, at], x_peers[d - 1],
                    )
                )
        for e in range(2):
            r.hidq[e, columns(x, TOK)] = r.hall[2 * x + e, 16:]
        return moves

    def states():
        x_pre = conv(0, conv_x)
        x_conv = silu(x_pre)
        r.xpre[...] = x_pre
        r.xconv[...] = x_conv
        b_t = r.bconv[...].T
        for h in range(PER):
            r.state[0, h] = exact(b_t, r.to_end[h] * (step_of(h) * x_conv))

    def inners():
        x_conv = r.xconv[...]
        for h in range(PER):
            r.inner[h] = exact(r.mix[h], step_of(h) * x_conv) + skip_gain[:, h : h + 1] * x_conv

    first_of, first_other = pl.ds(2 * k, 2), pl.ds(2 * (1 - k), 2)

    def scan(way):
        state = r.state.at[way]
        move = go(state.at[first_other], r.csib.at[way], r.cs.at[0, way], r.cs.at[1, way], sibling)
        yield
        move.wait_recv()
        d_mine = [jnp.where(k == 0, r.dec[h : h + 1], r.dec[2 + h : 3 + h]) for h in range(2)]
        d_other = [jnp.where(k == 0, r.dsib[h : h + 1], r.dsib[2 + h : 3 + h]) for h in range(2)]
        mine_first = (k == 0) if way == 0 else (k == 1)
        for h in range(2):
            own, theirs = state[2 * k + h], r.csib[way, h]
            near = jnp.where(mine_first, theirs, own)
            far = jnp.where(mine_first, own, theirs)
            d_near = jnp.where(mine_first, d_other[h], d_mine[h])
            both = far * d_near + near
            r.zsend[way, 16 * h : 16 * h + 16] = both.reshape(16, 8, HD)
        moves = []
        for i, p in enumerate(plane):
            at = way * 31 + i
            there = p[0] * NZ + p[1]
            moves.append(
                go(r.zsend.at[way, there], r.zrecv.at[way, chip], r.zs.at[0, at], r.zs.at[1, at], p)
            )
        r.zrecv[way, chip] = r.zsend[way, chip]
        yield
        arrived(moves)
        enters = jnp.zeros((8, HD), F32)
        for j in range(CHIPS) if way == 0 else range(CHIPS - 1, -1, -1):
            r.zbs[way, j] = enters
            enters = r.drecv[j] * enters + r.zrecv[way, j]
        moves = []
        for i, p in enumerate(plane):
            at = way * 31 + i
            there = p[0] * NZ + p[1]
            moves.append(
                go(r.zbs.at[way, there], r.zbr.at[way, chip], r.bs.at[0, at], r.bs.at[1, at], p)
            )
        r.zbr[way, chip] = r.zbs[way, chip]
        yield
        arrived(moves)
        for h in range(2):
            entering = r.zbr[way, 16 * h : 16 * h + 16].reshape(HD, HD)
            own, theirs = state[2 * k + h], r.csib[way, h]
            d_first = jnp.where(mine_first, d_mine[h], d_other[h])
            second = d_first * entering + jnp.where(mine_first, own, theirs)
            r.inc[way, 2 * k + h] = jnp.where(mine_first, entering, second)
            r.cback[way, h] = jnp.where(mine_first, second, entering)
        move = go(r.cback.at[way], r.inc.at[way, first_of], r.ks.at[0, way], r.ks.at[1, way], sibling)
        yield
        move.wait_recv()
        yield

    receive(1)
    pass_on(3)
    d_move.wait_recv()
    for h in range(2):
        chip_decay = r.dec[...] * r.dsib[...]
        decay_row = jnp.where(k == 0, chip_decay[h : h + 1], chip_decay[2 + h : 3 + h])
        r.dsend[h] = jnp.broadcast_to(decay_row, (8, HD))
    decay_moves = [
        go(r.dsend.at[lax.div(p[0], 2)], r.drecv.at[chip], r.ds.at[0, i], r.ds.at[1, i], p)
        for i, p in enumerate(plane)
    ]
    r.drecv[chip] = r.dsend[lax.div(x, 2)]

    receive(2)
    inputs()
    wx_move.wait()
    projected = project((0, 1, -1, 2, -2, 3, -3))
    pass_on(4)
    projected = projected + project((4,))
    r.ext[:, :HD] = projected[8:].astype(BF16).astype(F32)
    states()
    forward = scan(0)
    next(forward)
    cq_move = queries()
    receive(3)
    next(forward)
    arrived(decay_moves)
    hq_moves = hidden_over_x()
    sibling_queries(cq_move)
    attend(z, True)
    attend(right(1), False)
    attend(left(1), False)
    receive(4)
    readouts()
    inners()
    attend(right(2), False)
    next(forward)
    attend(left(2), False)
    attend(right(3), False)
    attend(left(3), False)
    attend(right(4), False)
    half = PER * TOK
    r.stat[:1] = r.m_s[:1, half:]
    r.stat[1:2] = r.l_s[:1, half:]
    r.stat[2:] = jnp.zeros((6, half), F32)
    o_moves = [
        go(r.acc.at[:, pl.ds(half, half)], r.acc_in, r.co.at[0, 0], r.co.at[1, 0], sibling),
        go(r.stat, r.stat_in, r.co.at[0, 1], r.co.at[1, 1], sibling),
    ]
    next(forward)
    arrived(o_moves)
    other, mine_max = r.stat_in[:1], r.m_s[:1, :half]
    both = jnp.maximum(other, mine_max)
    a0, a1 = jnp.exp2(mine_max - both), jnp.exp2(other - both)
    norm = r.l_s[:1, :half] * a0 + r.stat_in[1:2] * a1
    result = (r.acc[:, :half] * a0 + r.acc_in[...] * a1) / norm
    for h in range(PER):
        r.target[h] = result[:, h * TOK : (h + 1) * TOK].T
    next(forward)
    for h in range(PER):
        student = r.inner[h] + r.growth[h] * exact(r.read[h], r.inc[0, h])
        out_s[:, h * HD : (h + 1) * HD] = student.astype(BF16)
        r.up[h] = 2.0 * (student - r.target[h]) / (HEAD_TOTAL * HD)
        r.state[1, h] = exact((r.growth[h] * r.read[h]).T, r.up[h])

    backward = scan(1)
    next(backward)
    next(backward)
    x_grad = jnp.zeros((TOK, HD), F32)
    for h in range(PER):
        up = r.up[h]
        x_grad = x_grad + step_of(h) * exact(r.mix[h].T, up) + skip_gain[:, h : h + 1] * up
    arrived(hq_moves)
    for e in range(2):
        r.hid_t[e] = r.hidq[e].T
    next(backward)

    for move in sent:
        move.wait_send()
    sent.clear()

    @pl.when(c < LAST)
    def _():
        tail(0).wait_send()
        tail(1).wait_send()
        end.wait_send()

    for way in range(2):
        for step in range(1, 5):
            for part in hidden_parts(way, step):
                hidden_copy(way, step, part).wait_send()

    for source, to in FIRST:

        @pl.when(x == source)
        def _(source=source, to=to):
            first_copy(source, to).wait_send()

    for xs in range(NX):

        @pl.when(in_ring(xs))
        def _(xs=xs):
            for way in range(2):
                for step in range(1, (4, 3)[way] + 1):
                    ring_copy(way, step, xs).wait_send()

        if xs < 3:

            @pl.when(x == xs)
            def _(xs=xs):
                for column in range(NZ):
                    across(column, xs).wait_send()

    next(backward)
    next(backward)
    b_conv = r.bconv[...]
    for h in range(PER):
        x_grad = x_grad + step_of(h) * r.to_end[h] * exact(b_conv, r.inc[1, h])
    x_pre = r.xpre[...]
    sigma = 1.0 / (1.0 + jnp.exp(-x_pre))
    r.ext2[:TOK] = x_grad * sigma * (1.0 + x_pre * (1.0 - sigma))
    r.ext2[TOK:] = jnp.zeros((8, HD), F32)
    r.ext3[:16] = jnp.zeros((16, HD), F32)
    r.ext3[16:] = r.ext2[:8]
    grad, share = jnp.zeros((TOK, HD), F32), jnp.zeros((16, HD), F32)
    for j in range(CONV):
        first = CONV - 1 - j
        grad = grad + conv_x[j : j + 1, :] * r.ext2[first : first + TOK]
        share = share + conv_x[j : j + 1, :] * r.ext3[first : first + 16]
    r.share[...] = share
    r.last[x] = grad[TOK - 16 :]

    def share_copy(i):
        return remote(
            r.share, r.shares.at[previous[0]], r.hs.at[0, i], r.hs.at[1, previous[0]], before[i]
        )

    @pl.when(c > 0)
    def _():
        for i in range(NX):
            share_copy(i).start()

    here = r.ig.at[pl.ds(pl.multiple_of(x * TOK, TOK), TOK - 16)]
    here[...] = grad[: TOK - 16].astype(BF16)
    moves = []
    for d, p in enumerate(x_peers):
        moves.append(go(r.last.at[x], r.last.at[x], r.igs.at[0, d], r.igs.at[1, d], p))
        moves.append(go(here, here, r.igs.at[0, 3 + d], r.igs.at[1, 3 + d], p))
    at_end = (z == NZ - 1) & (k == NK - 1)
    for i in range(NX):
        arrival = remote(r.share, r.shares.at[i], r.hs.at[0, i], r.hs.at[1, i], sibling)
        if i < NX - 1:
            arrival.wait_recv()
        else:
            pl.when(jnp.logical_not(at_end))(arrival.wait_recv)

            @pl.when(at_end)
            def _(i=i):
                r.shares[i] = jnp.zeros((16, HD), F32)

    arrived(moves)
    for i in range(NX):
        r.ig[(i + 1) * TOK - 16 : (i + 1) * TOK] = (r.last[i] + r.shares[i]).astype(BF16)
    for e in range(2):
        product = jnp.dot(r.hid_t[e], r.ig[...], preferred_element_type=F32)
        r.part[4 * e : 4 * e + 4] = product.reshape(4, NK, 64, HD)
    go(r.part.at[:, 1 - k], r.wrecv, r.wc.at[0], r.wc.at[1], sibling).wait_recv()
    for i in range(NZ):
        r.wsend[i] = r.part[i, k] + r.wrecv[i]
    moves = [
        go(r.wsend.at[p[1]], r.wzr.at[z], r.wz.at[0, d], r.wz.at[1, d], p)
        for d, p in enumerate(z_peers)
    ]
    r.wzr[z] = r.wsend[z]
    arrived(moves)
    total = r.wzr[0]
    for i in range(1, NZ):
        total = total + r.wzr[i]
    out_w[...] = total

    for move in sent:
        move.wait_send()

    @pl.when(c > 0)
    def _():
        for i in range(NX):
            share_copy(i).wait_send()


def local(
    query_proj, keyval_proj, hidden, weight_x, conv_x, conv_b, conv_c, step_size, decay_log, skip_gain
):
    args = (
        query_proj, keyval_proj.reshape(16, KV * 2 * HD), hidden, weight_x, step_size,
        decay_log.reshape(1, PER), skip_gain.reshape(1, PER), conv_x, conv_b, conv_c,
    )
    return pl.pallas_call(
        layer,
        out_shape=(
            jax.ShapeDtypeStruct((TOK, PER * HD), BF16),
            jax.ShapeDtypeStruct((64, HD), F32),
        ),
        in_specs=[pl.BlockSpec(memory_space=pl.ANY if i in (0, 2, 3) else pltpu.VMEM) for i in range(len(args))],
        out_specs=[pl.BlockSpec(memory_space=pltpu.VMEM)] * 2,
        scratch_shapes=list(scratch().values()),
        compiler_params=pltpu.CompilerParams(
            collective_id=0, has_side_effects=True, vmem_limit_bytes=48 * 2**20
        ),
    )(*args)


def solution(mesh):
    finer = Mesh(mesh.devices.reshape(NX, NZ, NK, mesh.shape["mp"]), CTX_MP)
    placed = (
        P(CTX_MP, None),
        P(CTX_MP, None, None),
        P(CTX, "mp"),
        P(None, "mp"),
        P(None, "mp"),
        P(None, "mp"),
        P(None, "mp"),
        P(CTX, "mp"),
        P("mp"),
        P("mp"),
    )
    return jax.shard_map(
        local, mesh=finer, in_specs=placed, out_specs=(P(CTX, "mp"), P(CTX, "mp")), check_vma=False
    )
```
